256 devices in a mesh: px: 16 (over y, x_hi, core), py: 16 (over z, x_lo).
Axes of the slice: x: 4 (x_hi: 2, x_lo: 2; x = x_hi * 2 + x_lo), y: 4, z: 8, core: 2. Of those that a mesh axis runs over, the one named last changes fastest.
Arguments:
- state: float32 [5, 256, 256, 192], P(None, 'px', 'py'), may hold values from -6 to 6
- memory: float32 [5, 256, 256, 192], P(None, 'px', 'py'), may hold values from -3 to 3
- level_steps: int32 [192], replicated, may hold values from 1 to 3
- building_height: int32 [256, 256], P('px', 'py'), may hold values from 0 to 24
Outputs:
- updated: float32 [5, 256, 256, 192], P(None, 'px', 'py')
- pressure: float32 [256, 256, 192], P('px', 'py')
The draws below stay inside these ranges and needn't reach their ends.
All inputs are finite; a program needn't handle non-finite values.
Results may differ from the reference program's by a relative error of at most 0.0003.
Values sent between devices are 32-bit elements; how exact they have to be, the bound alone decides.
No kernel may reach another device: no remote copies, remote signals or barrier semaphores. Data moves between devices by JAX's collectives and lax.ppermute only.
A program may use at most 64 MiB of HBM per device.

```python
import jax
import jax.numpy as jnp
from jax import lax

NZ = 192
NX = 256
NY = 256


def set_ends(entries, rng, low, top_value):
    extent = entries.shape
    spot = [jax.random.randint(jax.random.fold_in(rng, axis), (), 0, extent[axis]) for axis in range(len(extent))]
    entries = entries.at[tuple(spot)].set(low)
    longest = extent.index(max(extent))
    spot[longest] = (spot[longest] + 1) % extent[longest]
    return entries.at[tuple(spot)].set(top_value)


def level_of(own_key, extent, split, low, largest):
    loudness = 1.0
    for dim, shards_of in split:
        steps = jax.random.uniform(jax.random.fold_in(jax.random.fold_in(own_key, 6), dim), (shards_of,), jnp.float32, low / len(split), largest / len(split))
        loudness = loudness * jnp.repeat(jnp.exp(steps), extent[dim] // shards_of).reshape((-1,) + (1,) * (len(extent) - 1 - dim))
    return loudness


def normal_values(key, extent, width, bound, shards=(), kind=jnp.bfloat16):
    entries = width * jax.random.normal(key, extent, jnp.float32)
    if shards:
        entries = entries * level_of(key, extent, shards, -0.22, 0.18)
    return jnp.clip(entries, -bound, bound).astype(kind)


def setup_inputs(seed: int = 0) -> dict:
    streams_of = jax.random.split(jax.random.key(seed), 5)
    return {
        "state": normal_values(streams_of[0], (5, NX, NY, NZ), 1.0, 6.0, ((1, 16), (2, 16)), jnp.float32),
        "memory": normal_values(streams_of[1], (5, NX, NY, NZ), 0.5, 3.0, ((1, 16), (2, 16)), jnp.float32),
        "level_steps": set_ends(jax.random.randint(streams_of[2], (NZ,), 1, 4), jax.random.fold_in(streams_of[2], 1), 1, 3).astype(jnp.int32),
        "building_height": set_ends(jax.random.randint(streams_of[3], (NX, NY), 0, 25), jax.random.fold_in(streams_of[3], 1), 0, 24).astype(jnp.int32),
    }


RK_KEEP = -5.0 / 9.0
RK_STEP = 15.0 / 16.0
TIME_STEP = 0.1
DIFFUSION = 0.05
BUOYANCY = 0.3


def level_geometry(level_steps):
    thickness = level_steps.astype(jnp.float32)
    spacing = jnp.concatenate([0.5 * (thickness[:-1] + thickness[1:]), thickness[-1:]])
    return thickness, spacing


def below_level(values):
    return jnp.concatenate([jnp.zeros_like(values[..., :1]), values[..., :-1]], axis=-1)


def above_level(values):
    return jnp.concatenate([values[..., 1:], values[..., -1:]], axis=-1)


def column_terms(values, z_velocity, thickness, spacing):
    upper_values = above_level(values)
    flux_up = z_velocity * (values + upper_values) * 0.5
    slope_up = (upper_values - values) / spacing
    return (flux_up - below_level(flux_up)) / thickness, (slope_up - below_level(slope_up)) / thickness


def column_operator(thickness, spacing):
    upward = 1.0 / (thickness * spacing)
    downward = jnp.concatenate([jnp.zeros_like(thickness[:1]), 1.0 / (thickness[1:] * spacing[:-1])])
    above_diag = jnp.concatenate([upward[:-1], jnp.zeros_like(thickness[:1])])
    return downward, -(upward + downward), above_diag


def eigenvalues(frequency, total):
    return 2.0 - 2.0 * jnp.cos((2.0 * jnp.pi / total) * frequency.astype(jnp.float32))


def tendency(values, x_velocity, y_velocity, z_velocity, thickness, spacing):
    east_cells = jnp.roll(values, -1, axis=0)
    west_cells = jnp.roll(values, 1, axis=0)
    north_cells = jnp.roll(values, -1, axis=1)
    south_cells = jnp.roll(values, 1, axis=1)
    x_west = jnp.roll(x_velocity, 1, axis=0)
    y_south = jnp.roll(y_velocity, 1, axis=1)
    advect = (x_velocity * (values + east_cells) - x_west * (west_cells + values)) * 0.5
    advect = advect + (y_velocity * (values + north_cells) - y_south * (south_cells + values)) * 0.5
    vertical, spread = column_terms(values, z_velocity, thickness, spacing)
    diffuse = east_cells + west_cells + north_cells + south_cells - 4.0 * values + spread
    return DIFFUSION * diffuse - advect - vertical


def thomas_solve(below_diag, above_diag, middle, eigen_shift, right_side):
    def forward(carry, item):
        ratio_prev, value_prev = carry
        low_coef, high_coef, mid_coef, right_here = item
        pivot = mid_coef - eigen_shift - low_coef * ratio_prev
        ratio = high_coef / pivot
        value_here = (right_here - low_coef * value_prev) / pivot
        return (ratio, value_here), (ratio, value_here)

    start = (jnp.zeros_like(eigen_shift), jnp.zeros_like(right_side[0]))
    _, (ratios, partial_values) = lax.scan(forward, start, (below_diag, above_diag, middle, right_side))

    def backward(after, item):
        ratio, value_here = item
        result_here = value_here - ratio * after
        return result_here, result_here

    _, solved = lax.scan(backward, jnp.zeros_like(right_side[0]), (ratios, partial_values), reverse=True)
    return solved


def reference(state, memory, level_steps, building_height):
    thickness, spacing = level_geometry(level_steps)
    levels = jnp.arange(NZ, dtype=jnp.int32)
    fluid_mask = jnp.where(levels[None, None, :] >= building_height[:, :, None], 1.0, 0.0).astype(jnp.float32)
    provisional = []
    for component in range(5):
        change = tendency(state[component], state[0], state[1], state[2], thickness, spacing)
        if component == 2:
            change = change + BUOYANCY * state[3]
        carried = RK_KEEP * memory[component] + TIME_STEP * fluid_mask * change
        provisional.append(state[component] + RK_STEP * carried)
    provisional_x, provisional_y, provisional_z = provisional[0], provisional[1], provisional[2]
    diverge = (provisional_x - jnp.roll(provisional_x, 1, axis=0)) + (provisional_y - jnp.roll(provisional_y, 1, axis=1))
    diverge = diverge + (provisional_z - below_level(provisional_z)) / thickness
    spectrum = jnp.fft.fft2(diverge, axes=(0, 1))
    right_side = jnp.stack([jnp.real(spectrum), jnp.imag(spectrum)]).astype(jnp.float32)
    right_side = jnp.transpose(right_side, (3, 0, 1, 2))
    eigen_shift = eigenvalues(jnp.arange(NX, dtype=jnp.int32), NX)[:, None] + eigenvalues(jnp.arange(NY, dtype=jnp.int32), NY)[None, :]
    below_diag, middle, above_diag = column_operator(thickness, spacing)
    solved = thomas_solve(below_diag, above_diag, middle, eigen_shift, right_side)
    solved = jnp.transpose(solved, (1, 2, 3, 0))
    pressure = jnp.real(jnp.fft.ifft2(lax.complex(solved[0], solved[1]), axes=(0, 1))).astype(jnp.float32)
    east_pressure = jnp.roll(pressure, -1, axis=0)
    north_pressure = jnp.roll(pressure, -1, axis=1)
    upper_pressure = jnp.concatenate([pressure[..., 1:], jnp.zeros_like(pressure[..., :1])], axis=-1)
    corrected_x = fluid_mask * (provisional_x - (east_pressure - pressure))
    corrected_y = fluid_mask * (provisional_y - (north_pressure - pressure))
    corrected_z = fluid_mask * (provisional_z - (upper_pressure - pressure) / spacing)
    updated = jnp.stack([corrected_x, corrected_y, corrected_z, provisional[3], provisional[4]])
    return updated, pressure
```

```python
import jax
import jax.numpy as jnp
import numpy as np
from jax import lax
from jax.experimental import pallas as pl
from jax.experimental.pallas import tpu as pltpu
from jax.sharding import PartitionSpec as P

RK_KEEP = -5.0 / 9.0
RK_STEP = 15.0 / 16.0
TIME_STEP = 0.1
DIFFUSION = 0.05
BUOYANCY = 0.3
HIGHEST = lax.Precision.HIGHEST

TILE = 16
LINE = 256
LEVELS = 192
WIDE = 256
CHUNK = LEVELS // TILE
FIRST = 192
SECOND = 208
STRIDES = (1, 2, 4, 8, 16, 32, 64, 128)


def tables():
    n = np.arange(LINE)
    angles = 2.0 * np.pi / LINE * (np.outer(n, n) % LINE)
    basis = (np.cos(angles) + np.sin(angles)) / np.sqrt(LINE)
    following = (n // TILE + 1) * TILE % LINE
    after = basis[following]
    chunk_lane = np.arange(WIDE)
    unpack = np.zeros((2, 128, WIDE))
    for which, lane in enumerate((FIRST, SECOND)):
        for z in range(LEVELS):
            unpack[which, lane - 128 + z % CHUNK, z] = 1.0
    pack = np.swapaxes(unpack, 1, 2)
    as32 = lambda a: np.ascontiguousarray(a, dtype=np.float32)
    return as32(basis), as32(after), as32(unpack), as32(pack)


BASIS, AFTER, UNPACK, PACK = tables()


def product(a, b, contract=((1,), (0,))):
    return lax.dot_general(
        a, b, (contract, ((), ())), precision=HIGHEST, preferred_element_type=jnp.float32
    )


def chunk_mask(shape, owner):
    lane = lax.broadcasted_iota(jnp.int32, shape, 1)
    row = lax.broadcasted_iota(jnp.int32, shape, 0)
    start = (row % TILE if owner == "low" else row // TILE) * CHUNK
    return (lane >= start) & (lane < start + CHUNK)


def lanes_up(a):
    return jnp.concatenate([a[:, 1:], a[:, -1:]], axis=1)


def lanes_down(a):
    return jnp.concatenate([jnp.zeros_like(a[:, :1]), a[:, :-1]], axis=1)


def edges_kernel(state, west, east, south, north):
    west[...] = state[:, 0]
    east[...] = state[:, TILE - 1]
    south[...] = state[:, :, 0]
    north[...] = state[:, :, TILE - 1]


def advance_fields(fields, state, memory, west, east, south, north, inv_rows, height, store):
    inv_thick = inv_rows[0:1, :]
    inv_space = inv_rows[1:2, :]
    level = lax.broadcasted_iota(jnp.int32, (TILE, LEVELS), 1)

    def x_faces(s, e, u):
        return e * (DIFFUSION - 0.5 * u) - s * (DIFFUSION + 0.5 * u)

    before = {f: x_faces(west[f], state[f, 0], west[0]) for f in fields}
    for x in range(TILE):
        u = state[0, x]
        v = state[1, x]
        w = state[2, x]
        u_to, u_from = DIFFUSION - 0.5 * u, DIFFUSION + 0.5 * u
        v_to, v_from = DIFFUSION - 0.5 * v, DIFFUSION + 0.5 * v
        w_to, w_from = DIFFUSION * inv_space - 0.5 * w, DIFFUSION * inv_space + 0.5 * w
        v_south = south[1, x : x + 1]
        fluid = jnp.where(level >= height[x], RK_STEP * TIME_STEP, 0.0)
        for f in fields:
            s = state[f, x]
            e = state[f, x + 1] if x < TILE - 1 else east[f]
            x_face = e * u_to - s * u_from
            upper_y = jnp.concatenate([s[1:], north[f, x : x + 1]], axis=0)
            y_face = upper_y * v_to - s * v_from
            first_y = x_faces(south[f, x : x + 1], s[:1], v_south)
            y_below = jnp.concatenate([first_y, y_face[:-1]], axis=0)
            z_face = lanes_up(s) * w_to - s * w_from
            change = (x_face - before[f]) + (y_face - y_below)
            change = change + (z_face - lanes_down(z_face)) * inv_thick
            if f == 2:
                change = change + BUOYANCY * state[3, x]
            before[f] = x_face
            store(f, x, s + (RK_STEP * RK_KEEP) * memory[f, x] + fluid * change)


def momentum_kernel(
    state, memory, west, east, south, north, inv_rows, height, pack, provisional, message
):
    def store(f, x, value):
        provisional[f, x] = value

    advance_fields(
        (0, 1, 2), state, memory, west, east, south, north, inv_rows, height, store
    )
    inv_thick = inv_rows[0:1, :]
    zeros = jnp.zeros((TILE, WIDE - LEVELS), jnp.float32)
    last_u = jnp.concatenate([provisional[0, TILE - 1], zeros], axis=1)
    u_packed = jnp.where(
        chunk_mask((LINE, WIDE), "high"), jnp.concatenate([last_u] * TILE, axis=0), 0.0
    )
    v_rows = []
    for x in range(TILE):
        last_v = jnp.broadcast_to(provisional[1, x, TILE - 1 :], (TILE, LEVELS))
        v_rows.append(jnp.concatenate([last_v, zeros], axis=1))
    v_packed = jnp.where(chunk_mask((LINE, WIDE), "low"), jnp.concatenate(v_rows, axis=0), 0.0)
    upper = product(v_packed, pack[0]) + product(u_packed, pack[1])
    for x in range(TILE):
        u = provisional[0, x]
        v = provisional[1, x]
        w = provisional[2, x]
        v_before = jnp.concatenate([jnp.zeros_like(v[:1]), v[:-1]], axis=0)
        diverge = (v - v_before) + (w - lanes_down(w)) * inv_thick
        diverge = diverge + (u - provisional[0, x - 1] if x else u)
        message[x, :, :128] = diverge[:, :128]
        message[x, :, 128:] = (
            jnp.concatenate([diverge[:, 128:], zeros], axis=1)
            + upper[x * TILE : (x + 1) * TILE]
        )


def scalars_kernel(state, memory, west, east, south, north, inv_rows, height, out):
    def store(f, x, value):
        out[f - 3, x] = value

    advance_fields((3, 4), state, memory, west, east, south, north, inv_rows, height, store)


def forward_y_kernel(lines, basis, after, unpack, spectrum):
    values = lines[...]
    extra = jnp.where(
        chunk_mask((LINE, WIDE), "low"), product(values[:, 128:], unpack[0]), 0.0
    )
    total = product(basis[...], values) - product(after[...], extra, ((0,), (0,)))
    spectrum[:, 0, :] = total


def rows_down(a, stride):
    return jnp.concatenate([jnp.zeros_like(a[:stride]), a[:-stride]], axis=0)


def rows_up(a, stride):
    return jnp.concatenate([a[stride:], jnp.zeros_like(a[:stride])], axis=0)


def factors_kernel(columns, shift, lower, upper, inverse):
    below = jnp.broadcast_to(columns[:, 0:1], (LEVELS, LINE))
    above = jnp.broadcast_to(columns[:, 2:3], (LEVELS, LINE))
    diagonal = columns[:, 1:2] - shift[...]
    for step, stride in enumerate(STRIDES):
        reciprocal = 1.0 / diagonal
        low = -below * rows_down(reciprocal, stride)
        high = -above * rows_up(reciprocal, stride)
        lower[step] = low
        upper[step] = high
        diagonal = diagonal + low * rows_down(above, stride) + high * rows_up(below, stride)
        below = low * rows_down(below, stride)
        above = high * rows_up(above, stride)
    inverse[...] = 1.0 / diagonal


def solve_kernel(lines, basis, after, unpack, pack, lower, upper, inverse, result):
    values = lines[:, 0, :]
    mask = chunk_mask((LINE, WIDE), "low")
    extra = jnp.where(mask, product(values[:, 128:], unpack[1]), 0.0)
    main = product(values, basis[...], ((0,), (0,)))
    fix = product(extra, after[...], ((0,), (0,)))
    right = main[:LEVELS] - fix[:LEVELS]
    for step, stride in enumerate(STRIDES):
        right = (
            right
            + lower[step] * rows_down(right, stride)
            + upper[step] * rows_up(right, stride)
        )
    solved = right * inverse[...]
    solved = jnp.concatenate([solved, jnp.zeros((WIDE - LEVELS, LINE), jnp.float32)], axis=0)
    back = product(basis[...], solved, ((1,), (1,)))
    beside = jnp.where(mask, product(after[...], solved, ((1,), (1,))), 0.0)
    result[:, 0, :128] = back[:, :128]
    result[:, 0, 128:] = back[:, 128:] + product(beside, pack[0])


def backward_y_kernel(lines, basis, after, pack, message):
    values = lines[:, 0, :]
    back = product(basis[...], values)
    beside = jnp.where(
        chunk_mask((LINE, WIDE), "low"), product(after[...], values), 0.0
    )
    message[:, :128] = back[:, :128]
    message[:, 128:] = back[:, 128:] + product(beside, pack[1])


def correct_kernel(message, provisional, scalars, inv_rows, height, unpack, updated, pressure):
    inv_space = inv_rows[1:2, :]
    level = lax.broadcasted_iota(jnp.int32, (TILE, LEVELS), 1)
    packed = message[:, :, 128:].reshape(LINE, 128)
    east = jnp.where(chunk_mask((LINE, WIDE), "high"), product(packed, unpack[0]), 0.0)
    east = east.reshape(TILE, TILE, WIDE).sum(axis=0)[:, :LEVELS]
    north = jnp.where(chunk_mask((LINE, WIDE), "low"), product(packed, unpack[1]), 0.0)
    north = north.reshape(TILE, TILE, WIDE).sum(axis=1)[:, :LEVELS]
    for x in range(TILE):
        p = message[x, :, :LEVELS]
        p_east = message[x + 1, :, :LEVELS] if x < TILE - 1 else east
        p_north = jnp.concatenate([p[1:], north[x : x + 1]], axis=0)
        p_upper = jnp.concatenate([p[:, 1:], jnp.zeros_like(p[:, :1])], axis=1)
        fluid = level >= height[x]
        updated[0, x] = jnp.where(fluid, provisional[0, x] - (p_east - p), 0.0)
        updated[1, x] = jnp.where(fluid, provisional[1, x] - (p_north - p), 0.0)
        updated[2, x] = jnp.where(fluid, provisional[2, x] - (p_upper - p) * inv_space, 0.0)
        updated[3, x] = scalars[0, x]
        updated[4, x] = scalars[1, x]
        pressure[x] = p


def shaped(*shape):
    return jax.ShapeDtypeStruct(shape, jnp.float32)


def call(kernel, out_shape, *operands, flops=0):
    count = sum(int(np.prod(a.shape)) for a in operands) * 4
    return pl.pallas_call(
        kernel,
        out_shape=out_shape,
        name=kernel.__name__,
        compiler_params=pltpu.CompilerParams(vmem_limit_bytes=40 * 1024 * 1024),
        cost_estimate=pl.CostEstimate(flops=flops, bytes_accessed=count, transcendentals=0),
    )(*operands)


def passed(block, axis, distance):
    count = lax.axis_size(axis)
    return lax.ppermute(block, axis, [((i - distance) % count, i) for i in range(count)])


def eigenvalues(frequency):
    return 2.0 - 2.0 * jnp.cos((2.0 * jnp.pi / LINE) * frequency.astype(jnp.float32))


def per_device(state, memory, level_steps, building_height):
    plane = shaped(5, TILE, LEVELS)
    edges = call(edges_kernel, [plane] * 4, state)
    west = passed(edges[1], "px", 1)
    east = passed(edges[0], "px", -1)
    south = passed(edges[3], "py", 1)
    north = passed(edges[2], "py", -1)

    thickness = level_steps.astype(jnp.float32)
    spacing = jnp.concatenate([0.5 * (thickness[:-1] + thickness[1:]), thickness[-1:]])
    inv_rows = jnp.stack([1.0 / thickness, 1.0 / spacing])
    height = building_height[:, :, None]
    upward = 1.0 / (thickness * spacing)
    downward = jnp.concatenate(
        [jnp.zeros_like(thickness[:1]), 1.0 / (thickness[1:] * spacing[:-1])]
    )
    above = jnp.concatenate([upward[:-1], jnp.zeros_like(thickness[:1])])
    columns = jnp.stack([downward, -(upward + downward), above], axis=1)
    own_y = lax.axis_index("px") * lax.axis_size("py") + lax.axis_index("py")
    shift = eigenvalues(jnp.arange(LINE, dtype=jnp.int32)) + eigenvalues(own_y)
    basis, after, unpack, pack = (jnp.asarray(a) for a in (BASIS, AFTER, UNPACK, PACK))

    halos = (west, east, south, north)
    provisional, message = call(
        momentum_kernel,
        [shaped(3, TILE, TILE, LEVELS), shaped(TILE, TILE, WIDE)],
        state, memory, *halos, inv_rows, height, pack,
        flops=10**7,
    )
    scalars = call(
        scalars_kernel, shaped(2, TILE, TILE, LEVELS), state, memory, *halos, inv_rows, height,
        flops=10**7,
    )
    factors = call(
        factors_kernel,
        [shaped(len(STRIDES), LEVELS, LINE), shaped(len(STRIDES), LEVELS, LINE), shaped(LEVELS, LINE)],
        columns, shift.reshape(1, LINE),
        flops=10**7,
    )
    lines = lax.all_to_all(message, "py", split_axis=0, concat_axis=0, tiled=True)
    spectrum = call(
        forward_y_kernel, shaped(LINE, 1, WIDE), lines.reshape(LINE, WIDE), basis, after, unpack
    )
    lines = lax.all_to_all(spectrum, ("px", "py"), split_axis=0, concat_axis=0, tiled=True)
    solved = call(
        solve_kernel, shaped(LINE, 1, WIDE), lines, basis, after, unpack, pack, *factors
    )
    lines = lax.all_to_all(solved, ("px", "py"), split_axis=0, concat_axis=0, tiled=True)
    message = call(backward_y_kernel, shaped(LINE, WIDE), lines, basis, after, pack)
    message = lax.all_to_all(
        message.reshape(TILE, TILE, WIDE), "py", split_axis=0, concat_axis=0, tiled=True
    )
    return call(
        correct_kernel,
        [shaped(5, TILE, TILE, LEVELS), shaped(TILE, TILE, LEVELS)],
        message, provisional, scalars, inv_rows, height, unpack,
    )


def solution(mesh):
    return jax.shard_map(
        per_device,
        mesh=mesh,
        in_specs=(P(None, "px", "py", None), P(None, "px", "py", None), P(), P("px", "py")),
        out_specs=(P(None, "px", "py", None), P("px", "py", None)),
        check_vma=False,
    )
```

```python
import jax
import jax.numpy as jnp
import numpy as np
from jax import lax
from jax.experimental import pallas as pl
from jax.experimental.pallas import tpu as pltpu
from jax.sharding import PartitionSpec as P

RK_KEEP = -5.0 / 9.0
RK_STEP = 15.0 / 16.0
TIME_STEP = 0.1
DIFFUSION = 0.05
BUOYANCY = 0.3
HIGHEST = lax.Precision.HIGHEST

TILE = 16
LINE = 256
LEVELS = 192
WIDE = 256
CHUNK = LEVELS // TILE
FIRST = 192
SECOND = 208
UNROLL = 3
MOST_VMEM = 50331648
STRIDES = (1, 2, 4, 8, 16, 32, 64, 128)


def tables():
    n = np.arange(LINE)
    angles = 2.0 * np.pi / LINE * (np.outer(n, n) % LINE)
    basis = (np.cos(angles) + np.sin(angles)) / np.sqrt(LINE)
    after = basis[(n[:TILE] + 1) * TILE % LINE]
    return basis.astype(np.float32), after.astype(np.float32)


BASIS, AFTER = tables()


def product(a, b, contract=((1,), (0,))):
    return lax.dot_general(
        a, b, (contract, ((), ())), precision=HIGHEST, preferred_element_type=jnp.float32
    )


def picked(values, places):
    high = values.astype(jnp.bfloat16)
    rest = values - high.astype(jnp.float32)
    middle = rest.astype(jnp.bfloat16)
    low = (rest - middle.astype(jnp.float32)).astype(jnp.bfloat16)
    dots = [
        jnp.dot(part, places, preferred_element_type=jnp.float32) for part in (low, middle, high)
    ]
    return (dots[0] + dots[1]) + dots[2]


def chunk_place(shape, level_dim, first):
    level = lax.broadcasted_iota(jnp.int32, shape, level_dim)
    lane = lax.broadcasted_iota(jnp.int32, shape, 1 - level_dim)
    chunk = jnp.floor((level.astype(jnp.float32) + 0.5) * (1.0 / CHUNK)).astype(jnp.int32)
    here = (level - chunk * CHUNK + (first - 128) == lane) & (level < LEVELS)
    return jnp.where(here, 1.0, 0.0).astype(jnp.bfloat16)


def pack_places(first):
    return chunk_place((WIDE, 128), 0, first)


def unpack_places(first):
    return chunk_place((128, WIDE), 1, first)


def each_block(rows):
    return jnp.concatenate(
        [jnp.broadcast_to(rows[b : b + 1], (TILE, rows.shape[1])) for b in range(TILE)], axis=0
    )


def level_rows(level_steps):
    thickness = level_steps[...].astype(jnp.float32)
    spacing = 0.5 * (thickness + lanes_up(thickness))
    return thickness, spacing


def chunk_mask(shape, owner):
    lane = lax.broadcasted_iota(jnp.int32, shape, 1)
    row = lax.broadcasted_iota(jnp.int32, shape, 0)
    start = (row % TILE if owner == "low" else row // TILE) * CHUNK
    return (lane >= start) & (lane < start + CHUNK)


def lanes_up(a):
    return jnp.concatenate([a[:, 1:], a[:, -1:]], axis=1)


def lanes_down(a):
    return jnp.concatenate([jnp.zeros_like(a[:, :1]), a[:, :-1]], axis=1)


def edges_kernel(state, west, east, south, north):
    west[...] = state[:, 0]
    east[...] = state[:, TILE - 1]
    south[...] = state[:, :, 0]
    north[...] = state[:, :, TILE - 1]


def advance_fields(fields, state, memory, west, east, south, north, level_steps, fluid, store):
    thickness, spacing = level_rows(level_steps)
    inv_thick = 1.0 / thickness
    inv_space = 1.0 / spacing

    def x_faces(s, e, u):
        return e * (DIFFUSION - 0.5 * u) - s * (DIFFUSION + 0.5 * u)

    def plane(x, before, east_of):
        u = state[0, x]
        v = state[1, x]
        w = state[2, x]
        u_to, u_from = DIFFUSION - 0.5 * u, DIFFUSION + 0.5 * u
        v_to, v_from = DIFFUSION - 0.5 * v, DIFFUSION + 0.5 * v
        w_to, w_from = DIFFUSION * inv_space - 0.5 * w, DIFFUSION * inv_space + 0.5 * w
        v_south = south[1, pl.ds(x, 1)]
        factor = (RK_STEP * TIME_STEP) * fluid[x]
        faces = []
        for i, f in enumerate(fields):
            s = state[f, x]
            x_face = east_of(f) * u_to - s * u_from
            upper_y = jnp.concatenate([s[1:], north[f, pl.ds(x, 1)]], axis=0)
            y_face = upper_y * v_to - s * v_from
            first_y = x_faces(south[f, pl.ds(x, 1)], s[:1], v_south)
            y_below = jnp.concatenate([first_y, y_face[:-1]], axis=0)
            z_face = lanes_up(s) * w_to - s * w_from
            change = (x_face - before[i]) + (y_face - y_below)
            change = change + (z_face - lanes_down(z_face)) * inv_thick
            if f == 2:
                change = change + BUOYANCY * state[3, x]
            faces.append(x_face)
            store(f, x, s + (RK_STEP * RK_KEEP) * memory[f, x] + factor * change)
        return tuple(faces)

    before = tuple(x_faces(west[f], state[f, 0], west[0]) for f in fields)
    before = lax.fori_loop(
        0, TILE - 1, lambda x, b: plane(x, b, lambda f: state[f, x + 1]), before, unroll=UNROLL
    )
    plane(TILE - 1, before, lambda f: east[f])


PART = 4


def parts_of(x):
    return pl.ds(x + 1 - PART, PART) if x % PART == PART - 1 else None


def fill_fluid(height, fluid):
    heights = each_block(height[...].astype(jnp.float32))
    row = lax.broadcasted_iota(jnp.int32, (LINE, TILE), 0)
    own = row % TILE == lax.broadcasted_iota(jnp.int32, (LINE, TILE), 1)
    bottom = jnp.sum(jnp.where(own, heights, 0.0), axis=1, keepdims=True)
    level = lax.broadcasted_iota(jnp.int32, (TILE, LEVELS), 1).astype(jnp.float32)
    for x in range(TILE):
        fluid[x] = jnp.where(level >= bottom[x * TILE : (x + 1) * TILE], 1.0, 0.0)


def momentum_kernel(
    state, memory, west, east, south, north, level_steps, height, message, provisional, fluid
):
    fill_fluid(height, fluid)

    def store(f, x, value):
        provisional[f, x] = value

    advance_fields(
        (0, 1, 2), state, memory, west, east, south, north, level_steps, fluid, store
    )
    inv_thick = 1.0 / level_rows(level_steps)[0]
    zeros = jnp.zeros((TILE, WIDE - LEVELS), jnp.float32)
    last_u = jnp.concatenate([provisional[0, TILE - 1], zeros], axis=1)
    u_packed = jnp.where(
        chunk_mask((LINE, WIDE), "high"), jnp.concatenate([last_u] * TILE, axis=0), 0.0
    )
    v_rows = []
    for x in range(TILE):
        last_v = jnp.broadcast_to(provisional[1, x, TILE - 1 :], (TILE, LEVELS))
        v_rows.append(jnp.concatenate([last_v, zeros], axis=1))
    v_packed = jnp.where(chunk_mask((LINE, WIDE), "low"), jnp.concatenate(v_rows, axis=0), 0.0)
    upper = picked(v_packed, pack_places(FIRST)) + picked(u_packed, pack_places(SECOND))
    for x in range(TILE):
        u = provisional[0, x]
        v = provisional[1, x]
        w = provisional[2, x]
        v_before = jnp.concatenate([jnp.zeros_like(v[:1]), v[:-1]], axis=0)
        diverge = (v - v_before) + (w - lanes_down(w)) * inv_thick
        diverge = diverge + (u - provisional[0, x - 1] if x else u)
        message[x, :, :128] = diverge[:, :128]
        message[x, :, 128:] = (
            jnp.concatenate([diverge[:, 128:], zeros], axis=1)
            + upper[x * TILE : (x + 1) * TILE]
        )


def loaded(pairs, sems):
    copies = [pltpu.make_async_copy(a, b, sems.at[i]) for i, (a, b) in enumerate(pairs)]
    for copy in copies:
        copy.start()
    return copies


def unpacked(values, first):
    mask = chunk_mask((LINE, WIDE), "low")
    spread = jnp.where(mask, picked(values[:, 128:], unpack_places(first)), 0.0)
    return spread.reshape(TILE, TILE, WIDE).sum(axis=1)


def repacked(rows, first):
    chunks = jnp.where(chunk_mask((LINE, WIDE), "low"), each_block(rows), 0.0)
    return picked(chunks, pack_places(first))


def forward_y_kernel(lines, basis, after, spectrum):
    values = lines[...]
    extra = unpacked(values, FIRST)
    total = product(basis[...], values) - product(after[...], extra, ((0,), (0,)))
    spectrum[:, 0, :] = total


def column_of(row):
    shape = (LEVELS, LEVELS)
    own = lax.broadcasted_iota(jnp.int32, shape, 0) == lax.broadcasted_iota(jnp.int32, shape, 1)
    return jnp.sum(jnp.where(own, row, 0.0), axis=1, keepdims=True)


def reduced(diagonal, coupling, right):
    for stride in STRIDES:
        shared = LEVELS - stride
        reciprocal = 1.0 / diagonal
        near = coupling[:shared]
        from_above = near * reciprocal[stride:]
        from_below = near * reciprocal[:shared]
        gap = jnp.zeros((stride, right.shape[1]), jnp.float32)
        low = lambda a: jnp.concatenate([a, gap], axis=0)
        high = lambda a: jnp.concatenate([gap, a], axis=0)
        right = right - low(from_above * right[stride:]) - high(from_below * right[:shared])
        diagonal = diagonal - low(near * from_above) - high(near * from_below)
        if shared > stride:
            coupling = low(-from_above * coupling[stride:])
    return right / diagonal


def side_kernel(
    state, memory, west, east, south, north, level_steps, height,
    provisional, updated, fluid,
    state_here, memory_here, halo_here, fluid_here, fields, sems,
):
    halos = (west, east, south, north)
    pairs = [(state, state_here), (memory, memory_here)]
    pairs += [(halo, halo_here.at[i]) for i, halo in enumerate(halos)]
    arriving = loaded(pairs, sems)
    fill_fluid(height, fluid_here)
    leaving = loaded([(fluid_here, fluid)], sems.at[pl.ds(6, 1)])
    for copy in arriving:
        copy.wait()

    def store(f, x, value):
        fields[f, x] = value

    advance_fields(
        (0, 1, 2, 3, 4), state_here, memory_here, *[halo_here.at[i] for i in range(4)],
        level_steps, fluid_here, store,
    )
    pairs = [(fields.at[0:3], provisional), (fields.at[3:5], updated.at[3:5])]
    leaving += loaded(pairs, sems.at[pl.ds(7, 2)])
    for copy in leaving:
        copy.wait()


def solve_kernel(lines, basis, after, level_steps, shift, result):
    thickness, spacing = level_rows(level_steps)
    level = lax.broadcasted_iota(jnp.int32, (1, LEVELS), 1)
    inv_space = 1.0 / spacing
    thick = column_of(thickness)
    diagonal = column_of(inv_space + lanes_down(inv_space)) + thick * shift[...]
    between = column_of(jnp.where(level < LEVELS - 1, -inv_space, 0.0))
    coupling = jnp.broadcast_to(between, (LEVELS, LINE))
    values = lines[:, 0, :]
    extra = unpacked(values, SECOND)
    main = product(values, basis[...], ((0,), (0,)))
    fix = product(extra, after[...], ((0,), (0,)))
    right = thick * (fix[:LEVELS] - main[:LEVELS])
    solved = reduced(diagonal, coupling, right)
    solved = jnp.concatenate([solved, jnp.zeros((WIDE - LEVELS, LINE), jnp.float32)], axis=0)
    back = product(basis[...], solved, ((1,), (1,)))
    beside = product(after[...], solved, ((1,), (1,)))
    result[:, 0, :128] = back[:, :128]
    result[:, 0, 128:] = back[:, 128:] + repacked(beside, FIRST)


def backward_y_kernel(lines, basis, after, message):
    values = lines[:, 0, :]
    back = product(basis[...], values)
    beside = product(after[...], values)
    message[:, :128] = back[:, :128]
    message[:, 128:] = back[:, 128:] + repacked(beside, SECOND)


def correct_kernel(
    message, provisional, level_steps, fluid, updated_in, updated, pressure, fields, cells, sems
):
    copies = []
    inv_space = 1.0 / level_rows(level_steps)[1]
    packed = message[:, :, 128:].reshape(LINE, 128)
    east = jnp.where(chunk_mask((LINE, WIDE), "high"), picked(packed, unpack_places(FIRST)), 0.0)
    east = east.reshape(TILE, TILE, WIDE).sum(axis=0)[:, :LEVELS]
    north = unpacked(message[...].reshape(LINE, WIDE), SECOND)[:, :LEVELS]
    for x in range(TILE):
        p = message[x, :, :LEVELS]
        p_east = message[x + 1, :, :LEVELS] if x < TILE - 1 else east
        p_north = jnp.concatenate([p[1:], north[x : x + 1]], axis=0)
        p_upper = jnp.concatenate([p[:, 1:], jnp.zeros_like(p[:, :1])], axis=1)
        open_cell = fluid[x]
        fields[0, x] = open_cell * (provisional[0, x] - (p_east - p))
        fields[1, x] = open_cell * (provisional[1, x] - (p_north - p))
        fields[2, x] = open_cell * (provisional[2, x] - (p_upper - p) * inv_space)
        cells[x] = p
        part = parts_of(x)
        if part is not None:
            pairs = [(fields.at[:, part], updated.at[0:3, part]), (cells.at[part], pressure.at[part])]
            copies += loaded(pairs, sems.at[pl.ds(x // PART * 2, 2)])
    for copy in copies:
        copy.wait()


def shaped(*shape):
    return jax.ShapeDtypeStruct(shape, jnp.float32)


def call(kernel, out_shape, *operands, flops=0, vmem=12 * 1024 * 1024, **options):
    here = pl.BlockSpec(memory_space=pltpu.VMEM)
    options.setdefault("in_specs", [here] * len(operands))
    options.setdefault("out_specs", jax.tree.map(lambda _: here, out_shape))
    count = sum(int(np.prod(a.shape)) for a in operands) * 4
    return pl.pallas_call(
        kernel,
        out_shape=out_shape,
        name=kernel.__name__,
        compiler_params=pltpu.CompilerParams(vmem_limit_bytes=vmem),
        cost_estimate=pl.CostEstimate(flops=flops, bytes_accessed=count, transcendentals=0),
        **options,
    )(*operands)


def passed(block, axis, distance):
    count = lax.axis_size(axis)
    return lax.ppermute(block, axis, [((i - distance) % count, i) for i in range(count)])


def eigenvalues(frequency):
    return 2.0 - 2.0 * jnp.cos((2.0 * jnp.pi / LINE) * frequency.astype(jnp.float32))


def per_device(state, memory, level_steps, building_height):
    plane = shaped(5, TILE, LEVELS)
    edges = call(edges_kernel, [plane] * 4, state)
    west = passed(edges[1], "px", 1)
    east = passed(edges[0], "px", -1)
    south = passed(edges[3], "py", 1)
    north = passed(edges[2], "py", -1)

    steps = level_steps.reshape(1, LEVELS)
    own_y = lax.axis_index("px") * lax.axis_size("py") + lax.axis_index("py")
    shift = eigenvalues(jnp.arange(LINE, dtype=jnp.int32)) + eigenvalues(own_y)
    basis, after = jnp.asarray(BASIS), jnp.asarray(AFTER)
    vmem, hbm = pl.BlockSpec(memory_space=pltpu.VMEM), pl.BlockSpec(memory_space=pltpu.HBM)
    scratch = lambda *shape: pltpu.VMEM(shape, jnp.float32)
    sems = pltpu.SemaphoreType.DMA

    halos = (west, east, south, north)
    message = call(
        momentum_kernel,
        shaped(TILE, TILE, WIDE),
        state, memory, *halos, steps, building_height,
        flops=10**7,
        scratch_shapes=[scratch(3, TILE, TILE, LEVELS), scratch(TILE, TILE, LEVELS)],
    )
    provisional, updated, fluid = call(
        side_kernel,
        [
            shaped(3, TILE, TILE, LEVELS),
            shaped(5, TILE, TILE, LEVELS),
            shaped(TILE, TILE, LEVELS),
        ],
        state, memory, *halos, steps, building_height,
        flops=2 * 10**7,
        vmem=MOST_VMEM,
        in_specs=[hbm] * 6 + [vmem] * 2,
        out_specs=[hbm] * 3,
        scratch_shapes=[
            scratch(5, TILE, TILE, LEVELS),
            scratch(5, TILE, TILE, LEVELS),
            scratch(4, 5, TILE, LEVELS),
            scratch(TILE, TILE, LEVELS),
            scratch(5, TILE, TILE, LEVELS),
            sems((9,)),
        ],
    )
    lines = lax.all_to_all(message, "py", split_axis=0, concat_axis=0, tiled=True)
    spectrum = call(
        forward_y_kernel, shaped(LINE, 1, WIDE), lines.reshape(LINE, WIDE), basis, after
    )
    lines = lax.all_to_all(spectrum, ("px", "py"), split_axis=0, concat_axis=0, tiled=True)
    lines, provisional = lax.optimization_barrier((lines, provisional))
    solved = call(
        solve_kernel, shaped(LINE, 1, WIDE), lines, basis, after, steps, shift.reshape(1, LINE)
    )
    lines = lax.all_to_all(solved, ("px", "py"), split_axis=0, concat_axis=0, tiled=True)
    message = call(backward_y_kernel, shaped(LINE, WIDE), lines, basis, after)
    message = lax.all_to_all(
        message.reshape(TILE, TILE, WIDE), "py", split_axis=0, concat_axis=0, tiled=True
    )
    return call(
        correct_kernel,
        [shaped(5, TILE, TILE, LEVELS), shaped(TILE, TILE, LEVELS)],
        message, provisional, steps, fluid, updated,
        in_specs=[vmem] * 4 + [hbm],
        out_specs=[hbm] * 2,
        input_output_aliases={4: 0},
        scratch_shapes=[
            scratch(3, TILE, TILE, LEVELS), scratch(TILE, TILE, LEVELS), sems((2 * TILE // PART,))
        ],
    )


def solution(mesh):
    return jax.shard_map(
        per_device,
        mesh=mesh,
        in_specs=(P(None, "px", "py", None), P(None, "px", "py", None), P(), P("px", "py")),
        out_specs=(P(None, "px", "py", None), P("px", "py", None)),
        check_vma=False,
    )
```

```python
import jax
import jax.numpy as jnp
import numpy as np
from jax import lax
from jax.experimental import pallas as pl
from jax.experimental.pallas import tpu as pltpu
from jax.sharding import PartitionSpec as P

RK_KEEP = -5.0 / 9.0
RK_STEP = 15.0 / 16.0
TIME_STEP = 0.1
DIFFUSION = 0.05
BUOYANCY = 0.3
HIGHEST = lax.Precision.HIGHEST

TILE = 16
LINE = 256
LEVELS = 192
WIDE = 256
CHUNK = LEVELS // TILE
FIRST = 192
SECOND = 208
UNROLL = 3
MOST_VMEM = 48 * 1024 * 1024
STRIDES = (1, 2, 4, 8, 16, 32, 64, 128)


def tables():
    n = np.arange(LINE)
    angles = 2.0 * np.pi / LINE * (np.outer(n, n) % LINE)
    basis = (np.cos(angles) + np.sin(angles)) / np.sqrt(LINE)
    after = basis[(n[:TILE] + 1) * TILE % LINE]
    return basis.astype(np.float32), after.astype(np.float32)


BASIS, AFTER = tables()


def product(a, b, contract=((1,), (0,))):
    return lax.dot_general(
        a, b, (contract, ((), ())), precision=HIGHEST, preferred_element_type=jnp.float32
    )


def picked(values, places):
    high = values.astype(jnp.bfloat16)
    rest = values - high.astype(jnp.float32)
    middle = rest.astype(jnp.bfloat16)
    low = (rest - middle.astype(jnp.float32)).astype(jnp.bfloat16)
    dots = [
        jnp.dot(part, places, preferred_element_type=jnp.float32) for part in (low, middle, high)
    ]
    return (dots[0] + dots[1]) + dots[2]


def chunk_place(shape, level_dim, first):
    level = lax.broadcasted_iota(jnp.int32, shape, level_dim)
    lane = lax.broadcasted_iota(jnp.int32, shape, 1 - level_dim)
    chunk = jnp.floor((level.astype(jnp.float32) + 0.5) * (1.0 / CHUNK)).astype(jnp.int32)
    here = (level - chunk * CHUNK + (first - 128) == lane) & (level < LEVELS)
    return jnp.where(here, 1.0, 0.0).astype(jnp.bfloat16)


def pack_places(first):
    return chunk_place((WIDE, 128), 0, first)


def unpack_places(first):
    return chunk_place((128, WIDE), 1, first)


def each_block(rows):
    return jnp.concatenate(
        [jnp.broadcast_to(rows[b : b + 1], (TILE, rows.shape[1])) for b in range(TILE)], axis=0
    )


def every_block(rows):
    return jnp.concatenate([rows] * TILE, axis=0)


def level_rows(level_steps):
    thickness = level_steps[...].astype(jnp.float32)
    spacing = 0.5 * (thickness + lanes_up(thickness))
    return thickness, spacing


def chunk_mask(shape, owner):
    lane = lax.broadcasted_iota(jnp.int32, shape, 1)
    row = lax.broadcasted_iota(jnp.int32, shape, 0)
    start = (row % TILE if owner == "low" else row // TILE) * CHUNK
    return (lane >= start) & (lane < start + CHUNK)


def lanes_up(a):
    return jnp.concatenate([a[:, 1:], a[:, -1:]], axis=1)


def lanes_down(a):
    return jnp.concatenate([jnp.zeros_like(a[:, :1]), a[:, :-1]], axis=1)


def edges_kernel(state, west, east, south, north):
    west[...] = state[:, 0]
    east[...] = state[:, TILE - 1]
    south[...] = state[:, :, 0]
    north[...] = state[:, :, TILE - 1]


def advance_fields(fields, state, memory, west, east, south, north, level_steps, fluid, store):
    thickness, spacing = level_rows(level_steps)
    inv_thick = 1.0 / thickness
    inv_space = 1.0 / spacing

    def x_faces(s, e, u):
        return e * (DIFFUSION - 0.5 * u) - s * (DIFFUSION + 0.5 * u)

    def plane(x, before, east_of):
        u = state[0, x]
        v = state[1, x]
        w = state[2, x]
        u_to, u_from = DIFFUSION - 0.5 * u, DIFFUSION + 0.5 * u
        v_to, v_from = DIFFUSION - 0.5 * v, DIFFUSION + 0.5 * v
        w_to, w_from = DIFFUSION * inv_space - 0.5 * w, DIFFUSION * inv_space + 0.5 * w
        v_south = south[1, pl.ds(x, 1)]
        factor = (RK_STEP * TIME_STEP) * fluid[x]
        faces = []
        for i, f in enumerate(fields):
            s = state[f, x]
            x_face = east_of(f) * u_to - s * u_from
            upper_y = jnp.concatenate([s[1:], north[f, pl.ds(x, 1)]], axis=0)
            y_face = upper_y * v_to - s * v_from
            first_y = x_faces(south[f, pl.ds(x, 1)], s[:1], v_south)
            y_below = jnp.concatenate([first_y, y_face[:-1]], axis=0)
            z_face = lanes_up(s) * w_to - s * w_from
            change = (x_face - before[i]) + (y_face - y_below)
            change = change + (z_face - lanes_down(z_face)) * inv_thick
            if f == 2:
                change = change + BUOYANCY * state[3, x]
            faces.append(x_face)
            store(f, x, s + (RK_STEP * RK_KEEP) * memory[f, x] + factor * change)
        return tuple(faces)

    before = tuple(x_faces(west[f], state[f, 0], west[0]) for f in fields)
    before = lax.fori_loop(
        0, TILE - 1, lambda x, b: plane(x, b, lambda f: state[f, x + 1]), before, unroll=UNROLL
    )
    plane(TILE - 1, before, lambda f: east[f])


PART = 4


def parts_of(x):
    return pl.ds(x + 1 - PART, PART) if x % PART == PART - 1 else None


def fill_fluid(height, fluid):
    heights = each_block(height[...].astype(jnp.float32))
    row = lax.broadcasted_iota(jnp.int32, (LINE, TILE), 0)
    own = row % TILE == lax.broadcasted_iota(jnp.int32, (LINE, TILE), 1)
    bottom = jnp.sum(jnp.where(own, heights, 0.0), axis=1, keepdims=True)
    level = lax.broadcasted_iota(jnp.int32, (TILE, LEVELS), 1).astype(jnp.float32)
    for x in range(TILE):
        fluid[x] = jnp.where(level >= bottom[x * TILE : (x + 1) * TILE], 1.0, 0.0)


def momentum_kernel(
    state, memory, west, east, south, north, level_steps, height, message, provisional, fluid
):
    fill_fluid(height, fluid)

    def store(f, x, value):
        provisional[f, x] = value

    advance_fields(
        (0, 1, 2), state, memory, west, east, south, north, level_steps, fluid, store
    )
    inv_thick = 1.0 / level_rows(level_steps)[0]
    zeros = jnp.zeros((TILE, WIDE - LEVELS), jnp.float32)
    last_u = jnp.concatenate([provisional[0, TILE - 1], zeros], axis=1)
    u_packed = jnp.where(chunk_mask((LINE, WIDE), "low"), each_block(last_u), 0.0)
    last_v = jnp.concatenate([provisional[1, :, TILE - 1], zeros], axis=1)
    v_packed = jnp.where(chunk_mask((LINE, WIDE), "high"), every_block(last_v), 0.0)
    upper = picked(u_packed, pack_places(FIRST)) + picked(v_packed, pack_places(SECOND))
    upper = upper.reshape(TILE, TILE, 128)
    for x in range(TILE):
        u = provisional[0, x]
        v = provisional[1, x]
        w = provisional[2, x]
        v_before = jnp.concatenate([jnp.zeros_like(v[:1]), v[:-1]], axis=0)
        diverge = (v - v_before) + (w - lanes_down(w)) * inv_thick
        diverge = diverge + (u - provisional[0, x - 1] if x else u)
        message[:, x, :128] = diverge[:, :128]
        message[:, x, 128:] = jnp.concatenate([diverge[:, 128:], zeros], axis=1) + upper[:, x]


def loaded(pairs, sems):
    copies = [pltpu.make_async_copy(a, b, sems.at[i]) for i, (a, b) in enumerate(pairs)]
    for copy in copies:
        copy.start()
    return copies


def unpacked(values, first, owner):
    mask = chunk_mask((LINE, WIDE), owner)
    spread = jnp.where(mask, picked(values[:, 128:], unpack_places(first)), 0.0)
    return spread.reshape(TILE, TILE, WIDE).sum(axis=1 if owner == "low" else 0)


def repacked(rows, first):
    chunks = jnp.where(chunk_mask((LINE, WIDE), "low"), each_block(rows), 0.0)
    return picked(chunks, pack_places(first))


def forward_kernel(lines, basis, after, spectrum):
    values = lines[...]
    extra = unpacked(values, FIRST, "low")
    total = product(basis[...], values) - product(after[...], extra, ((0,), (0,)))
    spectrum[:, 0, :] = total


def column_of(row):
    shape = (LEVELS, LEVELS)
    own = lax.broadcasted_iota(jnp.int32, shape, 0) == lax.broadcasted_iota(jnp.int32, shape, 1)
    return jnp.sum(jnp.where(own, row, 0.0), axis=1, keepdims=True)


def reduced(diagonal, coupling, right):
    for stride in STRIDES:
        shared = LEVELS - stride
        reciprocal = 1.0 / diagonal
        near = coupling[:shared]
        from_above = near * reciprocal[stride:]
        from_below = near * reciprocal[:shared]
        gap = jnp.zeros((stride, right.shape[1]), jnp.float32)
        low = lambda a: jnp.concatenate([a, gap], axis=0)
        high = lambda a: jnp.concatenate([gap, a], axis=0)
        right = right - low(from_above * right[stride:]) - high(from_below * right[:shared])
        diagonal = diagonal - low(near * from_above) - high(near * from_below)
        if shared > stride:
            coupling = low(-from_above * coupling[stride:])
    return right / diagonal


def side_kernel(
    state, memory, west, east, south, north, level_steps, height,
    provisional, updated, fluid_kept, state_here, memory_here, halo_here, fluid, fields, sems,
):
    halos = (west, east, south, north)
    pairs = [(state, state_here), (memory, memory_here)]
    pairs += [(halo, halo_here.at[i]) for i, halo in enumerate(halos)]
    arriving = loaded(pairs, sems)
    fill_fluid(height, fluid)
    leaving = loaded([(fluid, fluid_kept)], sems.at[pl.ds(6, 1)])
    for copy in arriving:
        copy.wait()

    def store(f, x, value):
        fields[f, x] = value

    advance_fields(
        (0, 1, 2, 3, 4), state_here, memory_here, *[halo_here.at[i] for i in range(4)],
        level_steps, fluid, store,
    )
    pairs = [(fields.at[0:3], provisional), (fields.at[3:5], updated.at[3:5])]
    leaving += loaded(pairs, sems.at[pl.ds(7, 2)])
    for copy in leaving:
        copy.wait()


def solve_kernel(lines, basis, after, level_steps, shift, result):
    thickness, spacing = level_rows(level_steps)
    level = lax.broadcasted_iota(jnp.int32, (1, LEVELS), 1)
    inv_space = 1.0 / spacing
    thick = column_of(thickness)
    diagonal = column_of(inv_space + lanes_down(inv_space)) + thick * shift[...]
    between = column_of(jnp.where(level < LEVELS - 1, -inv_space, 0.0))
    coupling = jnp.broadcast_to(between, (LEVELS, LINE))
    values = lines[:, 0, :]
    extra = unpacked(values, SECOND, "low")
    main = product(values, basis[...], ((0,), (0,)))
    fix = product(extra, after[...], ((0,), (0,)))
    right = thick * (fix[:LEVELS] - main[:LEVELS])
    solved = reduced(diagonal, coupling, right)
    solved = jnp.concatenate([solved, jnp.zeros((WIDE - LEVELS, LINE), jnp.float32)], axis=0)
    back = product(basis[...], solved, ((1,), (1,)))
    beside = product(after[...], solved, ((1,), (1,)))
    result[:, 0, :128] = back[:, :128]
    result[:, 0, 128:] = back[:, 128:] + repacked(beside, FIRST)


def backward_kernel(lines, basis, after, message):
    values = lines[:, 0, :]
    back = product(basis[...], values)
    beside = product(after[...], values)
    message[:, :128] = back[:, :128]
    message[:, 128:] = back[:, 128:] + repacked(beside, SECOND)


def correct_kernel(
    message, provisional, level_steps, fluid, kept, updated, pressure, fields, cells, sems
):
    copies = []
    inv_space = 1.0 / level_rows(level_steps)[1]
    lines = message[...].reshape(LINE, WIDE)
    north = unpacked(lines, FIRST, "high")[:, :LEVELS]
    east = unpacked(lines, SECOND, "low")[:, :LEVELS]
    for x in range(TILE):
        p = message[:, x, :LEVELS]
        p_east = message[:, x + 1, :LEVELS] if x < TILE - 1 else east
        p_north = jnp.concatenate([p[1:], north[x : x + 1]], axis=0)
        p_upper = jnp.concatenate([p[:, 1:], jnp.zeros_like(p[:, :1])], axis=1)
        open_cell = fluid[x]
        fields[0, x] = open_cell * (provisional[0, x] - (p_east - p))
        fields[1, x] = open_cell * (provisional[1, x] - (p_north - p))
        fields[2, x] = open_cell * (provisional[2, x] - (p_upper - p) * inv_space)
        cells[x] = p
        part = parts_of(x)
        if part is not None:
            pairs = [(fields.at[:, part], updated.at[0:3, part]), (cells.at[part], pressure.at[part])]
            copies += loaded(pairs, sems.at[pl.ds(x // PART * 2, 2)])
    for copy in copies:
        copy.wait()


def shaped(*shape):
    return jax.ShapeDtypeStruct(shape, jnp.float32)


def call(kernel, out_shape, *operands, flops=0, vmem=12 * 1024 * 1024, **options):
    here = pl.BlockSpec(memory_space=pltpu.VMEM)
    options.setdefault("in_specs", [here] * len(operands))
    options.setdefault("out_specs", jax.tree.map(lambda _: here, out_shape))
    count = sum(int(np.prod(a.shape)) for a in operands) * 4
    return pl.pallas_call(
        kernel,
        out_shape=out_shape,
        name=kernel.__name__,
        compiler_params=pltpu.CompilerParams(vmem_limit_bytes=vmem),
        cost_estimate=pl.CostEstimate(flops=flops, bytes_accessed=count, transcendentals=0),
        **options,
    )(*operands)


def passed(block, axis, distance):
    count = lax.axis_size(axis)
    return lax.ppermute(block, axis, [((i - distance) % count, i) for i in range(count)])


def eigenvalues(frequency):
    return 2.0 - 2.0 * jnp.cos((2.0 * jnp.pi / LINE) * frequency.astype(jnp.float32))


def per_device(state, memory, level_steps, building_height):
    plane = shaped(5, TILE, LEVELS)
    edges = call(edges_kernel, [plane] * 4, state)
    west = passed(edges[1], "px", 1)
    east = passed(edges[0], "px", -1)
    south = passed(edges[3], "py", 1)
    north = passed(edges[2], "py", -1)

    steps = level_steps.reshape(1, LEVELS)
    own_x = lax.axis_index("py") * lax.axis_size("px") + lax.axis_index("px")
    shift = eigenvalues(jnp.arange(LINE, dtype=jnp.int32)) + eigenvalues(own_x)
    basis, after = jnp.asarray(BASIS), jnp.asarray(AFTER)
    vmem, hbm = pl.BlockSpec(memory_space=pltpu.VMEM), pl.BlockSpec(memory_space=pltpu.HBM)
    scratch = lambda *shape: pltpu.VMEM(shape, jnp.float32)
    sems = pltpu.SemaphoreType.DMA

    halos = (west, east, south, north)
    message = call(
        momentum_kernel,
        shaped(TILE, TILE, WIDE),
        state, memory, *halos, steps, building_height,
        flops=10**7,
        scratch_shapes=[scratch(3, TILE, TILE, LEVELS), scratch(TILE, TILE, LEVELS)],
    )
    provisional, updated, fluid = call(
        side_kernel,
        [
            shaped(3, TILE, TILE, LEVELS),
            shaped(5, TILE, TILE, LEVELS),
            shaped(TILE, TILE, LEVELS),
        ],
        state, memory, *halos, steps, building_height,
        flops=2 * 10**7,
        vmem=MOST_VMEM,
        in_specs=[hbm] * 6 + [vmem] * 2,
        out_specs=[hbm] * 3,
        scratch_shapes=[
            scratch(5, TILE, TILE, LEVELS),
            scratch(5, TILE, TILE, LEVELS),
            scratch(4, 5, TILE, LEVELS),
            scratch(TILE, TILE, LEVELS),
            scratch(5, TILE, TILE, LEVELS),
            sems((9,)),
        ],
    )
    lines = lax.all_to_all(message, "px", split_axis=0, concat_axis=0, tiled=True)
    spectrum = call(
        forward_kernel, shaped(LINE, 1, WIDE), lines.reshape(LINE, WIDE), basis, after
    )
    lines = lax.all_to_all(spectrum, ("py", "px"), split_axis=0, concat_axis=0, tiled=True)
    lines, provisional = lax.optimization_barrier((lines, provisional))
    solved = call(
        solve_kernel, shaped(LINE, 1, WIDE), lines, basis, after, steps, shift.reshape(1, LINE)
    )
    lines = lax.all_to_all(solved, ("py", "px"), split_axis=0, concat_axis=0, tiled=True)
    message = call(backward_kernel, shaped(LINE, WIDE), lines, basis, after)
    message = lax.all_to_all(
        message.reshape(TILE, TILE, WIDE), "px", split_axis=0, concat_axis=0, tiled=True
    )
    return call(
        correct_kernel,
        [shaped(5, TILE, TILE, LEVELS), shaped(TILE, TILE, LEVELS)],
        message, provisional, steps, fluid, updated,
        in_specs=[vmem] * 4 + [hbm],
        out_specs=[hbm] * 2,
        input_output_aliases={4: 0},
        scratch_shapes=[
            scratch(3, TILE, TILE, LEVELS), scratch(TILE, TILE, LEVELS), sems((2 * TILE // PART,))
        ],
    )


def solution(mesh):
    return jax.shard_map(
        per_device,
        mesh=mesh,
        in_specs=(P(None, "px", "py", None), P(None, "px", "py", None), P(), P("px", "py")),
        out_specs=(P(None, "px", "py", None), P("px", "py", None)),
        check_vma=False,
    )
```

```python
import jax
import jax.numpy as jnp
import numpy as np
from jax import lax
from jax.experimental import pallas as pl
from jax.experimental.pallas import tpu as pltpu
from jax.sharding import PartitionSpec as P

RK_KEEP = -5.0 / 9.0
RK_STEP = 15.0 / 16.0
TIME_STEP = 0.1
DIFFUSION = 0.05
BUOYANCY = 0.3
HIGHEST = lax.Precision.HIGHEST

TILE = 16
LINE = 256
LEVELS = 192
WIDE = 256
CHUNK = LEVELS // TILE
FIRST = 192
SECOND = 208
UNROLL = 3
MOST_VMEM = 48 * 1024 * 1024
STRIDES = (1, 2, 4, 8, 16, 32, 64, 128)


def tables():
    n = np.arange(LINE)
    angles = 2.0 * np.pi / LINE * (np.outer(n, n) % LINE)
    basis = (np.cos(angles) + np.sin(angles)) / np.sqrt(LINE)
    after = basis[(n[:TILE] + 1) * TILE % LINE]
    return basis.astype(np.float32), after.astype(np.float32)


BASIS, AFTER = tables()


def product(a, b, contract=((1,), (0,))):
    return lax.dot_general(
        a, b, (contract, ((), ())), precision=HIGHEST, preferred_element_type=jnp.float32
    )


def picked(values, places):
    high = values.astype(jnp.bfloat16)
    rest = values - high.astype(jnp.float32)
    middle = rest.astype(jnp.bfloat16)
    low = (rest - middle.astype(jnp.float32)).astype(jnp.bfloat16)
    dots = [
        jnp.dot(part, places, preferred_element_type=jnp.float32) for part in (low, middle, high)
    ]
    return (dots[0] + dots[1]) + dots[2]


def chunk_place(shape, level_dim, first):
    level = lax.broadcasted_iota(jnp.int32, shape, level_dim)
    lane = lax.broadcasted_iota(jnp.int32, shape, 1 - level_dim)
    chunk = jnp.floor((level.astype(jnp.float32) + 0.5) * (1.0 / CHUNK)).astype(jnp.int32)
    here = (level - chunk * CHUNK + (first - 128) == lane) & (level < LEVELS)
    return jnp.where(here, 1.0, 0.0).astype(jnp.bfloat16)


def pack_places(first):
    return chunk_place((WIDE, 128), 0, first)


def unpack_places(first):
    return chunk_place((128, WIDE), 1, first)


def each_block(rows):
    return jnp.concatenate(
        [jnp.broadcast_to(rows[b : b + 1], (TILE, rows.shape[1])) for b in range(TILE)], axis=0
    )


def every_block(rows):
    return jnp.concatenate([rows] * TILE, axis=0)


def level_rows(level_steps):
    thickness = level_steps[...].astype(jnp.float32)
    spacing = 0.5 * (thickness + lanes_up(thickness))
    return thickness, spacing


def chunk_mask(shape, owner):
    lane = lax.broadcasted_iota(jnp.int32, shape, 1)
    row = lax.broadcasted_iota(jnp.int32, shape, 0)
    start = (row % TILE if owner == "low" else row // TILE) * CHUNK
    return (lane >= start) & (lane < start + CHUNK)


def lanes_up(a):
    return jnp.concatenate([a[:, 1:], a[:, -1:]], axis=1)


def lanes_down(a):
    return jnp.concatenate([jnp.zeros_like(a[:, :1]), a[:, :-1]], axis=1)


def edges_kernel(state, west, east, south, north):
    west[...] = state[:, 0]
    east[...] = state[:, TILE - 1]
    south[...] = state[:, :, 0]
    north[...] = state[:, :, TILE - 1]


def faces(s, e, u):
    return e * (DIFFUSION - 0.5 * u) - s * (DIFFUSION + 0.5 * u)


def advance_fields(fields, state, memory, halos, level_steps, fluid, store):
    thickness, spacing = level_rows(level_steps)
    inv_thick = 1.0 / thickness
    inv_space = 1.0 / spacing
    nothing = jnp.zeros((TILE, LEVELS), jnp.float32)
    if halos:
        west, east, south, north = halos

    def plane(x, before, east_of):
        u = state[0, x]
        v = state[1, x]
        w = state[2, x]
        u_to, u_from = DIFFUSION - 0.5 * u, DIFFUSION + 0.5 * u
        v_to, v_from = DIFFUSION - 0.5 * v, DIFFUSION + 0.5 * v
        w_to, w_from = DIFFUSION * inv_space - 0.5 * w, DIFFUSION * inv_space + 0.5 * w
        factor = (RK_STEP * TIME_STEP) * fluid[x]
        after = []
        for i, f in enumerate(fields):
            s = state[f, x]
            x_face = east_of(f) * u_to - s * u_from if east_of else nothing
            last_y, first_y = nothing[:1], nothing[:1]
            if halos:
                last_y = faces(s[TILE - 1 :], north[f, pl.ds(x, 1)], v[TILE - 1 :])
                first_y = faces(south[f, pl.ds(x, 1)], s[:1], south[1, pl.ds(x, 1)])
            y_face = jnp.concatenate([s[1:], s[:1]], axis=0) * v_to - s * v_from
            y_above = jnp.concatenate([y_face[:-1], last_y], axis=0)
            y_below = jnp.concatenate([first_y, y_face[:-1]], axis=0)
            z_face = lanes_up(s) * w_to - s * w_from
            change = (x_face - before[i]) + (y_above - y_below)
            change = change + (z_face - lanes_down(z_face)) * inv_thick
            if f == 2:
                change = change + BUOYANCY * state[3, x]
            after.append(x_face)
            store(f, x, s + (RK_STEP * RK_KEEP) * memory[f, x] + factor * change)
        return tuple(after)

    before = tuple(
        faces(west[f], state[f, 0], west[0]) if halos else nothing for f in fields
    )
    before = lax.fori_loop(
        0, TILE - 1, lambda x, b: plane(x, b, lambda f: state[f, x + 1]), before, unroll=UNROLL
    )
    plane(TILE - 1, before, (lambda f: east[f]) if halos else None)


PART = 4


def parts_of(x):
    return pl.ds(x + 1 - PART, PART) if x % PART == PART - 1 else None


def fill_fluid(height, fluid):
    heights = each_block(height[...].astype(jnp.float32))
    row = lax.broadcasted_iota(jnp.int32, (LINE, TILE), 0)
    own = row % TILE == lax.broadcasted_iota(jnp.int32, (LINE, TILE), 1)
    bottom = jnp.sum(jnp.where(own, heights, 0.0), axis=1, keepdims=True)
    level = lax.broadcasted_iota(jnp.int32, (TILE, LEVELS), 1).astype(jnp.float32)
    for x in range(TILE):
        fluid[x] = jnp.where(level >= bottom[x * TILE : (x + 1) * TILE], 1.0, 0.0)


def interior_kernel(state, memory, level_steps, height, provisional, fluid):
    fill_fluid(height, fluid)

    def store(f, x, value):
        provisional[f, x] = value

    advance_fields((0, 1, 2), state, memory, None, level_steps, fluid, store)


def momentum_kernel(
    state, inner, fluid, west, east, south, north, level_steps, message, provisional
):
    provisional[...] = inner[...]
    last, factor = TILE - 1, RK_STEP * TIME_STEP
    for f in range(3):
        provisional[f, 0] -= factor * fluid[0] * faces(west[f], state[f, 0], west[0])
        provisional[f, last] += factor * fluid[last] * faces(
            state[f, last], east[f], state[0, last]
        )
        provisional[f, :, 0] -= factor * fluid[:, 0] * faces(south[f], state[f, :, 0], south[1])
        provisional[f, :, last] += factor * fluid[:, last] * faces(
            state[f, :, last], north[f], state[1, :, last]
        )
    inv_thick = 1.0 / level_rows(level_steps)[0]
    zeros = jnp.zeros((TILE, WIDE - LEVELS), jnp.float32)
    last_u = jnp.concatenate([provisional[0, TILE - 1], zeros], axis=1)
    u_packed = jnp.where(chunk_mask((LINE, WIDE), "low"), each_block(last_u), 0.0)
    last_v = jnp.concatenate([provisional[1, :, TILE - 1], zeros], axis=1)
    v_packed = jnp.where(chunk_mask((LINE, WIDE), "high"), every_block(last_v), 0.0)
    upper = picked(u_packed, pack_places(FIRST)) + picked(v_packed, pack_places(SECOND))
    upper = upper.reshape(TILE, TILE, 128)
    for x in range(TILE):
        u = provisional[0, x]
        v = provisional[1, x]
        w = provisional[2, x]
        v_before = jnp.concatenate([jnp.zeros_like(v[:1]), v[:-1]], axis=0)
        diverge = (v - v_before) + (w - lanes_down(w)) * inv_thick
        diverge = diverge + (u - provisional[0, x - 1] if x else u)
        message[:, x, :128] = diverge[:, :128]
        message[:, x, 128:] = jnp.concatenate([diverge[:, 128:], zeros], axis=1) + upper[:, x]


def loaded(pairs, sems):
    copies = [pltpu.make_async_copy(a, b, sems.at[i]) for i, (a, b) in enumerate(pairs)]
    for copy in copies:
        copy.start()
    return copies


def unpacked(values, first, owner):
    mask = chunk_mask((LINE, WIDE), owner)
    spread = jnp.where(mask, picked(values[:, 128:], unpack_places(first)), 0.0)
    return spread.reshape(TILE, TILE, WIDE).sum(axis=1 if owner == "low" else 0)


def repacked(rows, first):
    chunks = jnp.where(chunk_mask((LINE, WIDE), "low"), each_block(rows), 0.0)
    return picked(chunks, pack_places(first))


def forward_kernel(lines, basis, after, spectrum):
    values = lines[...]
    extra = unpacked(values, FIRST, "low")
    total = product(basis[...], values) - product(after[...], extra, ((0,), (0,)))
    spectrum[:, 0, :] = total


def column_of(row):
    shape = (LEVELS, LEVELS)
    own = lax.broadcasted_iota(jnp.int32, shape, 0) == lax.broadcasted_iota(jnp.int32, shape, 1)
    return jnp.sum(jnp.where(own, row, 0.0), axis=1, keepdims=True)


def reduced(diagonal, coupling, right):
    for stride in STRIDES:
        shared = LEVELS - stride
        reciprocal = 1.0 / diagonal
        near = coupling[:shared]
        from_above = near * reciprocal[stride:]
        from_below = near * reciprocal[:shared]
        gap = jnp.zeros((stride, right.shape[1]), jnp.float32)
        low = lambda a: jnp.concatenate([a, gap], axis=0)
        high = lambda a: jnp.concatenate([gap, a], axis=0)
        right = right - low(from_above * right[stride:]) - high(from_below * right[:shared])
        diagonal = diagonal - low(near * from_above) - high(near * from_below)
        if shared > stride:
            coupling = low(-from_above * coupling[stride:])
    return right / diagonal


def side_kernel(
    state, memory, west, east, south, north, level_steps, height,
    provisional, updated, fluid_kept, state_here, memory_here, halo_here, fluid, fields, sems,
):
    halos = (west, east, south, north)
    pairs = [(state, state_here), (memory, memory_here)]
    pairs += [(halo, halo_here.at[i]) for i, halo in enumerate(halos)]
    arriving = loaded(pairs, sems)
    fill_fluid(height, fluid)
    leaving = loaded([(fluid, fluid_kept)], sems.at[pl.ds(6, 1)])
    for copy in arriving:
        copy.wait()

    def store(f, x, value):
        fields[f, x] = value

    advance_fields(
        (0, 1, 2, 3, 4), state_here, memory_here, [halo_here.at[i] for i in range(4)],
        level_steps, fluid, store,
    )
    pairs = [(fields.at[0:3], provisional), (fields.at[3:5], updated.at[3:5])]
    leaving += loaded(pairs, sems.at[pl.ds(7, 2)])
    for copy in leaving:
        copy.wait()


def solve_kernel(lines, basis, after, level_steps, shift, result):
    thickness, spacing = level_rows(level_steps)
    level = lax.broadcasted_iota(jnp.int32, (1, LEVELS), 1)
    inv_space = 1.0 / spacing
    thick = column_of(thickness)
    diagonal = column_of(inv_space + lanes_down(inv_space)) + thick * shift[...]
    between = column_of(jnp.where(level < LEVELS - 1, -inv_space, 0.0))
    coupling = jnp.broadcast_to(between, (LEVELS, LINE))
    values = lines[:, 0, :]
    extra = unpacked(values, SECOND, "low")
    main = product(values, basis[...], ((0,), (0,)))
    fix = product(extra, after[...], ((0,), (0,)))
    right = thick * (fix[:LEVELS] - main[:LEVELS])
    solved = reduced(diagonal, coupling, right)
    solved = jnp.concatenate([solved, jnp.zeros((WIDE - LEVELS, LINE), jnp.float32)], axis=0)
    back = product(basis[...], solved, ((1,), (1,)))
    beside = product(after[...], solved, ((1,), (1,)))
    result[:, 0, :128] = back[:, :128]
    result[:, 0, 128:] = back[:, 128:] + repacked(beside, FIRST)


def backward_kernel(lines, basis, after, message):
    values = lines[:, 0, :]
    back = product(basis[...], values)
    beside = product(after[...], values)
    message[:, :128] = back[:, :128]
    message[:, 128:] = back[:, 128:] + repacked(beside, SECOND)


def correct_kernel(
    message, provisional, level_steps, fluid, kept, updated, pressure, fields, cells, sems
):
    copies = []
    inv_space = 1.0 / level_rows(level_steps)[1]
    lines = message[...].reshape(LINE, WIDE)
    north = unpacked(lines, FIRST, "high")[:, :LEVELS]
    east = unpacked(lines, SECOND, "low")[:, :LEVELS]
    for x in range(TILE):
        p = message[:, x, :LEVELS]
        p_east = message[:, x + 1, :LEVELS] if x < TILE - 1 else east
        p_north = jnp.concatenate([p[1:], north[x : x + 1]], axis=0)
        p_upper = jnp.concatenate([p[:, 1:], jnp.zeros_like(p[:, :1])], axis=1)
        open_cell = fluid[x]
        fields[0, x] = open_cell * (provisional[0, x] - (p_east - p))
        fields[1, x] = open_cell * (provisional[1, x] - (p_north - p))
        fields[2, x] = open_cell * (provisional[2, x] - (p_upper - p) * inv_space)
        cells[x] = p
        part = parts_of(x)
        if part is not None:
            pairs = [(fields.at[:, part], updated.at[0:3, part]), (cells.at[part], pressure.at[part])]
            copies += loaded(pairs, sems.at[pl.ds(x // PART * 2, 2)])
    for copy in copies:
        copy.wait()


def shaped(*shape):
    return jax.ShapeDtypeStruct(shape, jnp.float32)


def call(kernel, out_shape, *operands, flops=0, vmem=12 * 1024 * 1024, **options):
    here = pl.BlockSpec(memory_space=pltpu.VMEM)
    options.setdefault("in_specs", [here] * len(operands))
    options.setdefault("out_specs", jax.tree.map(lambda _: here, out_shape))
    count = sum(int(np.prod(a.shape)) for a in operands) * 4
    return pl.pallas_call(
        kernel,
        out_shape=out_shape,
        name=kernel.__name__,
        compiler_params=pltpu.CompilerParams(vmem_limit_bytes=vmem),
        cost_estimate=pl.CostEstimate(flops=flops, bytes_accessed=count, transcendentals=0),
        **options,
    )(*operands)


def passed(block, axis, distance):
    count = lax.axis_size(axis)
    return lax.ppermute(block, axis, [((i - distance) % count, i) for i in range(count)])


def eigenvalues(frequency):
    return 2.0 - 2.0 * jnp.cos((2.0 * jnp.pi / LINE) * frequency.astype(jnp.float32))


def per_device(state, memory, level_steps, building_height):
    plane = shaped(5, TILE, LEVELS)
    edges = call(edges_kernel, [plane] * 4, state)
    west = passed(edges[1], "px", 1)
    east = passed(edges[0], "px", -1)
    south = passed(edges[3], "py", 1)
    north = passed(edges[2], "py", -1)

    steps = level_steps.reshape(1, LEVELS)
    own_x = lax.axis_index("py") * lax.axis_size("px") + lax.axis_index("px")
    shift = eigenvalues(jnp.arange(LINE, dtype=jnp.int32)) + eigenvalues(own_x)
    basis, after = jnp.asarray(BASIS), jnp.asarray(AFTER)
    vmem, hbm = pl.BlockSpec(memory_space=pltpu.VMEM), pl.BlockSpec(memory_space=pltpu.HBM)
    scratch = lambda *shape: pltpu.VMEM(shape, jnp.float32)
    sems = pltpu.SemaphoreType.DMA

    halos = (west, east, south, north)
    inner, fluid = call(
        interior_kernel,
        [shaped(3, TILE, TILE, LEVELS), shaped(TILE, TILE, LEVELS)],
        state, memory, steps, building_height,
        flops=10**7,
    )
    message = call(
        momentum_kernel,
        shaped(TILE, TILE, WIDE),
        state, inner, fluid, *halos, steps,
        flops=10**7,
        scratch_shapes=[scratch(3, TILE, TILE, LEVELS)],
    )
    provisional, updated, fluid = call(
        side_kernel,
        [
            shaped(3, TILE, TILE, LEVELS),
            shaped(5, TILE, TILE, LEVELS),
            shaped(TILE, TILE, LEVELS),
        ],
        state, memory, *halos, steps, building_height,
        flops=2 * 10**7,
        vmem=MOST_VMEM,
        in_specs=[hbm] * 6 + [vmem] * 2,
        out_specs=[hbm] * 3,
        scratch_shapes=[
            scratch(5, TILE, TILE, LEVELS),
            scratch(5, TILE, TILE, LEVELS),
            scratch(4, 5, TILE, LEVELS),
            scratch(TILE, TILE, LEVELS),
            scratch(5, TILE, TILE, LEVELS),
            sems((9,)),
        ],
    )
    lines = lax.all_to_all(message, "px", split_axis=0, concat_axis=0, tiled=True)
    spectrum = call(
        forward_kernel, shaped(LINE, 1, WIDE), lines.reshape(LINE, WIDE), basis, after
    )
    lines = lax.all_to_all(spectrum, ("py", "px"), split_axis=0, concat_axis=0, tiled=True)
    lines, provisional = lax.optimization_barrier((lines, provisional))
    solved = call(
        solve_kernel, shaped(LINE, 1, WIDE), lines, basis, after, steps, shift.reshape(1, LINE)
    )
    lines = lax.all_to_all(solved, ("py", "px"), split_axis=0, concat_axis=0, tiled=True)
    message = call(backward_kernel, shaped(LINE, WIDE), lines, basis, after)
    message = lax.all_to_all(
        message.reshape(TILE, TILE, WIDE), "px", split_axis=0, concat_axis=0, tiled=True
    )
    return call(
        correct_kernel,
        [shaped(5, TILE, TILE, LEVELS), shaped(TILE, TILE, LEVELS)],
        message, provisional, steps, fluid, updated,
        in_specs=[vmem] * 4 + [hbm],
        out_specs=[hbm] * 2,
        input_output_aliases={4: 0},
        scratch_shapes=[
            scratch(3, TILE, TILE, LEVELS), scratch(TILE, TILE, LEVELS), sems((2 * TILE // PART,))
        ],
    )


def solution(mesh):
    return jax.shard_map(
        per_device,
        mesh=mesh,
        in_specs=(P(None, "px", "py", None), P(None, "px", "py", None), P(), P("px", "py")),
        out_specs=(P(None, "px", "py", None), P("px", "py", None)),
        check_vma=False,
    )
```

```python
import jax
import jax.numpy as jnp
import numpy as np
from jax import lax
from jax.experimental import pallas as pl
from jax.experimental.pallas import tpu as pltpu
from jax.sharding import PartitionSpec as P

RK_KEEP = -5.0 / 9.0
RK_STEP = 15.0 / 16.0
TIME_STEP = 0.1
DIFFUSION = 0.05
BUOYANCY = 0.3
HIGHEST = lax.Precision.HIGHEST

TILE = 16
LINE = 256
LEVELS = 192
WIDE = 256
CHUNK = LEVELS // TILE
FIRST = 192
SECOND = 208
UNROLL = 3
MOST_VMEM = 48 * 1024 * 1024
STRIDES = (1, 2, 4, 8, 16, 32, 64, 128)


def tables():
    n = np.arange(LINE)
    angles = 2.0 * np.pi / LINE * (np.outer(n, n) % LINE)
    basis = (np.cos(angles) + np.sin(angles)) / np.sqrt(LINE)
    after = basis[(n[:TILE] + 1) * TILE % LINE]
    return basis.astype(np.float32), after.astype(np.float32)


BASIS, AFTER = tables()


def product(a, b, contract=((1,), (0,))):
    return lax.dot_general(
        a, b, (contract, ((), ())), precision=HIGHEST, preferred_element_type=jnp.float32
    )


def picked(values, places):
    high = values.astype(jnp.bfloat16)
    rest = values - high.astype(jnp.float32)
    middle = rest.astype(jnp.bfloat16)
    low = (rest - middle.astype(jnp.float32)).astype(jnp.bfloat16)
    dots = [
        jnp.dot(part, places, preferred_element_type=jnp.float32) for part in (low, middle, high)
    ]
    return (dots[0] + dots[1]) + dots[2]


def chunk_place(shape, level_dim, first):
    level = lax.broadcasted_iota(jnp.int32, shape, level_dim)
    lane = lax.broadcasted_iota(jnp.int32, shape, 1 - level_dim)
    chunk = jnp.floor((level.astype(jnp.float32) + 0.5) * (1.0 / CHUNK)).astype(jnp.int32)
    here = (level - chunk * CHUNK + (first - 128) == lane) & (level < LEVELS)
    return jnp.where(here, 1.0, 0.0).astype(jnp.bfloat16)


def pack_places(first):
    return chunk_place((WIDE, 128), 0, first)


def unpack_places(first):
    return chunk_place((128, WIDE), 1, first)


def each_block(rows):
    return jnp.concatenate(
        [jnp.broadcast_to(rows[b : b + 1], (TILE, rows.shape[1])) for b in range(TILE)], axis=0
    )


def every_block(rows):
    return jnp.concatenate([rows] * TILE, axis=0)


def level_rows(level_steps):
    thickness = level_steps[...].astype(jnp.float32)
    spacing = 0.5 * (thickness + lanes_up(thickness))
    return thickness, spacing


def chunk_mask(shape, owner):
    lane = lax.broadcasted_iota(jnp.int32, shape, 1)
    row = lax.broadcasted_iota(jnp.int32, shape, 0)
    start = (row % TILE if owner == "low" else row // TILE) * CHUNK
    return (lane >= start) & (lane < start + CHUNK)


def lanes_up(a):
    return jnp.concatenate([a[:, 1:], a[:, -1:]], axis=1)


def lanes_down(a):
    return jnp.concatenate([jnp.zeros_like(a[:, :1]), a[:, :-1]], axis=1)


def odd(axis):
    return lax.rem(lax.axis_index(axis), 2) == 1


def edges_kernel(state, x_outer, x_inner, y_outer, y_inner):
    low, high = state[:, 0], state[:, TILE - 1]
    x_outer[...] = jnp.where(odd("px"), high, low)
    x_inner[...] = jnp.where(odd("px"), low, high)
    low, high = state[:, :, 0], state[:, :, TILE - 1]
    y_outer[...] = jnp.where(odd("py"), high, low)
    y_inner[...] = jnp.where(odd("py"), low, high)


def faces(s, e, u):
    return e * (DIFFUSION - 0.5 * u) - s * (DIFFUSION + 0.5 * u)


def advance_fields(fields, state, memory, halos, level_steps, fluid, store):
    thickness, spacing = level_rows(level_steps)
    inv_thick = 1.0 / thickness
    inv_space = 1.0 / spacing
    nothing = jnp.zeros((TILE, LEVELS), jnp.float32)
    if halos:
        west, east, south, north = halos

    def plane(x, before, east_of):
        u = state[0, x]
        v = state[1, x]
        w = state[2, x]
        u_to, u_from = DIFFUSION - 0.5 * u, DIFFUSION + 0.5 * u
        v_to, v_from = DIFFUSION - 0.5 * v, DIFFUSION + 0.5 * v
        w_to, w_from = DIFFUSION * inv_space - 0.5 * w, DIFFUSION * inv_space + 0.5 * w
        factor = (RK_STEP * TIME_STEP) * fluid[x]
        after = []
        for i, f in enumerate(fields):
            s = state[f, x]
            x_face = east_of(f) * u_to - s * u_from if east_of else nothing
            last_y, first_y = nothing[:1], nothing[:1]
            if halos:
                last_y = faces(s[TILE - 1 :], north[f, pl.ds(x, 1)], v[TILE - 1 :])
                first_y = faces(south[f, pl.ds(x, 1)], s[:1], south[1, pl.ds(x, 1)])
            y_face = jnp.concatenate([s[1:], s[:1]], axis=0) * v_to - s * v_from
            y_above = jnp.concatenate([y_face[:-1], last_y], axis=0)
            y_below = jnp.concatenate([first_y, y_face[:-1]], axis=0)
            z_face = lanes_up(s) * w_to - s * w_from
            change = (x_face - before[i]) + (y_above - y_below)
            change = change + (z_face - lanes_down(z_face)) * inv_thick
            if f == 2:
                change = change + BUOYANCY * state[3, x]
            after.append(x_face)
            store(f, x, s + (RK_STEP * RK_KEEP) * memory[f, x] + factor * change)
        return tuple(after)

    before = tuple(
        faces(west[f], state[f, 0], west[0]) if halos else nothing for f in fields
    )
    before = lax.fori_loop(
        0, TILE - 1, lambda x, b: plane(x, b, lambda f: state[f, x + 1]), before, unroll=UNROLL
    )
    plane(TILE - 1, before, (lambda f: east[f]) if halos else None)


PART = 4


def parts_of(x):
    return pl.ds(x + 1 - PART, PART) if x % PART == PART - 1 else None


def fill_fluid(height, fluid):
    heights = each_block(height[...].astype(jnp.float32))
    row = lax.broadcasted_iota(jnp.int32, (LINE, TILE), 0)
    own = row % TILE == lax.broadcasted_iota(jnp.int32, (LINE, TILE), 1)
    bottom = jnp.sum(jnp.where(own, heights, 0.0), axis=1, keepdims=True)
    level = lax.broadcasted_iota(jnp.int32, (TILE, LEVELS), 1).astype(jnp.float32)
    for x in range(TILE):
        fluid[x] = jnp.where(level >= bottom[x * TILE : (x + 1) * TILE], 1.0, 0.0)


def interior_kernel(state, memory, level_steps, height, provisional, fluid):
    fill_fluid(height, fluid)

    def store(f, x, value):
        provisional[f, x] = value

    advance_fields((0, 1, 2), state, memory, None, level_steps, fluid, store)


def momentum_kernel(
    state, inner, fluid, x_outer, x_inner, y_outer, y_inner, level_steps, message, provisional
):
    provisional[...] = inner[...]
    odd_x, odd_y = odd("px"), odd("py")
    west = [jnp.where(odd_x, x_inner[f], x_outer[f]) for f in range(3)]
    east = [jnp.where(odd_x, x_outer[f], x_inner[f]) for f in range(3)]
    south = [jnp.where(odd_y, y_inner[f], y_outer[f]) for f in range(3)]
    north = [jnp.where(odd_y, y_outer[f], y_inner[f]) for f in range(3)]
    last, factor = TILE - 1, RK_STEP * TIME_STEP
    for f in range(3):
        provisional[f, 0] -= factor * fluid[0] * faces(west[f], state[f, 0], west[0])
        provisional[f, last] += factor * fluid[last] * faces(
            state[f, last], east[f], state[0, last]
        )
        provisional[f, :, 0] -= factor * fluid[:, 0] * faces(south[f], state[f, :, 0], south[1])
        provisional[f, :, last] += factor * fluid[:, last] * faces(
            state[f, :, last], north[f], state[1, :, last]
        )
    inv_thick = 1.0 / level_rows(level_steps)[0]
    zeros = jnp.zeros((TILE, WIDE - LEVELS), jnp.float32)
    last_u = jnp.concatenate([provisional[0, TILE - 1], zeros], axis=1)
    u_packed = jnp.where(chunk_mask((LINE, WIDE), "low"), each_block(last_u), 0.0)
    last_v = jnp.concatenate([provisional[1, :, TILE - 1], zeros], axis=1)
    v_packed = jnp.where(chunk_mask((LINE, WIDE), "high"), every_block(last_v), 0.0)
    upper = picked(u_packed, pack_places(FIRST)) + picked(v_packed, pack_places(SECOND))
    upper = upper.reshape(TILE, TILE, 128)
    for x in range(TILE):
        u = provisional[0, x]
        v = provisional[1, x]
        w = provisional[2, x]
        v_before = jnp.concatenate([jnp.zeros_like(v[:1]), v[:-1]], axis=0)
        diverge = (v - v_before) + (w - lanes_down(w)) * inv_thick
        diverge = diverge + (u - provisional[0, x - 1] if x else u)
        message[:, x, :128] = diverge[:, :128]
        message[:, x, 128:] = jnp.concatenate([diverge[:, 128:], zeros], axis=1) + upper[:, x]


def loaded(pairs, sems):
    copies = [pltpu.make_async_copy(a, b, sems.at[i]) for i, (a, b) in enumerate(pairs)]
    for copy in copies:
        copy.start()
    return copies


def unpacked(values, first, owner):
    mask = chunk_mask((LINE, WIDE), owner)
    spread = jnp.where(mask, picked(values[:, 128:], unpack_places(first)), 0.0)
    return spread.reshape(TILE, TILE, WIDE).sum(axis=1 if owner == "low" else 0)


def repacked(rows, first):
    chunks = jnp.where(chunk_mask((LINE, WIDE), "low"), each_block(rows), 0.0)
    return picked(chunks, pack_places(first))


def forward_kernel(lines, basis, after, spectrum):
    values = lines[...]
    extra = unpacked(values, FIRST, "low")
    total = product(basis[...], values) - product(after[...], extra, ((0,), (0,)))
    spectrum[:, 0, :] = total


def column_of(row):
    shape = (LEVELS, LEVELS)
    own = lax.broadcasted_iota(jnp.int32, shape, 0) == lax.broadcasted_iota(jnp.int32, shape, 1)
    return jnp.sum(jnp.where(own, row, 0.0), axis=1, keepdims=True)


def reduced(diagonal, coupling, right):
    for stride in STRIDES:
        shared = LEVELS - stride
        reciprocal = 1.0 / diagonal
        near = coupling[:shared]
        from_above = near * reciprocal[stride:]
        from_below = near * reciprocal[:shared]
        gap = jnp.zeros((stride, right.shape[1]), jnp.float32)
        low = lambda a: jnp.concatenate([a, gap], axis=0)
        high = lambda a: jnp.concatenate([gap, a], axis=0)
        right = right - low(from_above * right[stride:]) - high(from_below * right[:shared])
        diagonal = diagonal - low(near * from_above) - high(near * from_below)
        if shared > stride:
            coupling = low(-from_above * coupling[stride:])
    return right / diagonal


def side_kernel(
    state, memory, x_outer, x_inner, y_outer, y_inner, level_steps, height,
    provisional, updated, fluid_kept, state_here, memory_here, halo_here, fluid, fields, sems,
):
    pairs = [(state, state_here), (memory, memory_here)]
    first_x, first_y = odd("px").astype(jnp.int32), odd("py").astype(jnp.int32)
    pairs += [(x_outer, halo_here.at[first_x]), (x_inner, halo_here.at[1 - first_x])]
    pairs += [(y_outer, halo_here.at[2 + first_y]), (y_inner, halo_here.at[3 - first_y])]
    arriving = loaded(pairs, sems)
    fill_fluid(height, fluid)
    leaving = loaded([(fluid, fluid_kept)], sems.at[pl.ds(6, 1)])
    for copy in arriving:
        copy.wait()

    def store(f, x, value):
        fields[f, x] = value

    advance_fields(
        (0, 1, 2, 3, 4), state_here, memory_here, [halo_here.at[i] for i in range(4)],
        level_steps, fluid, store,
    )
    pairs = [(fields.at[0:3], provisional), (fields.at[3:5], updated.at[3:5])]
    leaving += loaded(pairs, sems.at[pl.ds(7, 2)])
    for copy in leaving:
        copy.wait()


def solve_kernel(lines, basis, after, level_steps, shift, result):
    thickness, spacing = level_rows(level_steps)
    level = lax.broadcasted_iota(jnp.int32, (1, LEVELS), 1)
    inv_space = 1.0 / spacing
    thick = column_of(thickness)
    diagonal = column_of(inv_space + lanes_down(inv_space)) + thick * shift[...]
    between = column_of(jnp.where(level < LEVELS - 1, -inv_space, 0.0))
    coupling = jnp.broadcast_to(between, (LEVELS, LINE))
    values = lines[:, 0, :]
    extra = unpacked(values, SECOND, "low")
    main = product(values, basis[...], ((0,), (0,)))
    fix = product(extra, after[...], ((0,), (0,)))
    right = thick * (fix[:LEVELS] - main[:LEVELS])
    solved = reduced(diagonal, coupling, right)
    solved = jnp.concatenate([solved, jnp.zeros((WIDE - LEVELS, LINE), jnp.float32)], axis=0)
    back = product(basis[...], solved, ((1,), (1,)))
    beside = product(after[...], solved, ((1,), (1,)))
    result[:, 0, :128] = back[:, :128]
    result[:, 0, 128:] = back[:, 128:] + repacked(beside, FIRST)


def backward_kernel(lines, basis, after, message):
    values = lines[:, 0, :]
    back = product(basis[...], values)
    beside = product(after[...], values)
    message[:, :128] = back[:, :128]
    message[:, 128:] = back[:, 128:] + repacked(beside, SECOND)


def correct_kernel(
    message, provisional, level_steps, fluid, kept, updated, pressure, fields, cells, sems
):
    copies = []
    inv_space = 1.0 / level_rows(level_steps)[1]
    lines = message[...].reshape(LINE, WIDE)
    north = unpacked(lines, FIRST, "high")[:, :LEVELS]
    east = unpacked(lines, SECOND, "low")[:, :LEVELS]
    for x in range(TILE):
        p = message[:, x, :LEVELS]
        p_east = message[:, x + 1, :LEVELS] if x < TILE - 1 else east
        p_north = jnp.concatenate([p[1:], north[x : x + 1]], axis=0)
        p_upper = jnp.concatenate([p[:, 1:], jnp.zeros_like(p[:, :1])], axis=1)
        open_cell = fluid[x]
        fields[0, x] = open_cell * (provisional[0, x] - (p_east - p))
        fields[1, x] = open_cell * (provisional[1, x] - (p_north - p))
        fields[2, x] = open_cell * (provisional[2, x] - (p_upper - p) * inv_space)
        cells[x] = p
        part = parts_of(x)
        if part is not None:
            pairs = [(fields.at[:, part], updated.at[0:3, part]), (cells.at[part], pressure.at[part])]
            copies += loaded(pairs, sems.at[pl.ds(x // PART * 2, 2)])
    for copy in copies:
        copy.wait()


def shaped(*shape):
    return jax.ShapeDtypeStruct(shape, jnp.float32)


def call(kernel, out_shape, *operands, flops=0, vmem=12 * 1024 * 1024, **options):
    here = pl.BlockSpec(memory_space=pltpu.VMEM)
    options.setdefault("in_specs", [here] * len(operands))
    options.setdefault("out_specs", jax.tree.map(lambda _: here, out_shape))
    count = sum(int(np.prod(a.shape)) for a in operands) * 4
    return pl.pallas_call(
        kernel,
        out_shape=out_shape,
        name=kernel.__name__,
        compiler_params=pltpu.CompilerParams(vmem_limit_bytes=vmem),
        cost_estimate=pl.CostEstimate(flops=flops, bytes_accessed=count, transcendentals=0),
        **options,
    )(*operands)


def swapped(block, axis, outer):
    count = lax.axis_size(axis)
    partner = [((i + outer) ^ 1) - outer for i in range(count)]
    return lax.ppermute(block, axis, [(i, p % count) for i, p in enumerate(partner)])


def eigenvalues(frequency):
    return 2.0 - 2.0 * jnp.cos((2.0 * jnp.pi / LINE) * frequency.astype(jnp.float32))


def per_device(state, memory, level_steps, building_height):
    plane = shaped(5, TILE, LEVELS)
    edges = call(edges_kernel, [plane] * 4, state)
    halos = [
        swapped(edges[i], axis, outer)
        for i, (axis, outer) in enumerate([("px", 1), ("px", 0), ("py", 1), ("py", 0)])
    ]

    steps = level_steps.reshape(1, LEVELS)
    own_x = lax.axis_index("py") * lax.axis_size("px") + lax.axis_index("px")
    shift = eigenvalues(jnp.arange(LINE, dtype=jnp.int32)) + eigenvalues(own_x)
    basis, after = jnp.asarray(BASIS), jnp.asarray(AFTER)
    vmem, hbm = pl.BlockSpec(memory_space=pltpu.VMEM), pl.BlockSpec(memory_space=pltpu.HBM)
    scratch = lambda *shape: pltpu.VMEM(shape, jnp.float32)
    sems = pltpu.SemaphoreType.DMA

    inner, fluid = call(
        interior_kernel,
        [shaped(3, TILE, TILE, LEVELS), shaped(TILE, TILE, LEVELS)],
        state, memory, steps, building_height,
        flops=10**7,
    )
    message = call(
        momentum_kernel,
        shaped(TILE, TILE, WIDE),
        state, inner, fluid, *halos, steps,
        flops=10**7,
        scratch_shapes=[scratch(3, TILE, TILE, LEVELS)],
    )
    provisional, updated, fluid = call(
        side_kernel,
        [
            shaped(3, TILE, TILE, LEVELS),
            shaped(5, TILE, TILE, LEVELS),
            shaped(TILE, TILE, LEVELS),
        ],
        state, memory, *halos, steps, building_height,
        flops=2 * 10**7,
        vmem=MOST_VMEM,
        in_specs=[hbm] * 6 + [vmem] * 2,
        out_specs=[hbm] * 3,
        scratch_shapes=[
            scratch(5, TILE, TILE, LEVELS),
            scratch(5, TILE, TILE, LEVELS),
            scratch(4, 5, TILE, LEVELS),
            scratch(TILE, TILE, LEVELS),
            scratch(5, TILE, TILE, LEVELS),
            sems((9,)),
        ],
    )
    lines = lax.all_to_all(message, "px", split_axis=0, concat_axis=0, tiled=True)
    spectrum = call(
        forward_kernel, shaped(LINE, 1, WIDE), lines.reshape(LINE, WIDE), basis, after
    )
    lines = lax.all_to_all(spectrum, ("py", "px"), split_axis=0, concat_axis=0, tiled=True)
    lines, provisional = lax.optimization_barrier((lines, provisional))
    solved = call(
        solve_kernel, shaped(LINE, 1, WIDE), lines, basis, after, steps, shift.reshape(1, LINE)
    )
    lines = lax.all_to_all(solved, ("py", "px"), split_axis=0, concat_axis=0, tiled=True)
    message = call(backward_kernel, shaped(LINE, WIDE), lines, basis, after)
    message = lax.all_to_all(
        message.reshape(TILE, TILE, WIDE), "px", split_axis=0, concat_axis=0, tiled=True
    )
    return call(
        correct_kernel,
        [shaped(5, TILE, TILE, LEVELS), shaped(TILE, TILE, LEVELS)],
        message, provisional, steps, fluid, updated,
        in_specs=[vmem] * 4 + [hbm],
        out_specs=[hbm] * 2,
        input_output_aliases={4: 0},
        scratch_shapes=[
            scratch(3, TILE, TILE, LEVELS), scratch(TILE, TILE, LEVELS), sems((2 * TILE // PART,))
        ],
    )


def solution(mesh):
    return jax.shard_map(
        per_device,
        mesh=mesh,
        in_specs=(P(None, "px", "py", None), P(None, "px", "py", None), P(), P("px", "py")),
        out_specs=(P(None, "px", "py", None), P("px", "py", None)),
        check_vma=False,
    )
```

```python
import jax
import jax.numpy as jnp
import numpy as np
from jax import lax
from jax.experimental import pallas as pl
from jax.experimental.pallas import tpu as pltpu
from jax.sharding import PartitionSpec as P

RK_KEEP = -5.0 / 9.0
RK_STEP = 15.0 / 16.0
TIME_STEP = 0.1
DIFFUSION = 0.05
BUOYANCY = 0.3
HIGHEST = lax.Precision.HIGHEST

TILE = 16
LINE = 256
LEVELS = 192
WIDE = 256
CHUNK = LEVELS // TILE
FIRST = 192
SECOND = 208
UNROLL = 3
MOST_VMEM = 48 * 1024 * 1024
STRIDES = (1, 2, 4, 8, 16, 32, 64, 128)


def table():
    n = np.arange(LINE)
    angles = 2.0 * np.pi / LINE * (np.outer(n, n) % LINE)
    basis = (np.cos(angles) + np.sin(angles)) / np.sqrt(LINE)
    return basis.astype(np.float32)


BASIS = table()


def product(a, b, contract=((1,), (0,))):
    return lax.dot_general(
        a, b, (contract, ((), ())), precision=HIGHEST, preferred_element_type=jnp.float32
    )


def picked(values, places):
    high = values.astype(jnp.bfloat16)
    rest = values - high.astype(jnp.float32)
    middle = rest.astype(jnp.bfloat16)
    low = (rest - middle.astype(jnp.float32)).astype(jnp.bfloat16)
    dots = [
        jnp.dot(part, places, preferred_element_type=jnp.float32) for part in (low, middle, high)
    ]
    return (dots[0] + dots[1]) + dots[2]


def chunk_place(shape, level_dim, first):
    level = lax.broadcasted_iota(jnp.int32, shape, level_dim)
    lane = lax.broadcasted_iota(jnp.int32, shape, 1 - level_dim)
    chunk = jnp.floor((level.astype(jnp.float32) + 0.5) * (1.0 / CHUNK)).astype(jnp.int32)
    here = (level - chunk * CHUNK + (first - 128) == lane) & (level < LEVELS)
    return jnp.where(here, 1.0, 0.0).astype(jnp.bfloat16)


def pack_places(first):
    return chunk_place((WIDE, 128), 0, first)


def unpack_places(first):
    return chunk_place((128, WIDE), 1, first)


def each_block(rows):
    return jnp.concatenate(
        [jnp.broadcast_to(rows[b : b + 1], (TILE, rows.shape[1])) for b in range(TILE)], axis=0
    )


def level_rows(level_steps):
    thickness = level_steps[...].astype(jnp.float32)
    spacing = 0.5 * (thickness + lanes_up(thickness))
    return thickness, spacing


def block_mask():
    lane = lax.broadcasted_iota(jnp.int32, (TILE, WIDE), 1)
    start = lax.broadcasted_iota(jnp.int32, (TILE, WIDE), 0) * CHUNK
    return (lane >= start) & (lane < start + CHUNK)


def lanes_up(a):
    return jnp.concatenate([a[:, 1:], a[:, -1:]], axis=1)


def lanes_down(a):
    return jnp.concatenate([jnp.zeros_like(a[:, :1]), a[:, :-1]], axis=1)


def odd(axis):
    return lax.rem(lax.axis_index(axis), 2) == 1


def edges_kernel(state, x_outer, x_inner, y_outer, y_inner):
    low, high = state[:, 0], state[:, TILE - 1]
    x_outer[...] = jnp.where(odd("px"), high, low)
    x_inner[...] = jnp.where(odd("px"), low, high)
    low, high = state[:, :, 0], state[:, :, TILE - 1]
    y_outer[...] = jnp.where(odd("py"), high, low)
    y_inner[...] = jnp.where(odd("py"), low, high)


def faces(s, e, u):
    return e * (DIFFUSION - 0.5 * u) - s * (DIFFUSION + 0.5 * u)


def advance_fields(fields, state, memory, halos, level_steps, fluid, store):
    thickness, spacing = level_rows(level_steps)
    inv_thick = 1.0 / thickness
    inv_space = 1.0 / spacing
    nothing = jnp.zeros((TILE, LEVELS), jnp.float32)
    if halos:
        west, east, south, north = halos

    def plane(x, before, east_of):
        u = state[0, x]
        v = state[1, x]
        w = state[2, x]
        u_to, u_from = DIFFUSION - 0.5 * u, DIFFUSION + 0.5 * u
        v_to, v_from = DIFFUSION - 0.5 * v, DIFFUSION + 0.5 * v
        w_to, w_from = DIFFUSION * inv_space - 0.5 * w, DIFFUSION * inv_space + 0.5 * w
        factor = (RK_STEP * TIME_STEP) * fluid[x]
        after = []
        for i, f in enumerate(fields):
            s = state[f, x]
            x_face = east_of(f) * u_to - s * u_from if east_of else nothing
            last_y, first_y = nothing[:1], nothing[:1]
            if halos:
                last_y = faces(s[TILE - 1 :], north[f, pl.ds(x, 1)], v[TILE - 1 :])
                first_y = faces(south[f, pl.ds(x, 1)], s[:1], south[1, pl.ds(x, 1)])
            y_face = jnp.concatenate([s[1:], s[:1]], axis=0) * v_to - s * v_from
            y_above = jnp.concatenate([y_face[:-1], last_y], axis=0)
            y_below = jnp.concatenate([first_y, y_face[:-1]], axis=0)
            z_face = lanes_up(s) * w_to - s * w_from
            change = (x_face - before[i]) + (y_above - y_below)
            change = change + (z_face - lanes_down(z_face)) * inv_thick
            if f == 2:
                change = change + BUOYANCY * state[3, x]
            after.append(x_face)
            store(f, x, s + (RK_STEP * RK_KEEP) * memory[f, x] + factor * change)
        return tuple(after)

    before = tuple(
        faces(west[f], state[f, 0], west[0]) if halos else nothing for f in fields
    )
    before = lax.fori_loop(
        0, TILE - 1, lambda x, b: plane(x, b, lambda f: state[f, x + 1]), before, unroll=UNROLL
    )
    plane(TILE - 1, before, (lambda f: east[f]) if halos else None)


PART = 4


def parts_of(x):
    return pl.ds(x + 1 - PART, PART) if x % PART == PART - 1 else None


def fill_fluid(height, fluid):
    heights = each_block(height[...].astype(jnp.float32))
    row = lax.broadcasted_iota(jnp.int32, (LINE, TILE), 0)
    own = row % TILE == lax.broadcasted_iota(jnp.int32, (LINE, TILE), 1)
    bottom = jnp.sum(jnp.where(own, heights, 0.0), axis=1, keepdims=True)
    level = lax.broadcasted_iota(jnp.int32, (TILE, LEVELS), 1).astype(jnp.float32)
    for x in range(TILE):
        fluid[x] = jnp.where(level >= bottom[x * TILE : (x + 1) * TILE], 1.0, 0.0)


def interior_kernel(state, memory, level_steps, height, provisional, fluid):
    fill_fluid(height, fluid)

    def store(f, x, value):
        provisional[f, x] = value

    advance_fields((0, 1, 2), state, memory, None, level_steps, fluid, store)


def momentum_kernel(
    state, inner, fluid, x_outer, x_inner, y_outer, y_inner, level_steps, message, provisional
):
    provisional[...] = inner[...]
    odd_x, odd_y = odd("px"), odd("py")
    west = [jnp.where(odd_x, x_inner[f], x_outer[f]) for f in range(3)]
    east = [jnp.where(odd_x, x_outer[f], x_inner[f]) for f in range(3)]
    south = [jnp.where(odd_y, y_inner[f], y_outer[f]) for f in range(3)]
    north = [jnp.where(odd_y, y_outer[f], y_inner[f]) for f in range(3)]
    last, factor = TILE - 1, RK_STEP * TIME_STEP
    for f in range(3):
        provisional[f, 0] -= factor * fluid[0] * faces(west[f], state[f, 0], west[0])
        provisional[f, last] += factor * fluid[last] * faces(
            state[f, last], east[f], state[0, last]
        )
        provisional[f, :, 0] -= factor * fluid[:, 0] * faces(south[f], state[f, :, 0], south[1])
        provisional[f, :, last] += factor * fluid[:, last] * faces(
            state[f, :, last], north[f], state[1, :, last]
        )
    inv_thick = 1.0 / level_rows(level_steps)[0]
    zeros = jnp.zeros((TILE, WIDE - LEVELS), jnp.float32)
    mask = block_mask()
    last_u = jnp.concatenate([provisional[0, TILE - 1], zeros], axis=1)
    u_packed = jnp.concatenate(
        [jnp.where(mask, last_u[y : y + 1], 0.0) for y in range(TILE)], axis=0
    )
    last_v = jnp.concatenate([provisional[1, :, TILE - 1], zeros], axis=1)
    ones = jnp.where(mask, 1.0, 0.0)
    v_packed = jnp.concatenate([last_v * ones[y : y + 1] for y in range(TILE)], axis=0)
    upper = picked(u_packed, pack_places(FIRST)) + picked(v_packed, pack_places(SECOND))
    upper = upper.reshape(TILE, TILE, 128)
    for x in range(TILE):
        u = provisional[0, x]
        v = provisional[1, x]
        w = provisional[2, x]
        v_before = jnp.concatenate([jnp.zeros_like(v[:1]), v[:-1]], axis=0)
        diverge = (v - v_before) + (w - lanes_down(w)) * inv_thick
        diverge = diverge + (u - provisional[0, x - 1] if x else u)
        message[:, x, :128] = diverge[:, :128]
        message[:, x, 128:] = jnp.concatenate([diverge[:, 128:], zeros], axis=1) + upper[:, x]


def loaded(pairs, sems):
    copies = [pltpu.make_async_copy(a, b, sems.at[i]) for i, (a, b) in enumerate(pairs)]
    for copy in copies:
        copy.start()
    return copies


def unpacked(values, first, owner):
    spread = picked(values[:, 128:], unpack_places(first)).reshape(TILE, TILE, WIDE)
    mask = block_mask()
    if owner == "low":
        return jnp.where(mask[None], spread, 0.0).sum(axis=1)
    ones = jnp.where(mask, 1.0, 0.0)
    return sum(spread[b] * ones[b : b + 1] for b in range(TILE))


def lessened(values, first):
    extra = unpacked(values, first, "low")
    extra = jnp.concatenate([extra[TILE - 1 :], extra[: TILE - 1]], axis=0)
    blocks = values.reshape(TILE, TILE, WIDE)
    start = lax.broadcasted_iota(jnp.int32, blocks.shape, 1) == 0
    return jnp.where(start, blocks - extra[:, None, :], blocks).reshape(LINE, WIDE)


def repacked(back, first):
    mask = block_mask()
    rows = [back[b * TILE : b * TILE + 1] for b in range(TILE)]
    chunks = [jnp.where(mask, row, 0.0) for row in rows[1:] + rows[:1]]
    return picked(jnp.concatenate(chunks, axis=0), pack_places(first))


def forward_kernel(lines, basis, spectrum):
    spectrum[:, 0, :] = product(basis[...], lessened(lines[...], FIRST))


def column_of(row):
    shape = (LEVELS, LEVELS)
    own = lax.broadcasted_iota(jnp.int32, shape, 0) == lax.broadcasted_iota(jnp.int32, shape, 1)
    return jnp.sum(jnp.where(own, row, 0.0), axis=1, keepdims=True)


def reduced(diagonal, coupling, right):
    for stride in STRIDES:
        shared = LEVELS - stride
        reciprocal = 1.0 / diagonal
        near = coupling[:shared]
        from_above = near * reciprocal[stride:]
        from_below = near * reciprocal[:shared]
        gap = jnp.zeros((stride, right.shape[1]), jnp.float32)
        low = lambda a: jnp.concatenate([a, gap], axis=0)
        high = lambda a: jnp.concatenate([gap, a], axis=0)
        right = right - low(from_above * right[stride:]) - high(from_below * right[:shared])
        diagonal = diagonal - low(near * from_above) - high(near * from_below)
        if shared > stride:
            coupling = low(-from_above * coupling[stride:])
    return right / diagonal


def side_kernel(
    state, memory, x_outer, x_inner, y_outer, y_inner, level_steps, height,
    provisional, updated, fluid_kept, state_here, memory_here, halo_here, fluid, fields, sems,
):
    pairs = [(state, state_here), (memory, memory_here)]
    first_x, first_y = odd("px").astype(jnp.int32), odd("py").astype(jnp.int32)
    pairs += [(x_outer, halo_here.at[first_x]), (x_inner, halo_here.at[1 - first_x])]
    pairs += [(y_outer, halo_here.at[2 + first_y]), (y_inner, halo_here.at[3 - first_y])]
    arriving = loaded(pairs, sems)
    fill_fluid(height, fluid)
    leaving = loaded([(fluid, fluid_kept)], sems.at[pl.ds(6, 1)])
    for copy in arriving:
        copy.wait()

    def store(f, x, value):
        fields[f, x] = value

    advance_fields(
        (0, 1, 2, 3, 4), state_here, memory_here, [halo_here.at[i] for i in range(4)],
        level_steps, fluid, store,
    )
    pairs = [(fields.at[0:3], provisional), (fields.at[3:5], updated.at[3:5])]
    leaving += loaded(pairs, sems.at[pl.ds(7, 2)])
    for copy in leaving:
        copy.wait()


def solve_kernel(lines, basis, level_steps, shift, result, tiled):
    tiled[...] = lines[:, 0, :]
    thickness, spacing = level_rows(level_steps)
    level = lax.broadcasted_iota(jnp.int32, (1, LEVELS), 1)
    inv_space = 1.0 / spacing
    thick = column_of(thickness)
    diagonal = column_of(inv_space + lanes_down(inv_space)) + thick * shift[...]
    between = column_of(jnp.where(level < LEVELS - 1, -inv_space, 0.0))
    coupling = jnp.broadcast_to(between, (LEVELS, LINE))
    values = lessened(tiled[...], SECOND)
    main = product(values, basis[...], ((0,), (0,)))
    right = thick * (-main[:LEVELS])
    solved = reduced(diagonal, coupling, right)
    solved = jnp.concatenate([solved, jnp.zeros((WIDE - LEVELS, LINE), jnp.float32)], axis=0)
    back = product(basis[...], solved, ((1,), (1,)))
    result[:, 0, :128] = back[:, :128]
    result[:, 0, 128:] = back[:, 128:] + repacked(back, FIRST)


def backward_kernel(lines, basis, message, tiled):
    tiled[...] = lines[:, 0, :]
    back = product(basis[...], tiled[...])
    message[:, :128] = back[:, :128]
    message[:, 128:] = back[:, 128:] + repacked(back, SECOND)


def correct_kernel(
    message, provisional, level_steps, fluid, kept, updated, pressure, fields, cells, sems
):
    copies = []
    inv_space = 1.0 / level_rows(level_steps)[1]
    lines = message[...].reshape(LINE, WIDE)
    north = unpacked(lines, FIRST, "high")[:, :LEVELS]
    east = unpacked(lines, SECOND, "low")[:, :LEVELS]
    for x in range(TILE):
        p = message[:, x, :LEVELS]
        p_east = message[:, x + 1, :LEVELS] if x < TILE - 1 else east
        p_north = jnp.concatenate([p[1:], north[x : x + 1]], axis=0)
        p_upper = jnp.concatenate([p[:, 1:], jnp.zeros_like(p[:, :1])], axis=1)
        open_cell = fluid[x]
        fields[0, x] = open_cell * (provisional[0, x] - (p_east - p))
        fields[1, x] = open_cell * (provisional[1, x] - (p_north - p))
        fields[2, x] = open_cell * (provisional[2, x] - (p_upper - p) * inv_space)
        cells[x] = p
        part = parts_of(x)
        if part is not None:
            pairs = [(fields.at[:, part], updated.at[0:3, part]), (cells.at[part], pressure.at[part])]
            copies += loaded(pairs, sems.at[pl.ds(x // PART * 2, 2)])
    for copy in copies:
        copy.wait()


def shaped(*shape):
    return jax.ShapeDtypeStruct(shape, jnp.float32)


def call(kernel, out_shape, *operands, flops=0, vmem=12 * 1024 * 1024, **options):
    here = pl.BlockSpec(memory_space=pltpu.VMEM)
    options.setdefault("in_specs", [here] * len(operands))
    options.setdefault("out_specs", jax.tree.map(lambda _: here, out_shape))
    count = sum(int(np.prod(a.shape)) for a in operands) * 4
    return pl.pallas_call(
        kernel,
        out_shape=out_shape,
        name=kernel.__name__,
        compiler_params=pltpu.CompilerParams(vmem_limit_bytes=vmem),
        cost_estimate=pl.CostEstimate(flops=flops, bytes_accessed=count, transcendentals=0),
        **options,
    )(*operands)


def swapped(block, axis, outer):
    count = lax.axis_size(axis)
    partner = [((i + outer) ^ 1) - outer for i in range(count)]
    return lax.ppermute(block, axis, [(i, p % count) for i, p in enumerate(partner)])


def eigenvalues(frequency):
    return 2.0 - 2.0 * jnp.cos((2.0 * jnp.pi / LINE) * frequency.astype(jnp.float32))


def per_device(state, memory, level_steps, building_height):
    plane = shaped(5, TILE, LEVELS)
    edges = call(edges_kernel, [plane] * 4, state)
    halos = [
        swapped(edges[i], axis, outer)
        for i, (axis, outer) in enumerate([("px", 1), ("px", 0), ("py", 1), ("py", 0)])
    ]

    steps = level_steps.reshape(1, LEVELS)
    own_x = lax.axis_index("py") * lax.axis_size("px") + lax.axis_index("px")
    shift = eigenvalues(jnp.arange(LINE, dtype=jnp.int32)) + eigenvalues(own_x)
    basis = jnp.asarray(BASIS)
    vmem, hbm = pl.BlockSpec(memory_space=pltpu.VMEM), pl.BlockSpec(memory_space=pltpu.HBM)
    scratch = lambda *shape: pltpu.VMEM(shape, jnp.float32)
    sems = pltpu.SemaphoreType.DMA

    inner, fluid = call(
        interior_kernel,
        [shaped(3, TILE, TILE, LEVELS), shaped(TILE, TILE, LEVELS)],
        state, memory, steps, building_height,
        flops=10**7,
    )
    message = call(
        momentum_kernel,
        shaped(TILE, TILE, WIDE),
        state, inner, fluid, *halos, steps,
        flops=10**7,
        scratch_shapes=[scratch(3, TILE, TILE, LEVELS)],
    )
    provisional, updated, fluid = call(
        side_kernel,
        [
            shaped(3, TILE, TILE, LEVELS),
            shaped(5, TILE, TILE, LEVELS),
            shaped(TILE, TILE, LEVELS),
        ],
        state, memory, *halos, steps, building_height,
        flops=2 * 10**7,
        vmem=MOST_VMEM,
        in_specs=[hbm] * 6 + [vmem] * 2,
        out_specs=[hbm] * 3,
        scratch_shapes=[
            scratch(5, TILE, TILE, LEVELS),
            scratch(5, TILE, TILE, LEVELS),
            scratch(4, 5, TILE, LEVELS),
            scratch(TILE, TILE, LEVELS),
            scratch(5, TILE, TILE, LEVELS),
            sems((9,)),
        ],
    )
    lines = lax.all_to_all(message, "px", split_axis=0, concat_axis=0, tiled=True)
    spectrum = call(
        forward_kernel, shaped(LINE, 1, WIDE), lines.reshape(LINE, WIDE), basis
    )
    lines = lax.all_to_all(spectrum, ("py", "px"), split_axis=0, concat_axis=0, tiled=True)
    lines, provisional = lax.optimization_barrier((lines, provisional))
    solved = call(
        solve_kernel, shaped(LINE, 1, WIDE), lines, basis, steps, shift.reshape(1, LINE),
        scratch_shapes=[scratch(LINE, WIDE)],
    )
    lines = lax.all_to_all(solved, ("py", "px"), split_axis=0, concat_axis=0, tiled=True)
    message = call(
        backward_kernel, shaped(LINE, WIDE), lines, basis, scratch_shapes=[scratch(LINE, WIDE)]
    )
    message = lax.all_to_all(
        message.reshape(TILE, TILE, WIDE), "px", split_axis=0, concat_axis=0, tiled=True
    )
    return call(
        correct_kernel,
        [shaped(5, TILE, TILE, LEVELS), shaped(TILE, TILE, LEVELS)],
        message, provisional, steps, fluid, updated,
        in_specs=[vmem] * 4 + [hbm],
        out_specs=[hbm] * 2,
        input_output_aliases={4: 0},
        scratch_shapes=[
            scratch(3, TILE, TILE, LEVELS), scratch(TILE, TILE, LEVELS), sems((2 * TILE // PART,))
        ],
    )


def solution(mesh):
    return jax.shard_map(
        per_device,
        mesh=mesh,
        in_specs=(P(None, "px", "py", None), P(None, "px", "py", None), P(), P("px", "py")),
        out_specs=(P(None, "px", "py", None), P("px", "py", None)),
        check_vma=False,
    )
```

```python
import jax
import jax.numpy as jnp
import numpy as np
from jax import lax
from jax.experimental import pallas as pl
from jax.experimental.pallas import tpu as pltpu
from jax.sharding import PartitionSpec as P

RK_KEEP = -5.0 / 9.0
RK_STEP = 15.0 / 16.0
TIME_STEP = 0.1
DIFFUSION = 0.05
BUOYANCY = 0.3
HIGHEST = lax.Precision.HIGHEST

TILE = 16
LINE = 256
LEVELS = 192
WIDE = 256
CHUNK = LEVELS // TILE
FIELDS = 5
FIRST = 192
SECOND = 208
UNROLL = 3
STRIDES = (1, 2, 4, 8, 16, 32, 64, 128)


def table():
    n = np.arange(LINE)
    angles = 2.0 * np.pi / LINE * (np.outer(n, n) % LINE)
    basis = (np.cos(angles) + np.sin(angles)) / np.sqrt(LINE)
    return basis.astype(np.float32)


BASIS = table()


def product(a, b, contract=((1,), (0,))):
    return lax.dot_general(
        a, b, (contract, ((), ())), precision=HIGHEST, preferred_element_type=jnp.float32
    )


def picked(values, places):
    high = values.astype(jnp.bfloat16)
    rest = values - high.astype(jnp.float32)
    middle = rest.astype(jnp.bfloat16)
    low = (rest - middle.astype(jnp.float32)).astype(jnp.bfloat16)
    dots = [
        jnp.dot(part, places, preferred_element_type=jnp.float32) for part in (low, middle, high)
    ]
    return (dots[0] + dots[1]) + dots[2]


def chunk_place(shape, level_dim, first):
    level = lax.broadcasted_iota(jnp.int32, shape, level_dim)
    lane = lax.broadcasted_iota(jnp.int32, shape, 1 - level_dim)
    chunk = jnp.floor((level.astype(jnp.float32) + 0.5) * (1.0 / CHUNK)).astype(jnp.int32)
    here = (level - chunk * CHUNK + (first - 128) == lane) & (level < LEVELS)
    return jnp.where(here, 1.0, 0.0).astype(jnp.bfloat16)


def pack_places(first):
    return chunk_place((WIDE, 128), 0, first)


def unpack_places(first):
    return chunk_place((128, WIDE), 1, first)


def each_block(rows):
    return jnp.concatenate(
        [jnp.broadcast_to(rows[b : b + 1], (TILE, rows.shape[1])) for b in range(TILE)], axis=0
    )


def level_rows(level_steps):
    thickness = level_steps[...].astype(jnp.float32)
    spacing = 0.5 * (thickness + lanes_up(thickness))
    return thickness, spacing


def block_mask():
    lane = lax.broadcasted_iota(jnp.int32, (TILE, WIDE), 1)
    start = lax.broadcasted_iota(jnp.int32, (TILE, WIDE), 0) * CHUNK
    return (lane >= start) & (lane < start + CHUNK)


def lanes_up(a):
    return jnp.concatenate([a[:, 1:], a[:, -1:]], axis=1)


def lanes_down(a):
    return jnp.concatenate([jnp.zeros_like(a[:, :1]), a[:, :-1]], axis=1)


def odd(axis):
    return lax.rem(lax.axis_index(axis), 2) == 1


def edges_kernel(state, x_outer, x_inner, y_outer, y_inner):
    low, high = state[:, 0], state[:, TILE - 1]
    x_outer[...] = jnp.where(odd("px"), high, low)
    x_inner[...] = jnp.where(odd("px"), low, high)
    low, high = state[:, :, 0], state[:, :, TILE - 1]
    y_outer[...] = jnp.where(odd("py"), high, low)
    y_inner[...] = jnp.where(odd("py"), low, high)


def faces(s, e, u):
    return e * (DIFFUSION - 0.5 * u) - s * (DIFFUSION + 0.5 * u)


def advance_fields(state, memory, level_steps, fluid, store):
    thickness, spacing = level_rows(level_steps)
    inv_thick = 1.0 / thickness
    inv_space = 1.0 / spacing
    nothing = jnp.zeros((TILE, LEVELS), jnp.float32)

    def plane(x, before, east_of):
        u = state[0, x]
        v = state[1, x]
        w = state[2, x]
        u_to, u_from = DIFFUSION - 0.5 * u, DIFFUSION + 0.5 * u
        v_to, v_from = DIFFUSION - 0.5 * v, DIFFUSION + 0.5 * v
        w_to, w_from = DIFFUSION * inv_space - 0.5 * w, DIFFUSION * inv_space + 0.5 * w
        factor = (RK_STEP * TIME_STEP) * fluid[x]
        after = []
        for f in range(FIELDS):
            s = state[f, x]
            x_face = east_of(f) * u_to - s * u_from if east_of else nothing
            y_face = jnp.concatenate([s[1:], s[:1]], axis=0) * v_to - s * v_from
            y_above = jnp.concatenate([y_face[:-1], nothing[:1]], axis=0)
            y_below = jnp.concatenate([nothing[:1], y_face[:-1]], axis=0)
            z_face = lanes_up(s) * w_to - s * w_from
            change = (x_face - before[f]) + (y_above - y_below)
            change = change + (z_face - lanes_down(z_face)) * inv_thick
            if f == 2:
                change = change + BUOYANCY * state[3, x]
            after.append(x_face)
            store(f, x, s + (RK_STEP * RK_KEEP) * memory[f, x] + factor * change)
        return tuple(after)

    before = (nothing,) * FIELDS
    before = lax.fori_loop(
        0, TILE - 1, lambda x, b: plane(x, b, lambda f: state[f, x + 1]), before, unroll=UNROLL
    )
    plane(TILE - 1, before, None)


PART = 4


def parts_of(x):
    return pl.ds(x + 1 - PART, PART) if x % PART == PART - 1 else None


def fill_fluid(height, fluid):
    heights = each_block(height[...].astype(jnp.float32))
    row = lax.broadcasted_iota(jnp.int32, (LINE, TILE), 0)
    own = row % TILE == lax.broadcasted_iota(jnp.int32, (LINE, TILE), 1)
    bottom = jnp.sum(jnp.where(own, heights, 0.0), axis=1, keepdims=True)
    level = lax.broadcasted_iota(jnp.int32, (TILE, LEVELS), 1).astype(jnp.float32)
    for x in range(TILE):
        fluid[x] = jnp.where(level >= bottom[x * TILE : (x + 1) * TILE], 1.0, 0.0)


def interior_kernel(state, memory, level_steps, height, provisional, fluid):
    fill_fluid(height, fluid)

    def store(f, x, value):
        provisional[f, x] = value

    advance_fields(state, memory, level_steps, fluid, store)


def sides(field, x_outer, x_inner, y_outer, y_inner):
    odd_x, odd_y = odd("px"), odd("py")
    return (
        jnp.where(odd_x, x_inner[field], x_outer[field]),
        jnp.where(odd_x, x_outer[field], x_inner[field]),
        jnp.where(odd_y, y_inner[field], y_outer[field]),
        jnp.where(odd_y, y_outer[field], y_inner[field]),
    )


def add_outer_faces(total, target, edges, halos, fluid):
    last, factor = TILE - 1, RK_STEP * TIME_STEP
    west_u, south_v = sides(0, *halos)[0], sides(1, *halos)[2]
    east_u, north_v = sides(0, *edges)[1], sides(1, *edges)[3]
    for f in range(total):
        x_low, x_high, y_low, y_high = sides(f, *edges)
        west, east, south, north = sides(f, *halos)
        target[f, 0] -= factor * fluid[0] * faces(west, x_low, west_u)
        target[f, last] += factor * fluid[last] * faces(x_high, east, east_u)
        target[f, :, 0] -= factor * fluid[:, 0] * faces(south, y_low, south_v)
        target[f, :, last] += factor * fluid[:, last] * faces(y_high, north, north_v)


def momentum_kernel(inner, fluid, *rest):
    edges, halos, (level_steps, message, provisional) = rest[:4], rest[4:8], rest[8:]
    provisional[...] = inner[0:3]
    add_outer_faces(3, provisional, edges, halos, fluid)
    inv_thick = 1.0 / level_rows(level_steps)[0]
    zeros = jnp.zeros((TILE, WIDE - LEVELS), jnp.float32)
    mask = block_mask()
    last_u = jnp.concatenate([provisional[0, TILE - 1], zeros], axis=1)
    u_packed = jnp.concatenate(
        [jnp.where(mask, last_u[y : y + 1], 0.0) for y in range(TILE)], axis=0
    )
    last_v = jnp.concatenate([provisional[1, :, TILE - 1], zeros], axis=1)
    ones = jnp.where(mask, 1.0, 0.0)
    v_packed = jnp.concatenate([last_v * ones[y : y + 1] for y in range(TILE)], axis=0)
    upper = picked(u_packed, pack_places(FIRST)) + picked(v_packed, pack_places(SECOND))
    upper = upper.reshape(TILE, TILE, 128)
    for x in range(TILE):
        u = provisional[0, x]
        v = provisional[1, x]
        w = provisional[2, x]
        v_before = jnp.concatenate([jnp.zeros_like(v[:1]), v[:-1]], axis=0)
        diverge = (v - v_before) + (w - lanes_down(w)) * inv_thick
        diverge = diverge + (u - provisional[0, x - 1] if x else u)
        message[:, x, :128] = diverge[:, :128]
        message[:, x, 128:] = jnp.concatenate([diverge[:, 128:], zeros], axis=1) + upper[:, x]


def loaded(pairs, sems):
    copies = [pltpu.make_async_copy(a, b, sems.at[i]) for i, (a, b) in enumerate(pairs)]
    for copy in copies:
        copy.start()
    return copies


def unpacked(values, first, owner):
    spread = picked(values[:, 128:], unpack_places(first)).reshape(TILE, TILE, WIDE)
    mask = block_mask()
    if owner == "low":
        return jnp.where(mask[None], spread, 0.0).sum(axis=1)
    ones = jnp.where(mask, 1.0, 0.0)
    return sum(spread[b] * ones[b : b + 1] for b in range(TILE))


def lessened(values, first):
    extra = unpacked(values, first, "low")
    extra = jnp.concatenate([extra[TILE - 1 :], extra[: TILE - 1]], axis=0)
    blocks = values.reshape(TILE, TILE, WIDE)
    start = lax.broadcasted_iota(jnp.int32, blocks.shape, 1) == 0
    return jnp.where(start, blocks - extra[:, None, :], blocks).reshape(LINE, WIDE)


def repacked(back, first):
    mask = block_mask()
    rows = [back[b * TILE : b * TILE + 1] for b in range(TILE)]
    chunks = [jnp.where(mask, row, 0.0) for row in rows[1:] + rows[:1]]
    return picked(jnp.concatenate(chunks, axis=0), pack_places(first))


def forward_kernel(lines, basis, spectrum):
    spectrum[:, 0, :] = product(basis[...], lessened(lines[...], FIRST))


def column_of(row):
    shape = (LEVELS, LEVELS)
    own = lax.broadcasted_iota(jnp.int32, shape, 0) == lax.broadcasted_iota(jnp.int32, shape, 1)
    return jnp.sum(jnp.where(own, row, 0.0), axis=1, keepdims=True)


def reduced(diagonal, coupling, right):
    for stride in STRIDES:
        shared = LEVELS - stride
        reciprocal = 1.0 / diagonal
        near = coupling[:shared]
        from_above = near * reciprocal[stride:]
        from_below = near * reciprocal[:shared]
        gap = jnp.zeros((stride, right.shape[1]), jnp.float32)
        low = lambda a: jnp.concatenate([a, gap], axis=0)
        high = lambda a: jnp.concatenate([gap, a], axis=0)
        right = right - low(from_above * right[stride:]) - high(from_below * right[:shared])
        diagonal = diagonal - low(near * from_above) - high(near * from_below)
        if shared > stride:
            coupling = low(-from_above * coupling[stride:])
    return right / diagonal


def solve_kernel(lines, basis, level_steps, shift, result, tiled):
    tiled[...] = lines[:, 0, :]
    thickness, spacing = level_rows(level_steps)
    level = lax.broadcasted_iota(jnp.int32, (1, LEVELS), 1)
    inv_space = 1.0 / spacing
    thick = column_of(thickness)
    diagonal = column_of(inv_space + lanes_down(inv_space)) + thick * shift[...]
    between = column_of(jnp.where(level < LEVELS - 1, -inv_space, 0.0))
    coupling = jnp.broadcast_to(between, (LEVELS, LINE))
    values = lessened(tiled[...], SECOND)
    main = product(values, basis[...], ((0,), (0,)))
    right = thick * (-main[:LEVELS])
    solved = reduced(diagonal, coupling, right)
    solved = jnp.concatenate([solved, jnp.zeros((WIDE - LEVELS, LINE), jnp.float32)], axis=0)
    back = product(basis[...], solved, ((1,), (1,)))
    result[:, 0, :128] = back[:, :128]
    result[:, 0, 128:] = back[:, 128:] + repacked(back, FIRST)


def backward_kernel(lines, basis, message, tiled):
    tiled[...] = lines[:, 0, :]
    back = product(basis[...], tiled[...])
    message[:, :128] = back[:, :128]
    message[:, 128:] = back[:, 128:] + repacked(back, SECOND)


def correct_kernel(message, inner, fluid, *rest):
    edges, halos, level_steps = rest[:4], rest[4:8], rest[8]
    updated, pressure, fields, cells, sems = rest[9:]
    fields[...] = inner[...]
    add_outer_faces(FIELDS, fields, edges, halos, fluid)
    copies = loaded([(fields.at[3:5], updated.at[3:5])], sems.at[pl.ds(2 * TILE // PART, 1)])
    inv_space = 1.0 / level_rows(level_steps)[1]
    lines = message[...].reshape(LINE, WIDE)
    north = unpacked(lines, FIRST, "high")[:, :LEVELS]
    east = unpacked(lines, SECOND, "low")[:, :LEVELS]
    for x in range(TILE):
        p = message[:, x, :LEVELS]
        p_east = message[:, x + 1, :LEVELS] if x < TILE - 1 else east
        p_north = jnp.concatenate([p[1:], north[x : x + 1]], axis=0)
        p_upper = jnp.concatenate([p[:, 1:], jnp.zeros_like(p[:, :1])], axis=1)
        open_cell = fluid[x]
        fields[0, x] = open_cell * (fields[0, x] - (p_east - p))
        fields[1, x] = open_cell * (fields[1, x] - (p_north - p))
        fields[2, x] = open_cell * (fields[2, x] - (p_upper - p) * inv_space)
        cells[x] = p
        part = parts_of(x)
        if part is not None:
            pairs = [(fields.at[0:3, part], updated.at[0:3, part]), (cells.at[part], pressure.at[part])]
            copies += loaded(pairs, sems.at[pl.ds(x // PART * 2, 2)])
    for copy in copies:
        copy.wait()


def shaped(*shape):
    return jax.ShapeDtypeStruct(shape, jnp.float32)


def call(kernel, out_shape, *operands, flops=0, **options):
    here = pl.BlockSpec(memory_space=pltpu.VMEM)
    options.setdefault("in_specs", [here] * len(operands))
    options.setdefault("out_specs", jax.tree.map(lambda _: here, out_shape))
    count = sum(int(np.prod(a.shape)) for a in operands) * 4
    return pl.pallas_call(
        kernel,
        out_shape=out_shape,
        name=kernel.__name__,
        compiler_params=pltpu.CompilerParams(vmem_limit_bytes=12 * 1024 * 1024),
        cost_estimate=pl.CostEstimate(flops=flops, bytes_accessed=count, transcendentals=0),
        **options,
    )(*operands)


def swapped(block, axis, outer):
    count = lax.axis_size(axis)
    partner = [((i + outer) ^ 1) - outer for i in range(count)]
    return lax.ppermute(block, axis, [(i, p % count) for i, p in enumerate(partner)])


def eigenvalues(frequency):
    return 2.0 - 2.0 * jnp.cos((2.0 * jnp.pi / LINE) * frequency.astype(jnp.float32))


def per_device(state, memory, level_steps, building_height):
    plane = shaped(5, TILE, LEVELS)
    edges = call(edges_kernel, [plane] * 4, state)
    halos = [
        swapped(edges[i], axis, outer)
        for i, (axis, outer) in enumerate([("px", 1), ("px", 0), ("py", 1), ("py", 0)])
    ]

    steps = level_steps.reshape(1, LEVELS)
    own_x = lax.axis_index("py") * lax.axis_size("px") + lax.axis_index("px")
    shift = eigenvalues(jnp.arange(LINE, dtype=jnp.int32)) + eigenvalues(own_x)
    basis = jnp.asarray(BASIS)
    hbm = pl.BlockSpec(memory_space=pltpu.HBM)
    scratch = lambda *shape: pltpu.VMEM(shape, jnp.float32)
    sems = pltpu.SemaphoreType.DMA

    inner, fluid = call(
        interior_kernel,
        [shaped(FIELDS, TILE, TILE, LEVELS), shaped(TILE, TILE, LEVELS)],
        state, memory, steps, building_height,
        flops=10**7,
    )
    inner, shift = lax.optimization_barrier((inner, shift.reshape(1, LINE)))
    message = call(
        momentum_kernel,
        shaped(TILE, TILE, WIDE),
        inner, fluid, *edges, *halos, steps,
        flops=10**7,
        scratch_shapes=[scratch(3, TILE, TILE, LEVELS)],
    )
    lines = lax.all_to_all(message, "px", split_axis=0, concat_axis=0, tiled=True)
    spectrum = call(
        forward_kernel, shaped(LINE, 1, WIDE), lines.reshape(LINE, WIDE), basis
    )
    lines = lax.all_to_all(spectrum, ("py", "px"), split_axis=0, concat_axis=0, tiled=True)
    solved = call(
        solve_kernel, shaped(LINE, 1, WIDE), lines, basis, steps, shift,
        scratch_shapes=[scratch(LINE, WIDE)],
    )
    lines = lax.all_to_all(solved, ("py", "px"), split_axis=0, concat_axis=0, tiled=True)
    message = call(
        backward_kernel, shaped(LINE, WIDE), lines, basis, scratch_shapes=[scratch(LINE, WIDE)]
    )
    message = lax.all_to_all(
        message.reshape(TILE, TILE, WIDE), "px", split_axis=0, concat_axis=0, tiled=True
    )
    return call(
        correct_kernel,
        [shaped(5, TILE, TILE, LEVELS), shaped(TILE, TILE, LEVELS)],
        message, inner, fluid, *edges, *halos, steps,
        out_specs=[hbm] * 2,
        scratch_shapes=[
            scratch(FIELDS, TILE, TILE, LEVELS),
            scratch(TILE, TILE, LEVELS),
            sems((2 * TILE // PART + 1,)),
        ],
    )


def solution(mesh):
    return jax.shard_map(
        per_device,
        mesh=mesh,
        in_specs=(P(None, "px", "py", None), P(None, "px", "py", None), P(), P("px", "py")),
        out_specs=(P(None, "px", "py", None), P("px", "py", None)),
        check_vma=False,
    )
```

```python
import jax
import jax.numpy as jnp
import numpy as np
from jax import lax
from jax.experimental import pallas as pl
from jax.experimental.pallas import tpu as pltpu
from jax.sharding import PartitionSpec as P

RK_KEEP = -5.0 / 9.0
RK_STEP = 15.0 / 16.0
TIME_STEP = 0.1
DIFFUSION = 0.05
BUOYANCY = 0.3
HIGHEST = lax.Precision.HIGHEST

TILE = 16
LINE = 256
LEVELS = 192
WIDE = 256
CHUNK = LEVELS // TILE
FIELDS = 5
FIRST = 192
SECOND = 208
UNROLL = 3


def table():
    n = np.arange(LINE)
    angles = 2.0 * np.pi / LINE * (np.outer(n, n) % LINE)
    basis = (np.cos(angles) + np.sin(angles)) / np.sqrt(LINE)
    return basis.astype(np.float32)


BASIS = table()


def product(a, b, contract=((1,), (0,))):
    return lax.dot_general(
        a, b, (contract, ((), ())), precision=HIGHEST, preferred_element_type=jnp.float32
    )


def picked(values, places):
    high = values.astype(jnp.bfloat16)
    rest = values - high.astype(jnp.float32)
    middle = rest.astype(jnp.bfloat16)
    low = (rest - middle.astype(jnp.float32)).astype(jnp.bfloat16)
    dots = [
        jnp.dot(part, places, preferred_element_type=jnp.float32) for part in (low, middle, high)
    ]
    return (dots[0] + dots[1]) + dots[2]


def chunk_place(shape, level_dim, first):
    level = lax.broadcasted_iota(jnp.int32, shape, level_dim)
    lane = lax.broadcasted_iota(jnp.int32, shape, 1 - level_dim)
    chunk = jnp.floor((level.astype(jnp.float32) + 0.5) * (1.0 / CHUNK)).astype(jnp.int32)
    here = (level - chunk * CHUNK + (first - 128) == lane) & (level < LEVELS)
    return jnp.where(here, 1.0, 0.0).astype(jnp.bfloat16)


def pack_places(first):
    return chunk_place((WIDE, 128), 0, first)


def unpack_places(first):
    return chunk_place((128, WIDE), 1, first)


def each_block(rows):
    return jnp.concatenate(
        [jnp.broadcast_to(rows[b : b + 1], (TILE, rows.shape[1])) for b in range(TILE)], axis=0
    )


def level_rows(level_steps):
    thickness = level_steps[...].astype(jnp.float32)
    spacing = 0.5 * (thickness + lanes_up(thickness))
    return thickness, spacing


def block_mask():
    lane = lax.broadcasted_iota(jnp.int32, (TILE, WIDE), 1)
    start = lax.broadcasted_iota(jnp.int32, (TILE, WIDE), 0) * CHUNK
    return (lane >= start) & (lane < start + CHUNK)


def lanes_up(a):
    return jnp.concatenate([a[:, 1:], a[:, -1:]], axis=1)


def lanes_down(a):
    return jnp.concatenate([jnp.zeros_like(a[:, :1]), a[:, :-1]], axis=1)


def odd(axis):
    return lax.rem(lax.axis_index(axis), 2) == 1


def edges_kernel(state, x_outer, x_inner, y_outer, y_inner):
    low, high = state[:, 0], state[:, TILE - 1]
    x_outer[...] = jnp.where(odd("px"), high, low)
    x_inner[...] = jnp.where(odd("px"), low, high)
    low, high = state[:, :, 0], state[:, :, TILE - 1]
    y_outer[...] = jnp.where(odd("py"), high, low)
    y_inner[...] = jnp.where(odd("py"), low, high)


def faces(s, e, u):
    return e * (DIFFUSION - 0.5 * u) - s * (DIFFUSION + 0.5 * u)


def advance_fields(state, memory, level_steps, fluid, store):
    thickness, spacing = level_rows(level_steps)
    inv_thick = 1.0 / thickness
    inv_space = 1.0 / spacing
    nothing = jnp.zeros((TILE, LEVELS), jnp.float32)

    def plane(x, before, east_of):
        u = state[0, x]
        v = state[1, x]
        w = state[2, x]
        u_to, u_from = DIFFUSION - 0.5 * u, DIFFUSION + 0.5 * u
        v_to, v_from = DIFFUSION - 0.5 * v, DIFFUSION + 0.5 * v
        w_to, w_from = DIFFUSION * inv_space - 0.5 * w, DIFFUSION * inv_space + 0.5 * w
        factor = (RK_STEP * TIME_STEP) * fluid[x]
        after = []
        for f in range(FIELDS):
            s = state[f, x]
            x_face = east_of(f) * u_to - s * u_from if east_of else nothing
            y_face = jnp.concatenate([s[1:], s[:1]], axis=0) * v_to - s * v_from
            y_above = jnp.concatenate([y_face[:-1], nothing[:1]], axis=0)
            y_below = jnp.concatenate([nothing[:1], y_face[:-1]], axis=0)
            z_face = lanes_up(s) * w_to - s * w_from
            change = (x_face - before[f]) + (y_above - y_below)
            change = change + (z_face - lanes_down(z_face)) * inv_thick
            if f == 2:
                change = change + BUOYANCY * state[3, x]
            after.append(x_face)
            store(f, x, s + (RK_STEP * RK_KEEP) * memory[f, x] + factor * change)
        return tuple(after)

    before = (nothing,) * FIELDS
    before = lax.fori_loop(
        0, TILE - 1, lambda x, b: plane(x, b, lambda f: state[f, x + 1]), before, unroll=UNROLL
    )
    plane(TILE - 1, before, None)


PART = 4


def parts_of(x):
    return pl.ds(x + 1 - PART, PART) if x % PART == PART - 1 else None


def fill_fluid(height, fluid):
    heights = each_block(height[...].astype(jnp.float32))
    row = lax.broadcasted_iota(jnp.int32, (LINE, TILE), 0)
    own = row % TILE == lax.broadcasted_iota(jnp.int32, (LINE, TILE), 1)
    bottom = jnp.sum(jnp.where(own, heights, 0.0), axis=1, keepdims=True)
    level = lax.broadcasted_iota(jnp.int32, (TILE, LEVELS), 1).astype(jnp.float32)
    for x in range(TILE):
        fluid[x] = jnp.where(level >= bottom[x * TILE : (x + 1) * TILE], 1.0, 0.0)


def interior_kernel(state, memory, level_steps, height, provisional, fluid):
    fill_fluid(height, fluid)

    def store(f, x, value):
        provisional[f, x] = value

    advance_fields(state, memory, level_steps, fluid, store)


def sides(field, x_outer, x_inner, y_outer, y_inner):
    odd_x, odd_y = odd("px"), odd("py")
    return (
        jnp.where(odd_x, x_inner[field], x_outer[field]),
        jnp.where(odd_x, x_outer[field], x_inner[field]),
        jnp.where(odd_y, y_inner[field], y_outer[field]),
        jnp.where(odd_y, y_outer[field], y_inner[field]),
    )


def add_outer_faces(total, target, edges, halos, fluid):
    last, factor = TILE - 1, RK_STEP * TIME_STEP
    west_u, south_v = sides(0, *halos)[0], sides(1, *halos)[2]
    east_u, north_v = sides(0, *edges)[1], sides(1, *edges)[3]
    for f in range(total):
        x_low, x_high, y_low, y_high = sides(f, *edges)
        west, east, south, north = sides(f, *halos)
        target[f, 0] -= factor * fluid[0] * faces(west, x_low, west_u)
        target[f, last] += factor * fluid[last] * faces(x_high, east, east_u)
        target[f, :, 0] -= factor * fluid[:, 0] * faces(south, y_low, south_v)
        target[f, :, last] += factor * fluid[:, last] * faces(y_high, north, north_v)


def momentum_kernel(inner, fluid, *rest):
    edges, halos, (level_steps, message, provisional) = rest[:4], rest[4:8], rest[8:]
    provisional[...] = inner[0:3]
    add_outer_faces(3, provisional, edges, halos, fluid)
    inv_thick = 1.0 / level_rows(level_steps)[0]
    zeros = jnp.zeros((TILE, WIDE - LEVELS), jnp.float32)
    mask = block_mask()
    last_u = jnp.concatenate([provisional[0, TILE - 1], zeros], axis=1)
    u_packed = jnp.concatenate(
        [jnp.where(mask, last_u[y : y + 1], 0.0) for y in range(TILE)], axis=0
    )
    last_v = jnp.concatenate([provisional[1, :, TILE - 1], zeros], axis=1)
    ones = jnp.where(mask, 1.0, 0.0)
    v_packed = jnp.concatenate([last_v * ones[y : y + 1] for y in range(TILE)], axis=0)
    upper = picked(u_packed, pack_places(FIRST)) + picked(v_packed, pack_places(SECOND))
    upper = upper.reshape(TILE, TILE, 128)
    for x in range(TILE):
        u = provisional[0, x]
        v = provisional[1, x]
        w = provisional[2, x]
        v_before = jnp.concatenate([jnp.zeros_like(v[:1]), v[:-1]], axis=0)
        diverge = (v - v_before) + (w - lanes_down(w)) * inv_thick
        diverge = diverge + (u - provisional[0, x - 1] if x else u)
        message[:, x, :128] = diverge[:, :128]
        message[:, x, 128:] = jnp.concatenate([diverge[:, 128:], zeros], axis=1) + upper[:, x]


def loaded(pairs, sems):
    copies = [pltpu.make_async_copy(a, b, sems.at[i]) for i, (a, b) in enumerate(pairs)]
    for copy in copies:
        copy.start()
    return copies


def unpacked(values, first, owner):
    spread = picked(values[:, 128:], unpack_places(first)).reshape(TILE, TILE, WIDE)
    mask = block_mask()
    if owner == "low":
        return jnp.where(mask[None], spread, 0.0).sum(axis=1)
    ones = jnp.where(mask, 1.0, 0.0)
    return sum(spread[b] * ones[b : b + 1] for b in range(TILE))


def lessened(values, first):
    extra = unpacked(values, first, "low")
    extra = jnp.concatenate([extra[TILE - 1 :], extra[: TILE - 1]], axis=0)
    blocks = values.reshape(TILE, TILE, WIDE)
    start = lax.broadcasted_iota(jnp.int32, blocks.shape, 1) == 0
    return jnp.where(start, blocks - extra[:, None, :], blocks).reshape(LINE, WIDE)


def repacked(back, first):
    mask = block_mask()
    rows = [back[b * TILE : b * TILE + 1] for b in range(TILE)]
    chunks = [jnp.where(mask, row, 0.0) for row in rows[1:] + rows[:1]]
    return picked(jnp.concatenate(chunks, axis=0), pack_places(first))


def forward_kernel(lines, basis, spectrum):
    spectrum[:, 0, :] = product(basis[...], lessened(lines[...], FIRST))


def column_of(row, first):
    shape = (LEVELS // 2, LEVELS)
    level = 2 * lax.broadcasted_iota(jnp.int32, shape, 0) + first
    own = level == lax.broadcasted_iota(jnp.int32, shape, 1)
    return jnp.sum(jnp.where(own, row, 0.0), axis=1, keepdims=True)


def joined(ref, rows=slice(None)):
    return jnp.concatenate([ref[0, rows, :], ref[1, rows, :]], axis=1)


def keep(ref, rows, value):
    ref[0, rows, :] = value[:, :128]
    ref[1, rows, :] = value[:, 128:]


def even_odd(ref, levels):
    return [joined(ref, pl.ds(first, levels // 2, stride=2)) for first in (0, 1)]


def without_odd(diagonals, couplings, rights):
    (diagonal, odd_diagonal), (coupling, odd_coupling) = diagonals, couplings
    right, odd_right = rights
    inverse = 1.0 / odd_diagonal
    below, above = coupling * inverse, odd_coupling * inverse
    shifted = lambda a: jnp.concatenate([jnp.zeros_like(a[:1]), a[:-1]], axis=0)
    left = (
        diagonal - coupling * below - shifted(odd_coupling * above),
        -below * odd_coupling,
        right - below * odd_right - shifted(above * odd_right),
    )
    return left, (inverse * odd_right, below, above)


def put_back(even, rest, ref):
    own, below, above = rest
    next_even = jnp.concatenate([even[1:], jnp.zeros_like(even[:1])], axis=0)
    count = even.shape[0]
    keep(ref, pl.ds(0, count, stride=2), even)
    keep(ref, pl.ds(1, count, stride=2), own - below * even - above * next_even)


def reduced(diagonal, coupling, right):
    levels = right.shape[0]
    stride = 1
    while stride < levels:
        shared = levels - stride
        reciprocal = 1.0 / diagonal
        near = coupling[:shared]
        from_above = near * reciprocal[stride:]
        from_below = near * reciprocal[:shared]
        gap = jnp.zeros((stride, right.shape[1]), jnp.float32)
        low = lambda a: jnp.concatenate([a, gap], axis=0)
        high = lambda a: jnp.concatenate([gap, a], axis=0)
        right = right - low(from_above * right[stride:]) - high(from_below * right[:shared])
        diagonal = diagonal - low(near * from_above) - high(near * from_below)
        if shared > stride:
            coupling = low(-from_above * coupling[stride:])
        stride *= 2
    return right / diagonal


def solve_kernel(lines, basis, level_steps, shift, result, tiled, solved, *half):
    tiled[...] = lines[:, 0, :]
    thickness, spacing = level_rows(level_steps)
    level = lax.broadcasted_iota(jnp.int32, (1, LEVELS), 1)
    inv_space = 1.0 / spacing
    middle = inv_space + lanes_down(inv_space)
    between = jnp.where(level < LEVELS - 1, -inv_space, 0.0)
    thick = [column_of(thickness, first) for first in (0, 1)]
    diagonals = [column_of(middle, first) + thick[first] * shift[...] for first in (0, 1)]
    couplings = [column_of(between, first) for first in (0, 1)]
    values = lessened(tiled[...], SECOND)
    keep(solved, slice(None), product(values, basis[...], ((0,), (0,))))
    rights = [-t * part for t, part in zip(thick, even_odd(solved, LEVELS))]
    left, rest = without_odd(diagonals, couplings, rights)
    for ref, value in zip(half, left):
        keep(ref, slice(None), value)
    left, rest_of_half = without_odd(*[even_odd(ref, LEVELS // 2) for ref in half])
    put_back(reduced(*left), rest_of_half, half[0])
    put_back(joined(half[0]), rest, solved)
    keep(solved, slice(LEVELS, WIDE), jnp.zeros((WIDE - LEVELS, LINE), jnp.float32))
    back = product(basis[...], joined(solved), ((1,), (1,)))
    result[:, 0, :128] = back[:, :128]
    result[:, 0, 128:] = back[:, 128:] + repacked(back, FIRST)


def backward_kernel(lines, basis, message, tiled):
    tiled[...] = lines[:, 0, :]
    back = product(basis[...], tiled[...])
    message[:, :128] = back[:, :128]
    message[:, 128:] = back[:, 128:] + repacked(back, SECOND)


def correct_kernel(message, inner, fluid, *rest):
    edges, halos, level_steps = rest[:4], rest[4:8], rest[8]
    updated, pressure, fields, cells, sems = rest[9:]
    fields[...] = inner[...]
    add_outer_faces(FIELDS, fields, edges, halos, fluid)
    copies = loaded([(fields.at[3:5], updated.at[3:5])], sems.at[pl.ds(2 * TILE // PART, 1)])
    inv_space = 1.0 / level_rows(level_steps)[1]
    lines = message[...].reshape(LINE, WIDE)
    north = unpacked(lines, FIRST, "high")[:, :LEVELS]
    east = unpacked(lines, SECOND, "low")[:, :LEVELS]
    for x in range(TILE):
        p = message[:, x, :LEVELS]
        p_east = message[:, x + 1, :LEVELS] if x < TILE - 1 else east
        p_north = jnp.concatenate([p[1:], north[x : x + 1]], axis=0)
        p_upper = jnp.concatenate([p[:, 1:], jnp.zeros_like(p[:, :1])], axis=1)
        open_cell = fluid[x]
        fields[0, x] = open_cell * (fields[0, x] - (p_east - p))
        fields[1, x] = open_cell * (fields[1, x] - (p_north - p))
        fields[2, x] = open_cell * (fields[2, x] - (p_upper - p) * inv_space)
        cells[x] = p
        part = parts_of(x)
        if part is not None:
            pairs = [(fields.at[0:3, part], updated.at[0:3, part]), (cells.at[part], pressure.at[part])]
            copies += loaded(pairs, sems.at[pl.ds(x // PART * 2, 2)])
    for copy in copies:
        copy.wait()


def shaped(*shape):
    return jax.ShapeDtypeStruct(shape, jnp.float32)


def call(kernel, out_shape, *operands, flops=0, **options):
    here = pl.BlockSpec(memory_space=pltpu.VMEM)
    options.setdefault("in_specs", [here] * len(operands))
    options.setdefault("out_specs", jax.tree.map(lambda _: here, out_shape))
    count = sum(int(np.prod(a.shape)) for a in operands) * 4
    return pl.pallas_call(
        kernel,
        out_shape=out_shape,
        name=kernel.__name__,
        compiler_params=pltpu.CompilerParams(vmem_limit_bytes=12 * 1024 * 1024),
        cost_estimate=pl.CostEstimate(flops=flops, bytes_accessed=count, transcendentals=0),
        **options,
    )(*operands)


def swapped(block, axis, outer):
    count = lax.axis_size(axis)
    partner = [((i + outer) ^ 1) - outer for i in range(count)]
    return lax.ppermute(block, axis, [(i, p % count) for i, p in enumerate(partner)])


def eigenvalues(frequency):
    return 2.0 - 2.0 * jnp.cos((2.0 * jnp.pi / LINE) * frequency.astype(jnp.float32))


def per_device(state, memory, level_steps, building_height):
    plane = shaped(5, TILE, LEVELS)
    edges = call(edges_kernel, [plane] * 4, state)
    halos = [
        swapped(edges[i], axis, outer)
        for i, (axis, outer) in enumerate([("px", 1), ("px", 0), ("py", 1), ("py", 0)])
    ]

    steps = level_steps.reshape(1, LEVELS)
    own_x = lax.axis_index("py") * lax.axis_size("px") + lax.axis_index("px")
    shift = eigenvalues(jnp.arange(LINE, dtype=jnp.int32)) + eigenvalues(own_x)
    basis = jnp.asarray(BASIS)
    hbm = pl.BlockSpec(memory_space=pltpu.HBM)
    scratch = lambda *shape: pltpu.VMEM(shape, jnp.float32)
    sems = pltpu.SemaphoreType.DMA

    inner, fluid = call(
        interior_kernel,
        [shaped(FIELDS, TILE, TILE, LEVELS), shaped(TILE, TILE, LEVELS)],
        state, memory, steps, building_height,
        flops=10**7,
    )
    inner, shift = lax.optimization_barrier((inner, shift.reshape(1, LINE)))
    message = call(
        momentum_kernel,
        shaped(TILE, TILE, WIDE),
        inner, fluid, *edges, *halos, steps,
        flops=10**7,
        scratch_shapes=[scratch(3, TILE, TILE, LEVELS)],
    )
    lines = lax.all_to_all(message, "px", split_axis=0, concat_axis=0, tiled=True)
    spectrum = call(
        forward_kernel, shaped(LINE, 1, WIDE), lines.reshape(LINE, WIDE), basis
    )
    lines = lax.all_to_all(spectrum, ("py", "px"), split_axis=0, concat_axis=0, tiled=True)
    solved = call(
        solve_kernel, shaped(LINE, 1, WIDE), lines, basis, steps, shift,
        scratch_shapes=[scratch(LINE, WIDE), scratch(2, WIDE, 128)]
        + [scratch(2, LEVELS // 2, 128)] * 3,
    )
    lines = lax.all_to_all(solved, ("py", "px"), split_axis=0, concat_axis=0, tiled=True)
    message = call(
        backward_kernel, shaped(LINE, WIDE), lines, basis, scratch_shapes=[scratch(LINE, WIDE)]
    )
    message = lax.all_to_all(
        message.reshape(TILE, TILE, WIDE), "px", split_axis=0, concat_axis=0, tiled=True
    )
    return call(
        correct_kernel,
        [shaped(5, TILE, TILE, LEVELS), shaped(TILE, TILE, LEVELS)],
        message, inner, fluid, *edges, *halos, steps,
        out_specs=[hbm] * 2,
        scratch_shapes=[
            scratch(FIELDS, TILE, TILE, LEVELS),
            scratch(TILE, TILE, LEVELS),
            sems((2 * TILE // PART + 1,)),
        ],
    )


def solution(mesh):
    return jax.shard_map(
        per_device,
        mesh=mesh,
        in_specs=(P(None, "px", "py", None), P(None, "px", "py", None), P(), P("px", "py")),
        out_specs=(P(None, "px", "py", None), P("px", "py", None)),
        check_vma=False,
    )
```

```python
import jax
import jax.numpy as jnp
import numpy as np
from jax import lax
from jax.experimental import pallas as pl
from jax.experimental.pallas import tpu as pltpu
from jax.sharding import PartitionSpec as P

RK_KEEP = -5.0 / 9.0
RK_STEP = 15.0 / 16.0
TIME_STEP = 0.1
DIFFUSION = 0.05
BUOYANCY = 0.3
HIGHEST = lax.Precision.HIGHEST

TILE = 16
LINE = 256
LEVELS = 192
WIDE = 256
CHUNK = LEVELS // TILE
FIELDS = 5
FIRST = 192
SECOND = 208
UNROLL = 3


def table():
    n = np.arange(LINE)
    angles = 2.0 * np.pi / LINE * (np.outer(n, n) % LINE)
    basis = (np.cos(angles) + np.sin(angles)) / np.sqrt(LINE)
    return basis.astype(np.float32)


BASIS = table()


def product(a, b, contract=((1,), (0,))):
    return lax.dot_general(
        a, b, (contract, ((), ())), precision=HIGHEST, preferred_element_type=jnp.float32
    )


def picked(values, places):
    high = values.astype(jnp.bfloat16)
    rest = values - high.astype(jnp.float32)
    middle = rest.astype(jnp.bfloat16)
    low = (rest - middle.astype(jnp.float32)).astype(jnp.bfloat16)
    dots = [
        jnp.dot(part, places, preferred_element_type=jnp.float32) for part in (low, middle, high)
    ]
    return (dots[0] + dots[1]) + dots[2]


def chunk_place(shape, level_dim, first):
    level = lax.broadcasted_iota(jnp.int32, shape, level_dim)
    lane = lax.broadcasted_iota(jnp.int32, shape, 1 - level_dim)
    chunk = jnp.floor((level.astype(jnp.float32) + 0.5) * (1.0 / CHUNK)).astype(jnp.int32)
    here = (level - chunk * CHUNK + (first - 128) == lane) & (level < LEVELS)
    return jnp.where(here, 1.0, 0.0).astype(jnp.bfloat16)


def pack_places(first):
    return chunk_place((WIDE, 128), 0, first)


def unpack_places(first):
    return chunk_place((128, WIDE), 1, first)


def each_block(rows):
    return jnp.concatenate(
        [jnp.broadcast_to(rows[b : b + 1], (TILE, rows.shape[1])) for b in range(TILE)], axis=0
    )


def level_rows(level_steps):
    thickness = level_steps[...].astype(jnp.float32)
    spacing = 0.5 * (thickness + lanes_up(thickness))
    return thickness, spacing


def block_mask():
    lane = lax.broadcasted_iota(jnp.int32, (TILE, WIDE), 1)
    start = lax.broadcasted_iota(jnp.int32, (TILE, WIDE), 0) * CHUNK
    return (lane >= start) & (lane < start + CHUNK)


def lanes_up(a):
    return jnp.concatenate([a[:, 1:], a[:, -1:]], axis=1)


def lanes_down(a):
    return jnp.concatenate([jnp.zeros_like(a[:, :1]), a[:, :-1]], axis=1)


def odd(axis):
    return lax.rem(lax.axis_index(axis), 2) == 1


def edges_kernel(state, x_outer, x_inner, y_outer, y_inner):
    low, high = state[:, 0], state[:, TILE - 1]
    x_outer[...] = jnp.where(odd("px"), high, low)
    x_inner[...] = jnp.where(odd("px"), low, high)
    low, high = state[:, :, 0], state[:, :, TILE - 1]
    y_outer[...] = jnp.where(odd("py"), high, low)
    y_inner[...] = jnp.where(odd("py"), low, high)


def faces(s, e, u):
    return e * (DIFFUSION - 0.5 * u) - s * (DIFFUSION + 0.5 * u)


def advance_fields(state, memory, level_steps, fluid, store):
    thickness, spacing = level_rows(level_steps)
    inv_thick = 1.0 / thickness
    inv_space = 1.0 / spacing
    nothing = jnp.zeros((TILE, LEVELS), jnp.float32)

    def plane(x, before, east_of):
        u = state[0, x]
        v = state[1, x]
        w = state[2, x]
        u_to, u_from = DIFFUSION - 0.5 * u, DIFFUSION + 0.5 * u
        v_to, v_from = DIFFUSION - 0.5 * v, DIFFUSION + 0.5 * v
        w_to, w_from = DIFFUSION * inv_space - 0.5 * w, DIFFUSION * inv_space + 0.5 * w
        factor = (RK_STEP * TIME_STEP) * fluid[x]
        after = []
        for f in range(FIELDS):
            s = state[f, x]
            x_face = east_of(f) * u_to - s * u_from if east_of else nothing
            y_face = jnp.concatenate([s[1:], s[:1]], axis=0) * v_to - s * v_from
            y_above = jnp.concatenate([y_face[:-1], nothing[:1]], axis=0)
            y_below = jnp.concatenate([nothing[:1], y_face[:-1]], axis=0)
            z_face = lanes_up(s) * w_to - s * w_from
            change = (x_face - before[f]) + (y_above - y_below)
            change = change + (z_face - lanes_down(z_face)) * inv_thick
            if f == 2:
                change = change + BUOYANCY * state[3, x]
            after.append(x_face)
            store(f, x, s + (RK_STEP * RK_KEEP) * memory[f, x] + factor * change)
        return tuple(after)

    before = (nothing,) * FIELDS
    before = lax.fori_loop(
        0, TILE - 1, lambda x, b: plane(x, b, lambda f: state[f, x + 1]), before, unroll=UNROLL
    )
    plane(TILE - 1, before, None)


PART = 4


def parts_of(x):
    return pl.ds(x + 1 - PART, PART) if x % PART == PART - 1 else None


def fill_fluid(height, fluid):
    heights = each_block(height[...].astype(jnp.float32))
    row = lax.broadcasted_iota(jnp.int32, (LINE, TILE), 0)
    own = row % TILE == lax.broadcasted_iota(jnp.int32, (LINE, TILE), 1)
    bottom = jnp.sum(jnp.where(own, heights, 0.0), axis=1, keepdims=True)
    level = lax.broadcasted_iota(jnp.int32, (TILE, LEVELS), 1).astype(jnp.float32)
    for x in range(TILE):
        fluid[x] = jnp.where(level >= bottom[x * TILE : (x + 1) * TILE], 1.0, 0.0)


def divergence(du, dv, dw, inv_thick):
    dv_before = jnp.concatenate([jnp.zeros_like(dv[:1]), dv[:-1]], axis=0)
    return du + (dv - dv_before) + (dw - lanes_down(dw)) * inv_thick


def interior_kernel(state, memory, level_steps, height, provisional, fluid, message):
    fill_fluid(height, fluid)

    def store(f, x, value):
        provisional[f, x] = value

    advance_fields(state, memory, level_steps, fluid, store)
    inv_thick = 1.0 / level_rows(level_steps)[0]
    for x in range(TILE):
        u, v, w = (provisional[f, x] for f in range(3))
        du = u - provisional[0, x - 1] if x else u
        total = divergence(du, v, w, inv_thick)
        rest = jnp.zeros((TILE, WIDE - LEVELS), jnp.float32)
        message[:, x, :128] = total[:, :128]
        message[:, x, 128:] = jnp.concatenate([total[:, 128:], rest], axis=1)


def sides(field, x_outer, x_inner, y_outer, y_inner):
    odd_x, odd_y = odd("px"), odd("py")
    return (
        jnp.where(odd_x, x_inner[field], x_outer[field]),
        jnp.where(odd_x, x_outer[field], x_inner[field]),
        jnp.where(odd_y, y_inner[field], y_outer[field]),
        jnp.where(odd_y, y_outer[field], y_inner[field]),
    )


def outer_faces(total, edges, halos, fluid):
    last, factor = TILE - 1, RK_STEP * TIME_STEP
    west_u, south_v = sides(0, *halos)[0], sides(1, *halos)[2]
    east_u, north_v = sides(0, *edges)[1], sides(1, *edges)[3]
    added = []
    for f in range(total):
        x_low, x_high, y_low, y_high = sides(f, *edges)
        west, east, south, north = sides(f, *halos)
        added.append(
            (
                -factor * fluid[0] * faces(west, x_low, west_u),
                factor * fluid[last] * faces(x_high, east, east_u),
                -factor * fluid[:, 0] * faces(south, y_low, south_v),
                factor * fluid[:, last] * faces(y_high, north, north_v),
            )
        )
    return added


def add_outer_faces(total, target, edges, halos, fluid):
    last = TILE - 1
    for f, (west, east, south, north) in enumerate(outer_faces(total, edges, halos, fluid)):
        target[f, 0] += west
        target[f, last] += east
        target[f, :, 0] += south
        target[f, :, last] += north


def momentum_kernel(inner, fluid, inner_message, *rest):
    edges, halos, (level_steps, message) = rest[:4], rest[4:8], rest[8:]
    added = outer_faces(3, edges, halos, fluid)
    (west_u, east_u, south_u, north_u), (west_v, east_v, south_v, north_v), w_added = added
    last = TILE - 1
    inv_thick = 1.0 / level_rows(level_steps)[0]
    row = lax.broadcasted_iota(jnp.int32, (TILE, LEVELS), 0)

    def with_ends(plane, first_row, last_row):
        return plane + jnp.where(row == 0, first_row, 0.0) + jnp.where(row == last, last_row, 0.0)

    zeros = jnp.zeros((TILE, WIDE - LEVELS), jnp.float32)
    last_u = with_ends(inner[0, last] + east_u, south_u[last:], north_u[last:])
    last_v = with_ends(inner[1, :, last] + north_v, west_v[last:], east_v[last:])
    last_u = jnp.concatenate([last_u, zeros], axis=1)
    last_v = jnp.concatenate([last_v, zeros], axis=1)
    mask = block_mask()
    u_packed = jnp.concatenate(
        [jnp.where(mask, last_u[y : y + 1], 0.0) for y in range(TILE)], axis=0
    )
    ones = jnp.where(mask, 1.0, 0.0)
    v_packed = jnp.concatenate([last_v * ones[y : y + 1] for y in range(TILE)], axis=0)
    upper = picked(u_packed, pack_places(FIRST)) + picked(v_packed, pack_places(SECOND))
    message[:, :, :128] = inner_message[:, :, :128]
    message[:, :, 128:] = inner_message[:, :, 128:] + upper.reshape(TILE, TILE, 128)
    message[:, 0, :LEVELS] += divergence(west_u, west_v, w_added[0], inv_thick)
    message[:, 1, :LEVELS] -= west_u
    message[:, last, :LEVELS] += divergence(east_u, east_v, w_added[1], inv_thick)
    message[0, :, :LEVELS] += divergence(south_v, south_u, w_added[2], inv_thick)
    message[1, :, :LEVELS] -= south_v
    message[last, :, :LEVELS] += divergence(north_v, north_u, w_added[3], inv_thick)


def loaded(pairs, sems):
    copies = [pltpu.make_async_copy(a, b, sems.at[i]) for i, (a, b) in enumerate(pairs)]
    for copy in copies:
        copy.start()
    return copies


def unpacked(values, first, owner):
    spread = picked(values[:, 128:], unpack_places(first)).reshape(TILE, TILE, WIDE)
    mask = block_mask()
    if owner == "low":
        return jnp.where(mask[None], spread, 0.0).sum(axis=1)
    ones = jnp.where(mask, 1.0, 0.0)
    return sum(spread[b] * ones[b : b + 1] for b in range(TILE))


def lessened(values, first):
    extra = unpacked(values, first, "low")
    extra = jnp.concatenate([extra[TILE - 1 :], extra[: TILE - 1]], axis=0)
    blocks = values.reshape(TILE, TILE, WIDE)
    start = lax.broadcasted_iota(jnp.int32, blocks.shape, 1) == 0
    return jnp.where(start, blocks - extra[:, None, :], blocks).reshape(LINE, WIDE)


def repacked(back, first):
    mask = block_mask()
    rows = [back[b * TILE : b * TILE + 1] for b in range(TILE)]
    chunks = [jnp.where(mask, row, 0.0) for row in rows[1:] + rows[:1]]
    return picked(jnp.concatenate(chunks, axis=0), pack_places(first))


def forward_kernel(lines, basis, spectrum):
    spectrum[:, 0, :] = product(basis[...], lessened(lines[...], FIRST))


def column_of(row, first):
    shape = (LEVELS // 2, LEVELS)
    level = 2 * lax.broadcasted_iota(jnp.int32, shape, 0) + first
    own = level == lax.broadcasted_iota(jnp.int32, shape, 1)
    return jnp.sum(jnp.where(own, row, 0.0), axis=1, keepdims=True)


def joined(ref, rows=slice(None)):
    return jnp.concatenate([ref[0, rows, :], ref[1, rows, :]], axis=1)


def keep(ref, rows, value):
    ref[0, rows, :] = value[:, :128]
    ref[1, rows, :] = value[:, 128:]


def even_odd(ref, levels):
    return [joined(ref, pl.ds(first, levels // 2, stride=2)) for first in (0, 1)]


def without_odd(diagonals, couplings, rights):
    (diagonal, odd_diagonal), (coupling, odd_coupling) = diagonals, couplings
    right, odd_right = rights
    inverse = 1.0 / odd_diagonal
    below, above = coupling * inverse, odd_coupling * inverse
    shifted = lambda a: jnp.concatenate([jnp.zeros_like(a[:1]), a[:-1]], axis=0)
    left = (
        diagonal - coupling * below - shifted(odd_coupling * above),
        -below * odd_coupling,
        right - below * odd_right - shifted(above * odd_right),
    )
    return left, (inverse * odd_right, below, above)


def put_back(even, rest, ref):
    own, below, above = rest
    next_even = jnp.concatenate([even[1:], jnp.zeros_like(even[:1])], axis=0)
    count = even.shape[0]
    keep(ref, pl.ds(0, count, stride=2), even)
    keep(ref, pl.ds(1, count, stride=2), own - below * even - above * next_even)


def reduced(diagonal, coupling, right):
    levels = right.shape[0]
    stride = 1
    while stride < levels:
        shared = levels - stride
        reciprocal = 1.0 / diagonal
        near = coupling[:shared]
        from_above = near * reciprocal[stride:]
        from_below = near * reciprocal[:shared]
        gap = jnp.zeros((stride, right.shape[1]), jnp.float32)
        low = lambda a: jnp.concatenate([a, gap], axis=0)
        high = lambda a: jnp.concatenate([gap, a], axis=0)
        right = right - low(from_above * right[stride:]) - high(from_below * right[:shared])
        diagonal = diagonal - low(near * from_above) - high(near * from_below)
        if shared > stride:
            coupling = low(-from_above * coupling[stride:])
        stride *= 2
    return right / diagonal


def solve_kernel(lines, basis, level_steps, shift, result, tiled, solved, *half):
    tiled[...] = lines[:, 0, :]
    thickness, spacing = level_rows(level_steps)
    level = lax.broadcasted_iota(jnp.int32, (1, LEVELS), 1)
    inv_space = 1.0 / spacing
    middle = inv_space + lanes_down(inv_space)
    between = jnp.where(level < LEVELS - 1, -inv_space, 0.0)
    thick = [column_of(thickness, first) for first in (0, 1)]
    diagonals = [column_of(middle, first) + thick[first] * shift[...] for first in (0, 1)]
    couplings = [column_of(between, first) for first in (0, 1)]
    values = lessened(tiled[...], SECOND)
    keep(solved, slice(None), product(values, basis[...], ((0,), (0,))))
    rights = [-t * part for t, part in zip(thick, even_odd(solved, LEVELS))]
    left, rest = without_odd(diagonals, couplings, rights)
    for ref, value in zip(half, left):
        keep(ref, slice(None), value)
    left, rest_of_half = without_odd(*[even_odd(ref, LEVELS // 2) for ref in half])
    put_back(reduced(*left), rest_of_half, half[0])
    put_back(joined(half[0]), rest, solved)
    keep(solved, slice(LEVELS, WIDE), jnp.zeros((WIDE - LEVELS, LINE), jnp.float32))
    back = product(basis[...], joined(solved), ((1,), (1,)))
    result[:, 0, :128] = back[:, :128]
    result[:, 0, 128:] = back[:, 128:] + repacked(back, FIRST)


def backward_kernel(lines, basis, message, tiled):
    tiled[...] = lines[:, 0, :]
    back = product(basis[...], tiled[...])
    message[:, :128] = back[:, :128]
    message[:, 128:] = back[:, 128:] + repacked(back, SECOND)


def correct_kernel(message, inner, fluid, *rest):
    edges, halos, level_steps = rest[:4], rest[4:8], rest[8]
    updated, pressure, fields, cells, sems = rest[9:]
    fields[...] = inner[...]
    add_outer_faces(FIELDS, fields, edges, halos, fluid)
    copies = loaded([(fields.at[3:5], updated.at[3:5])], sems.at[pl.ds(2 * TILE // PART, 1)])
    inv_space = 1.0 / level_rows(level_steps)[1]
    lines = message[...].reshape(LINE, WIDE)
    north = unpacked(lines, FIRST, "high")[:, :LEVELS]
    east = unpacked(lines, SECOND, "low")[:, :LEVELS]
    for x in range(TILE):
        p = message[:, x, :LEVELS]
        p_east = message[:, x + 1, :LEVELS] if x < TILE - 1 else east
        p_north = jnp.concatenate([p[1:], north[x : x + 1]], axis=0)
        p_upper = jnp.concatenate([p[:, 1:], jnp.zeros_like(p[:, :1])], axis=1)
        open_cell = fluid[x]
        fields[0, x] = open_cell * (fields[0, x] - (p_east - p))
        fields[1, x] = open_cell * (fields[1, x] - (p_north - p))
        fields[2, x] = open_cell * (fields[2, x] - (p_upper - p) * inv_space)
        cells[x] = p
        part = parts_of(x)
        if part is not None:
            pairs = [(fields.at[0:3, part], updated.at[0:3, part]), (cells.at[part], pressure.at[part])]
            copies += loaded(pairs, sems.at[pl.ds(x // PART * 2, 2)])
    for copy in copies:
        copy.wait()


def shaped(*shape):
    return jax.ShapeDtypeStruct(shape, jnp.float32)


def call(kernel, out_shape, *operands, flops=0, **options):
    here = pl.BlockSpec(memory_space=pltpu.VMEM)
    options.setdefault("in_specs", [here] * len(operands))
    options.setdefault("out_specs", jax.tree.map(lambda _: here, out_shape))
    count = sum(int(np.prod(a.shape)) for a in operands) * 4
    return pl.pallas_call(
        kernel,
        out_shape=out_shape,
        name=kernel.__name__,
        compiler_params=pltpu.CompilerParams(vmem_limit_bytes=12 * 1024 * 1024),
        cost_estimate=pl.CostEstimate(flops=flops, bytes_accessed=count, transcendentals=0),
        **options,
    )(*operands)


def swapped(block, axis, outer):
    count = lax.axis_size(axis)
    partner = [((i + outer) ^ 1) - outer for i in range(count)]
    return lax.ppermute(block, axis, [(i, p % count) for i, p in enumerate(partner)])


def eigenvalues(frequency):
    return 2.0 - 2.0 * jnp.cos((2.0 * jnp.pi / LINE) * frequency.astype(jnp.float32))


def per_device(state, memory, level_steps, building_height):
    plane = shaped(5, TILE, LEVELS)
    edges = call(edges_kernel, [plane] * 4, state)
    own_x = lax.axis_index("py") * lax.axis_size("px") + lax.axis_index("px")
    shift = eigenvalues(jnp.arange(LINE, dtype=jnp.int32)) + eigenvalues(own_x)
    *edges, shift = lax.optimization_barrier((*edges, shift.reshape(1, LINE)))
    halos = [
        swapped(edges[i], axis, outer)
        for i, (axis, outer) in enumerate([("px", 1), ("px", 0), ("py", 1), ("py", 0)])
    ]

    steps = level_steps.reshape(1, LEVELS)
    basis = jnp.asarray(BASIS)
    hbm = pl.BlockSpec(memory_space=pltpu.HBM)
    scratch = lambda *shape: pltpu.VMEM(shape, jnp.float32)
    sems = pltpu.SemaphoreType.DMA

    inner, fluid, message = call(
        interior_kernel,
        [
            shaped(FIELDS, TILE, TILE, LEVELS),
            shaped(TILE, TILE, LEVELS),
            shaped(TILE, TILE, WIDE),
        ],
        state, memory, steps, building_height,
        flops=10**7,
    )
    message = call(
        momentum_kernel,
        shaped(TILE, TILE, WIDE),
        inner, fluid, message, *edges, *halos, steps,
        flops=10**7,
    )
    lines = lax.all_to_all(message, "px", split_axis=0, concat_axis=0, tiled=True)
    spectrum = call(
        forward_kernel, shaped(LINE, 1, WIDE), lines.reshape(LINE, WIDE), basis
    )
    lines = lax.all_to_all(spectrum, ("py", "px"), split_axis=0, concat_axis=0, tiled=True)
    solved = call(
        solve_kernel, shaped(LINE, 1, WIDE), lines, basis, steps, shift,
        scratch_shapes=[scratch(LINE, WIDE), scratch(2, WIDE, 128)]
        + [scratch(2, LEVELS // 2, 128)] * 3,
    )
    lines = lax.all_to_all(solved, ("py", "px"), split_axis=0, concat_axis=0, tiled=True)
    message = call(
        backward_kernel, shaped(LINE, WIDE), lines, basis, scratch_shapes=[scratch(LINE, WIDE)]
    )
    message = lax.all_to_all(
        message.reshape(TILE, TILE, WIDE), "px", split_axis=0, concat_axis=0, tiled=True
    )
    return call(
        correct_kernel,
        [shaped(5, TILE, TILE, LEVELS), shaped(TILE, TILE, LEVELS)],
        message, inner, fluid, *edges, *halos, steps,
        out_specs=[hbm] * 2,
        scratch_shapes=[
            scratch(FIELDS, TILE, TILE, LEVELS),
            scratch(TILE, TILE, LEVELS),
            sems((2 * TILE // PART + 1,)),
        ],
    )


def solution(mesh):
    return jax.shard_map(
        per_device,
        mesh=mesh,
        in_specs=(P(None, "px", "py", None), P(None, "px", "py", None), P(), P("px", "py")),
        out_specs=(P(None, "px", "py", None), P("px", "py", None)),
        check_vma=False,
    )
```

```python
import jax
import jax.numpy as jnp
import numpy as np
from jax import lax
from jax.experimental import pallas as pl
from jax.experimental.pallas import tpu as pltpu
from jax.sharding import PartitionSpec as P

RK_KEEP = -5.0 / 9.0
RK_STEP = 15.0 / 16.0
TIME_STEP = 0.1
DIFFUSION = 0.05
BUOYANCY = 0.3
HIGHEST = lax.Precision.HIGHEST

TILE = 16
LINE = 256
LEVELS = 192
WIDE = 256
CHUNK = LEVELS // TILE
FIELDS = 5
FIRST = 192
SECOND = 208
UNROLL = 3


def table():
    n = np.arange(LINE)
    angles = 2.0 * np.pi / LINE * (np.outer(n, n) % LINE)
    basis = (np.cos(angles) + np.sin(angles)) / np.sqrt(LINE)
    return basis.astype(np.float32)


BASIS = table()


def product(a, b, contract=((1,), (0,))):
    return lax.dot_general(
        a, b, (contract, ((), ())), precision=HIGHEST, preferred_element_type=jnp.float32
    )


def picked(values, places):
    high = values.astype(jnp.bfloat16)
    rest = values - high.astype(jnp.float32)
    middle = rest.astype(jnp.bfloat16)
    low = (rest - middle.astype(jnp.float32)).astype(jnp.bfloat16)
    dots = [
        jnp.dot(part, places, preferred_element_type=jnp.float32) for part in (low, middle, high)
    ]
    return (dots[0] + dots[1]) + dots[2]


def chunk_place(shape, level_dim, first):
    level = lax.broadcasted_iota(jnp.int32, shape, level_dim)
    lane = lax.broadcasted_iota(jnp.int32, shape, 1 - level_dim)
    chunk = jnp.floor((level.astype(jnp.float32) + 0.5) * (1.0 / CHUNK)).astype(jnp.int32)
    here = (level - chunk * CHUNK + (first - 128) == lane) & (level < LEVELS)
    return jnp.where(here, 1.0, 0.0).astype(jnp.bfloat16)


def pack_places(first):
    return chunk_place((WIDE, 128), 0, first)


def unpack_places(first):
    return chunk_place((128, WIDE), 1, first)


def each_block(rows):
    return jnp.concatenate(
        [jnp.broadcast_to(rows[b : b + 1], (TILE, rows.shape[1])) for b in range(TILE)], axis=0
    )


def level_rows(level_steps):
    thickness = level_steps[...].astype(jnp.float32)
    spacing = 0.5 * (thickness + lanes_up(thickness))
    return thickness, spacing


def block_mask():
    lane = lax.broadcasted_iota(jnp.int32, (TILE, WIDE), 1)
    start = lax.broadcasted_iota(jnp.int32, (TILE, WIDE), 0) * CHUNK
    return (lane >= start) & (lane < start + CHUNK)


def lanes_up(a):
    return jnp.concatenate([a[:, 1:], a[:, -1:]], axis=1)


def lanes_down(a):
    return jnp.concatenate([jnp.zeros_like(a[:, :1]), a[:, :-1]], axis=1)


def odd(axis):
    return lax.rem(lax.axis_index(axis), 2) == 1


def edges_kernel(state, x_outer, x_inner, y_outer, y_inner):
    low, high = state[:, 0], state[:, TILE - 1]
    x_outer[...] = jnp.where(odd("px"), high, low)
    x_inner[...] = jnp.where(odd("px"), low, high)
    low, high = state[:, :, 0], state[:, :, TILE - 1]
    y_outer[...] = jnp.where(odd("py"), high, low)
    y_inner[...] = jnp.where(odd("py"), low, high)


def faces(s, e, u):
    return e * (DIFFUSION - 0.5 * u) - s * (DIFFUSION + 0.5 * u)


def advance_fields(state, memory, level_steps, fluid, store):
    thickness, spacing = level_rows(level_steps)
    inv_thick = 1.0 / thickness
    inv_space = 1.0 / spacing
    nothing = jnp.zeros((TILE, LEVELS), jnp.float32)

    def plane(x, before, east_of):
        u = state[0, x]
        v = state[1, x]
        w = state[2, x]
        u_to, u_from = DIFFUSION - 0.5 * u, DIFFUSION + 0.5 * u
        v_to, v_from = DIFFUSION - 0.5 * v, DIFFUSION + 0.5 * v
        w_to, w_from = DIFFUSION * inv_space - 0.5 * w, DIFFUSION * inv_space + 0.5 * w
        factor = (RK_STEP * TIME_STEP) * fluid[x]
        after = []
        for f in range(FIELDS):
            s = state[f, x]
            x_face = east_of(f) * u_to - s * u_from if east_of else nothing
            y_face = jnp.concatenate([s[1:], s[:1]], axis=0) * v_to - s * v_from
            y_above = jnp.concatenate([y_face[:-1], nothing[:1]], axis=0)
            y_below = jnp.concatenate([nothing[:1], y_face[:-1]], axis=0)
            z_face = lanes_up(s) * w_to - s * w_from
            change = (x_face - before[f]) + (y_above - y_below)
            change = change + (z_face - lanes_down(z_face)) * inv_thick
            if f == 2:
                change = change + BUOYANCY * state[3, x]
            after.append(x_face)
            store(f, x, s + (RK_STEP * RK_KEEP) * memory[f, x] + factor * change)
        return tuple(after)

    before = (nothing,) * FIELDS
    before = lax.fori_loop(
        0, TILE - 1, lambda x, b: plane(x, b, lambda f: state[f, x + 1]), before, unroll=UNROLL
    )
    plane(TILE - 1, before, None)


PART = 4


def parts_of(x):
    return pl.ds(x + 1 - PART, PART) if x % PART == PART - 1 else None


def fill_fluid(height, fluid):
    heights = each_block(height[...].astype(jnp.float32))
    row = lax.broadcasted_iota(jnp.int32, (LINE, TILE), 0)
    own = row % TILE == lax.broadcasted_iota(jnp.int32, (LINE, TILE), 1)
    bottom = jnp.sum(jnp.where(own, heights, 0.0), axis=1, keepdims=True)
    level = lax.broadcasted_iota(jnp.int32, (TILE, LEVELS), 1).astype(jnp.float32)
    for x in range(TILE):
        fluid[x] = jnp.where(level >= bottom[x * TILE : (x + 1) * TILE], 1.0, 0.0)


def divergence(du, dv, dw, inv_thick):
    dv_before = jnp.concatenate([jnp.zeros_like(dv[:1]), dv[:-1]], axis=0)
    return du + (dv - dv_before) + (dw - lanes_down(dw)) * inv_thick


def interior_kernel(
    state, memory, level_steps, height, shift, provisional, fluid, message, shift_kept
):
    shift_kept[...] = shift[...]
    fill_fluid(height, fluid)

    def store(f, x, value):
        provisional[f, x] = value

    advance_fields(state, memory, level_steps, fluid, store)
    inv_thick = 1.0 / level_rows(level_steps)[0]
    for x in range(TILE):
        u, v, w = (provisional[f, x] for f in range(3))
        du = u - provisional[0, x - 1] if x else u
        total = divergence(du, v, w, inv_thick)
        rest = jnp.zeros((TILE, WIDE - LEVELS), jnp.float32)
        message[:, x, :128] = total[:, :128]
        message[:, x, 128:] = jnp.concatenate([total[:, 128:], rest], axis=1)


def sides(field, x_outer, x_inner, y_outer, y_inner):
    odd_x, odd_y = odd("px"), odd("py")
    return (
        jnp.where(odd_x, x_inner[field], x_outer[field]),
        jnp.where(odd_x, x_outer[field], x_inner[field]),
        jnp.where(odd_y, y_inner[field], y_outer[field]),
        jnp.where(odd_y, y_outer[field], y_inner[field]),
    )


def outer_faces(total, edges, halos, fluid):
    last, factor = TILE - 1, RK_STEP * TIME_STEP
    west_u, south_v = sides(0, *halos)[0], sides(1, *halos)[2]
    east_u, north_v = sides(0, *edges)[1], sides(1, *edges)[3]
    added = []
    for f in range(total):
        x_low, x_high, y_low, y_high = sides(f, *edges)
        west, east, south, north = sides(f, *halos)
        added.append(
            (
                -factor * fluid[0] * faces(west, x_low, west_u),
                factor * fluid[last] * faces(x_high, east, east_u),
                -factor * fluid[:, 0] * faces(south, y_low, south_v),
                factor * fluid[:, last] * faces(y_high, north, north_v),
            )
        )
    return added


def add_outer_faces(total, target, edges, halos, fluid):
    last = TILE - 1
    for f, (west, east, south, north) in enumerate(outer_faces(total, edges, halos, fluid)):
        target[f, 0] += west
        target[f, last] += east
        target[f, :, 0] += south
        target[f, :, last] += north


def momentum_kernel(inner, fluid, inner_message, *rest):
    edges, halos, (level_steps, message) = rest[:4], rest[4:8], rest[8:]
    added = outer_faces(3, edges, halos, fluid)
    (west_u, east_u, south_u, north_u), (west_v, east_v, south_v, north_v), w_added = added
    last = TILE - 1
    inv_thick = 1.0 / level_rows(level_steps)[0]
    row = lax.broadcasted_iota(jnp.int32, (TILE, LEVELS), 0)

    def with_ends(plane, first_row, last_row):
        return plane + jnp.where(row == 0, first_row, 0.0) + jnp.where(row == last, last_row, 0.0)

    zeros = jnp.zeros((TILE, WIDE - LEVELS), jnp.float32)
    last_u = with_ends(inner[0, last] + east_u, south_u[last:], north_u[last:])
    last_v = with_ends(inner[1, :, last] + north_v, west_v[last:], east_v[last:])
    last_u = jnp.concatenate([last_u, zeros], axis=1)
    last_v = jnp.concatenate([last_v, zeros], axis=1)
    mask = block_mask()
    u_packed = jnp.concatenate(
        [jnp.where(mask, last_u[y : y + 1], 0.0) for y in range(TILE)], axis=0
    )
    ones = jnp.where(mask, 1.0, 0.0)
    v_packed = jnp.concatenate([last_v * ones[y : y + 1] for y in range(TILE)], axis=0)
    upper = picked(u_packed, pack_places(FIRST)) + picked(v_packed, pack_places(SECOND))
    message[:, :, :128] = inner_message[:, :, :128]
    message[:, :, 128:] = inner_message[:, :, 128:] + upper.reshape(TILE, TILE, 128)
    message[:, 0, :LEVELS] += divergence(west_u, west_v, w_added[0], inv_thick)
    message[:, 1, :LEVELS] -= west_u
    message[:, last, :LEVELS] += divergence(east_u, east_v, w_added[1], inv_thick)
    message[0, :, :LEVELS] += divergence(south_v, south_u, w_added[2], inv_thick)
    message[1, :, :LEVELS] -= south_v
    message[last, :, :LEVELS] += divergence(north_v, north_u, w_added[3], inv_thick)


def loaded(pairs, sems):
    copies = [pltpu.make_async_copy(a, b, sems.at[i]) for i, (a, b) in enumerate(pairs)]
    for copy in copies:
        copy.start()
    return copies


def unpacked(values, first, owner):
    spread = picked(values[:, 128:], unpack_places(first)).reshape(TILE, TILE, WIDE)
    mask = block_mask()
    if owner == "low":
        return jnp.where(mask[None], spread, 0.0).sum(axis=1)
    ones = jnp.where(mask, 1.0, 0.0)
    return sum(spread[b] * ones[b : b + 1] for b in range(TILE))


def lessened(values, first):
    extra = unpacked(values, first, "low")
    extra = jnp.concatenate([extra[TILE - 1 :], extra[: TILE - 1]], axis=0)
    blocks = values.reshape(TILE, TILE, WIDE)
    start = lax.broadcasted_iota(jnp.int32, blocks.shape, 1) == 0
    return jnp.where(start, blocks - extra[:, None, :], blocks).reshape(LINE, WIDE)


def repacked(back, first):
    mask = block_mask()
    rows = [back[b * TILE : b * TILE + 1] for b in range(TILE)]
    chunks = [jnp.where(mask, row, 0.0) for row in rows[1:] + rows[:1]]
    return picked(jnp.concatenate(chunks, axis=0), pack_places(first))


def forward_kernel(lines, basis, spectrum):
    spectrum[:, 0, :] = product(basis[...], lessened(lines[...], FIRST))


def column_of(row, first):
    shape = (LEVELS // 2, LEVELS)
    level = 2 * lax.broadcasted_iota(jnp.int32, shape, 0) + first
    own = level == lax.broadcasted_iota(jnp.int32, shape, 1)
    return jnp.sum(jnp.where(own, row, 0.0), axis=1, keepdims=True)


def joined(ref, rows=slice(None)):
    return jnp.concatenate([ref[0, rows, :], ref[1, rows, :]], axis=1)


def keep(ref, rows, value):
    ref[0, rows, :] = value[:, :128]
    ref[1, rows, :] = value[:, 128:]


def even_odd(ref, levels):
    return [joined(ref, pl.ds(first, levels // 2, stride=2)) for first in (0, 1)]


def without_odd(diagonals, couplings, rights):
    (diagonal, odd_diagonal), (coupling, odd_coupling) = diagonals, couplings
    right, odd_right = rights
    inverse = 1.0 / odd_diagonal
    below, above = coupling * inverse, odd_coupling * inverse
    shifted = lambda a: jnp.concatenate([jnp.zeros_like(a[:1]), a[:-1]], axis=0)
    left = (
        diagonal - coupling * below - shifted(odd_coupling * above),
        -below * odd_coupling,
        right - below * odd_right - shifted(above * odd_right),
    )
    return left, (inverse * odd_right, below, above)


def put_back(even, rest, ref):
    own, below, above = rest
    next_even = jnp.concatenate([even[1:], jnp.zeros_like(even[:1])], axis=0)
    count = even.shape[0]
    keep(ref, pl.ds(0, count, stride=2), even)
    keep(ref, pl.ds(1, count, stride=2), own - below * even - above * next_even)


def reduced(diagonal, coupling, right):
    levels = right.shape[0]
    stride = 1
    while stride < levels:
        shared = levels - stride
        reciprocal = 1.0 / diagonal
        near = coupling[:shared]
        from_above = near * reciprocal[stride:]
        from_below = near * reciprocal[:shared]
        gap = jnp.zeros((stride, right.shape[1]), jnp.float32)
        low = lambda a: jnp.concatenate([a, gap], axis=0)
        high = lambda a: jnp.concatenate([gap, a], axis=0)
        right = right - low(from_above * right[stride:]) - high(from_below * right[:shared])
        diagonal = diagonal - low(near * from_above) - high(near * from_below)
        if shared > stride:
            coupling = low(-from_above * coupling[stride:])
        stride *= 2
    return right / diagonal


def solve_kernel(lines, basis, level_steps, shift, result, tiled, solved, *half):
    tiled[...] = lines[:, 0, :]
    thickness, spacing = level_rows(level_steps)
    level = lax.broadcasted_iota(jnp.int32, (1, LEVELS), 1)
    inv_space = 1.0 / spacing
    middle = inv_space + lanes_down(inv_space)
    between = jnp.where(level < LEVELS - 1, -inv_space, 0.0)
    thick = [column_of(thickness, first) for first in (0, 1)]
    diagonals = [column_of(middle, first) + thick[first] * shift[...] for first in (0, 1)]
    couplings = [column_of(between, first) for first in (0, 1)]
    values = lessened(tiled[...], SECOND)
    keep(solved, slice(None), product(values, basis[...], ((0,), (0,))))
    rights = [-t * part for t, part in zip(thick, even_odd(solved, LEVELS))]
    left, rest = without_odd(diagonals, couplings, rights)
    for ref, value in zip(half, left):
        keep(ref, slice(None), value)
    left, rest_of_half = without_odd(*[even_odd(ref, LEVELS // 2) for ref in half])
    put_back(reduced(*left), rest_of_half, half[0])
    put_back(joined(half[0]), rest, solved)
    keep(solved, slice(LEVELS, WIDE), jnp.zeros((WIDE - LEVELS, LINE), jnp.float32))
    back = product(basis[...], joined(solved), ((1,), (1,)))
    result[:, 0, :128] = back[:, :128]
    result[:, 0, 128:] = back[:, 128:] + repacked(back, FIRST)


def backward_kernel(lines, basis, message, tiled):
    tiled[...] = lines[:, 0, :]
    back = product(basis[...], tiled[...])
    message[:, :128] = back[:, :128]
    message[:, 128:] = back[:, 128:] + repacked(back, SECOND)


def correct_kernel(message, inner, fluid, *rest):
    edges, halos, level_steps = rest[:4], rest[4:8], rest[8]
    updated, pressure, fields, cells, sems = rest[9:]
    fields[...] = inner[...]
    add_outer_faces(FIELDS, fields, edges, halos, fluid)
    copies = loaded([(fields.at[3:5], updated.at[3:5])], sems.at[pl.ds(2 * TILE // PART, 1)])
    inv_space = 1.0 / level_rows(level_steps)[1]
    lines = message[...].reshape(LINE, WIDE)
    north = unpacked(lines, FIRST, "high")[:, :LEVELS]
    east = unpacked(lines, SECOND, "low")[:, :LEVELS]
    for x in range(TILE):
        p = message[:, x, :LEVELS]
        p_east = message[:, x + 1, :LEVELS] if x < TILE - 1 else east
        p_north = jnp.concatenate([p[1:], north[x : x + 1]], axis=0)
        p_upper = jnp.concatenate([p[:, 1:], jnp.zeros_like(p[:, :1])], axis=1)
        open_cell = fluid[x]
        fields[0, x] = open_cell * (fields[0, x] - (p_east - p))
        fields[1, x] = open_cell * (fields[1, x] - (p_north - p))
        fields[2, x] = open_cell * (fields[2, x] - (p_upper - p) * inv_space)
        cells[x] = p
        part = parts_of(x)
        if part is not None:
            pairs = [(fields.at[0:3, part], updated.at[0:3, part]), (cells.at[part], pressure.at[part])]
            copies += loaded(pairs, sems.at[pl.ds(x // PART * 2, 2)])
    for copy in copies:
        copy.wait()


def shaped(*shape):
    return jax.ShapeDtypeStruct(shape, jnp.float32)


def call(kernel, out_shape, *operands, flops=0, **options):
    here = pl.BlockSpec(memory_space=pltpu.VMEM)
    options.setdefault("in_specs", [here] * len(operands))
    options.setdefault("out_specs", jax.tree.map(lambda _: here, out_shape))
    count = sum(int(np.prod(a.shape)) for a in operands) * 4
    return pl.pallas_call(
        kernel,
        out_shape=out_shape,
        name=kernel.__name__,
        compiler_params=pltpu.CompilerParams(vmem_limit_bytes=12 * 1024 * 1024),
        cost_estimate=pl.CostEstimate(flops=flops, bytes_accessed=count, transcendentals=0),
        **options,
    )(*operands)


def swapped(block, axis, outer):
    count = lax.axis_size(axis)
    partner = [((i + outer) ^ 1) - outer for i in range(count)]
    return lax.ppermute(block, axis, [(i, p % count) for i, p in enumerate(partner)])


def eigenvalues(frequency):
    return 2.0 - 2.0 * jnp.cos((2.0 * jnp.pi / LINE) * frequency.astype(jnp.float32))


def per_device(state, memory, level_steps, building_height):
    plane = shaped(5, TILE, LEVELS)
    edges = call(edges_kernel, [plane] * 4, state)
    own_x = lax.axis_index("py") * lax.axis_size("px") + lax.axis_index("px")
    shift = eigenvalues(jnp.arange(LINE, dtype=jnp.int32)) + eigenvalues(own_x)
    halos = [
        swapped(edges[i], axis, outer)
        for i, (axis, outer) in enumerate([("px", 1), ("px", 0), ("py", 1), ("py", 0)])
    ]

    steps = level_steps.reshape(1, LEVELS)
    basis = jnp.asarray(BASIS)
    hbm = pl.BlockSpec(memory_space=pltpu.HBM)
    scratch = lambda *shape: pltpu.VMEM(shape, jnp.float32)
    sems = pltpu.SemaphoreType.DMA

    inner, fluid, message, shift = call(
        interior_kernel,
        [
            shaped(FIELDS, TILE, TILE, LEVELS),
            shaped(TILE, TILE, LEVELS),
            shaped(TILE, TILE, WIDE),
            shaped(1, LINE),
        ],
        state, memory, steps, building_height, shift.reshape(1, LINE),
        flops=10**7,
    )
    message = call(
        momentum_kernel,
        shaped(TILE, TILE, WIDE),
        inner, fluid, message, *edges, *halos, steps,
        flops=10**7,
    )
    lines = lax.all_to_all(message, "px", split_axis=0, concat_axis=0, tiled=True)
    spectrum = call(
        forward_kernel, shaped(LINE, 1, WIDE), lines.reshape(LINE, WIDE), basis
    )
    lines = lax.all_to_all(spectrum, ("py", "px"), split_axis=0, concat_axis=0, tiled=True)
    solved = call(
        solve_kernel, shaped(LINE, 1, WIDE), lines, basis, steps, shift,
        scratch_shapes=[scratch(LINE, WIDE), scratch(2, WIDE, 128)]
        + [scratch(2, LEVELS // 2, 128)] * 3,
    )
    lines = lax.all_to_all(solved, ("py", "px"), split_axis=0, concat_axis=0, tiled=True)
    message = call(
        backward_kernel, shaped(LINE, WIDE), lines, basis, scratch_shapes=[scratch(LINE, WIDE)]
    )
    message = lax.all_to_all(
        message.reshape(TILE, TILE, WIDE), "px", split_axis=0, concat_axis=0, tiled=True
    )
    return call(
        correct_kernel,
        [shaped(5, TILE, TILE, LEVELS), shaped(TILE, TILE, LEVELS)],
        message, inner, fluid, *edges, *halos, steps,
        out_specs=[hbm] * 2,
        scratch_shapes=[
            scratch(FIELDS, TILE, TILE, LEVELS),
            scratch(TILE, TILE, LEVELS),
            sems((2 * TILE // PART + 1,)),
        ],
    )


def solution(mesh):
    return jax.shard_map(
        per_device,
        mesh=mesh,
        in_specs=(P(None, "px", "py", None), P(None, "px", "py", None), P(), P("px", "py")),
        out_specs=(P(None, "px", "py", None), P("px", "py", None)),
        check_vma=False,
    )
```

```python
import jax
import jax.numpy as jnp
import numpy as np
from jax import lax
from jax.experimental import pallas as pl
from jax.experimental.pallas import tpu as pltpu
from jax.sharding import PartitionSpec as P

RK_KEEP = -5.0 / 9.0
RK_STEP = 15.0 / 16.0
TIME_STEP = 0.1
DIFFUSION = 0.05
BUOYANCY = 0.3
HIGHEST = lax.Precision.HIGHEST

TILE = 16
LINE = 256
LEVELS = 192
WIDE = 256
CHUNK = LEVELS // TILE
FIELDS = 5
FIRST = 192
SECOND = 208
UNROLL = 3


def table():
    n = np.arange(LINE)
    angles = 2.0 * np.pi / LINE * (np.outer(n, n) % LINE)
    basis = (np.cos(angles) + np.sin(angles)) / np.sqrt(LINE)
    return basis.astype(np.float32)


BASIS = table()


def product(a, b, contract=((1,), (0,))):
    return lax.dot_general(
        a, b, (contract, ((), ())), precision=HIGHEST, preferred_element_type=jnp.float32
    )


def picked(values, places):
    high = values.astype(jnp.bfloat16)
    rest = values - high.astype(jnp.float32)
    middle = rest.astype(jnp.bfloat16)
    low = (rest - middle.astype(jnp.float32)).astype(jnp.bfloat16)
    dots = [
        jnp.dot(part, places, preferred_element_type=jnp.float32) for part in (low, middle, high)
    ]
    return (dots[0] + dots[1]) + dots[2]


def chunk_place(shape, level_dim, first):
    level = lax.broadcasted_iota(jnp.int32, shape, level_dim)
    lane = lax.broadcasted_iota(jnp.int32, shape, 1 - level_dim)
    chunk = jnp.floor((level.astype(jnp.float32) + 0.5) * (1.0 / CHUNK)).astype(jnp.int32)
    here = (level - chunk * CHUNK + (first - 128) == lane) & (level < LEVELS)
    return jnp.where(here, 1.0, 0.0).astype(jnp.bfloat16)


def pack_places(first):
    return chunk_place((WIDE, 128), 0, first)


def unpack_places(first):
    return chunk_place((128, WIDE), 1, first)


def each_block(rows):
    return jnp.concatenate(
        [jnp.broadcast_to(rows[b : b + 1], (TILE, rows.shape[1])) for b in range(TILE)], axis=0
    )


def level_rows(level_steps):
    thickness = level_steps[...].astype(jnp.float32)
    spacing = 0.5 * (thickness + lanes_up(thickness))
    return thickness, spacing


def block_mask():
    lane = lax.broadcasted_iota(jnp.int32, (TILE, WIDE), 1)
    start = lax.broadcasted_iota(jnp.int32, (TILE, WIDE), 0) * CHUNK
    return (lane >= start) & (lane < start + CHUNK)


def lanes_up(a):
    return jnp.concatenate([a[:, 1:], a[:, -1:]], axis=1)


def lanes_down(a):
    return jnp.concatenate([jnp.zeros_like(a[:, :1]), a[:, :-1]], axis=1)


def odd(axis):
    return lax.rem(lax.axis_index(axis), 2) == 1


def edges_kernel(state, x_outer, x_inner, y_outer, y_inner):
    low, high = state[:, 0], state[:, TILE - 1]
    x_outer[...] = jnp.where(odd("px"), high, low)
    x_inner[...] = jnp.where(odd("px"), low, high)
    low, high = state[:, :, 0], state[:, :, TILE - 1]
    y_outer[...] = jnp.where(odd("py"), high, low)
    y_inner[...] = jnp.where(odd("py"), low, high)


def faces(s, e, u):
    return e * (DIFFUSION - 0.5 * u) - s * (DIFFUSION + 0.5 * u)


def advance_fields(state, memory, level_steps, fluid, store):
    thickness, spacing = level_rows(level_steps)
    inv_thick = 1.0 / thickness
    inv_space = 1.0 / spacing
    nothing = jnp.zeros((TILE, LEVELS), jnp.float32)

    def plane(x, before, east_of):
        u = state[0, x]
        v = state[1, x]
        w = state[2, x]
        u_to, u_from = DIFFUSION - 0.5 * u, DIFFUSION + 0.5 * u
        v_to, v_from = DIFFUSION - 0.5 * v, DIFFUSION + 0.5 * v
        w_to, w_from = DIFFUSION * inv_space - 0.5 * w, DIFFUSION * inv_space + 0.5 * w
        factor = (RK_STEP * TIME_STEP) * fluid[x]
        after = []
        for f in range(FIELDS):
            s = state[f, x]
            x_face = east_of(f) * u_to - s * u_from if east_of else nothing
            y_face = jnp.concatenate([s[1:], s[:1]], axis=0) * v_to - s * v_from
            y_above = jnp.concatenate([y_face[:-1], nothing[:1]], axis=0)
            y_below = jnp.concatenate([nothing[:1], y_face[:-1]], axis=0)
            z_face = lanes_up(s) * w_to - s * w_from
            change = (x_face - before[f]) + (y_above - y_below)
            change = change + (z_face - lanes_down(z_face)) * inv_thick
            if f == 2:
                change = change + BUOYANCY * state[3, x]
            after.append(x_face)
            store(f, x, s + (RK_STEP * RK_KEEP) * memory[f, x] + factor * change)
        return tuple(after)

    before = (nothing,) * FIELDS
    before = lax.fori_loop(
        0, TILE - 1, lambda x, b: plane(x, b, lambda f: state[f, x + 1]), before, unroll=UNROLL
    )
    plane(TILE - 1, before, None)


PART = 8


def parts_of(x):
    return pl.ds(x + 1 - PART, PART) if x % PART == PART - 1 else None


def fill_fluid(height, fluid):
    heights = each_block(height[...].astype(jnp.float32))
    row = lax.broadcasted_iota(jnp.int32, (LINE, TILE), 0)
    own = row % TILE == lax.broadcasted_iota(jnp.int32, (LINE, TILE), 1)
    bottom = jnp.sum(jnp.where(own, heights, 0.0), axis=1, keepdims=True)
    level = lax.broadcasted_iota(jnp.int32, (TILE, LEVELS), 1).astype(jnp.float32)
    for x in range(TILE):
        fluid[x] = jnp.where(level >= bottom[x * TILE : (x + 1) * TILE], 1.0, 0.0)


def divergence(du, dv, dw, inv_thick):
    dv_before = jnp.concatenate([jnp.zeros_like(dv[:1]), dv[:-1]], axis=0)
    return du + (dv - dv_before) + (dw - lanes_down(dw)) * inv_thick


def interior_kernel(
    state, memory, level_steps, height, shift, provisional, fluid, message, shift_kept
):
    shift_kept[...] = shift[...]
    fill_fluid(height, fluid)

    def store(f, x, value):
        provisional[f, x] = value

    advance_fields(state, memory, level_steps, fluid, store)
    inv_thick = 1.0 / level_rows(level_steps)[0]
    for x in range(TILE):
        u, v, w = (provisional[f, x] for f in range(3))
        du = u - provisional[0, x - 1] if x else u
        total = divergence(du, v, w, inv_thick)
        rest = jnp.zeros((TILE, WIDE - LEVELS), jnp.float32)
        message[:, x, :128] = total[:, :128]
        message[:, x, 128:] = jnp.concatenate([total[:, 128:], rest], axis=1)


def sides(field, x_outer, x_inner, y_outer, y_inner):
    odd_x, odd_y = odd("px"), odd("py")
    return (
        jnp.where(odd_x, x_inner[field], x_outer[field]),
        jnp.where(odd_x, x_outer[field], x_inner[field]),
        jnp.where(odd_y, y_inner[field], y_outer[field]),
        jnp.where(odd_y, y_outer[field], y_inner[field]),
    )


def outer_faces(total, edges, halos, fluid):
    last, factor = TILE - 1, RK_STEP * TIME_STEP
    west_u, south_v = sides(0, *halos)[0], sides(1, *halos)[2]
    east_u, north_v = sides(0, *edges)[1], sides(1, *edges)[3]
    added = []
    for f in range(total):
        x_low, x_high, y_low, y_high = sides(f, *edges)
        west, east, south, north = sides(f, *halos)
        added.append(
            (
                -factor * fluid[0] * faces(west, x_low, west_u),
                factor * fluid[last] * faces(x_high, east, east_u),
                -factor * fluid[:, 0] * faces(south, y_low, south_v),
                factor * fluid[:, last] * faces(y_high, north, north_v),
            )
        )
    return added


def add_outer_faces(total, target, edges, halos, fluid):
    last = TILE - 1
    for f, (west, east, south, north) in enumerate(outer_faces(total, edges, halos, fluid)):
        target[f, 0] += west
        target[f, last] += east
        target[f, :, 0] += south
        target[f, :, last] += north


def momentum_kernel(inner, fluid, inner_message, *rest):
    edges, halos, (level_steps, message) = rest[:4], rest[4:8], rest[8:]
    added = outer_faces(3, edges, halos, fluid)
    (west_u, east_u, south_u, north_u), (west_v, east_v, south_v, north_v), w_added = added
    last = TILE - 1
    inv_thick = 1.0 / level_rows(level_steps)[0]
    row = lax.broadcasted_iota(jnp.int32, (TILE, LEVELS), 0)

    def with_ends(plane, first_row, last_row):
        return plane + jnp.where(row == 0, first_row, 0.0) + jnp.where(row == last, last_row, 0.0)

    zeros = jnp.zeros((TILE, WIDE - LEVELS), jnp.float32)
    last_u = with_ends(inner[0, last] + east_u, south_u[last:], north_u[last:])
    last_v = with_ends(inner[1, :, last] + north_v, west_v[last:], east_v[last:])
    last_u = jnp.concatenate([last_u, zeros], axis=1)
    last_v = jnp.concatenate([last_v, zeros], axis=1)
    mask = block_mask()
    u_packed = jnp.concatenate(
        [jnp.where(mask, last_u[y : y + 1], 0.0) for y in range(TILE)], axis=0
    )
    ones = jnp.where(mask, 1.0, 0.0)
    v_packed = jnp.concatenate([last_v * ones[y : y + 1] for y in range(TILE)], axis=0)
    upper = picked(u_packed, pack_places(FIRST)) + picked(v_packed, pack_places(SECOND))
    message[:, :, :128] = inner_message[:, :, :128]
    message[:, :, 128:] = inner_message[:, :, 128:] + upper.reshape(TILE, TILE, 128)
    message[:, 0, :LEVELS] += divergence(west_u, west_v, w_added[0], inv_thick)
    message[:, 1, :LEVELS] -= west_u
    message[:, last, :LEVELS] += divergence(east_u, east_v, w_added[1], inv_thick)
    message[0, :, :LEVELS] += divergence(south_v, south_u, w_added[2], inv_thick)
    message[1, :, :LEVELS] -= south_v
    message[last, :, :LEVELS] += divergence(north_v, north_u, w_added[3], inv_thick)


def loaded(pairs, sems):
    copies = [pltpu.make_async_copy(a, b, sems.at[i]) for i, (a, b) in enumerate(pairs)]
    for copy in copies:
        copy.start()
    return copies


def unpacked(values, first, owner):
    spread = picked(values[:, 128:], unpack_places(first)).reshape(TILE, TILE, WIDE)
    mask = block_mask()
    if owner == "low":
        return jnp.where(mask[None], spread, 0.0).sum(axis=1)
    ones = jnp.where(mask, 1.0, 0.0)
    return sum(spread[b] * ones[b : b + 1] for b in range(TILE))


def lessened(values, first):
    extra = unpacked(values, first, "low")
    extra = jnp.concatenate([extra[TILE - 1 :], extra[: TILE - 1]], axis=0)
    blocks = values.reshape(TILE, TILE, WIDE)
    start = lax.broadcasted_iota(jnp.int32, blocks.shape, 1) == 0
    return jnp.where(start, blocks - extra[:, None, :], blocks).reshape(LINE, WIDE)


def repacked(back, first):
    mask = block_mask()
    rows = [back[b * TILE : b * TILE + 1] for b in range(TILE)]
    chunks = [jnp.where(mask, row, 0.0) for row in rows[1:] + rows[:1]]
    return picked(jnp.concatenate(chunks, axis=0), pack_places(first))


def forward_kernel(lines, basis, spectrum):
    spectrum[:, 0, :] = product(basis[...], lessened(lines[...], FIRST))


def column_of(row, first):
    shape = (LEVELS // 2, LEVELS)
    level = 2 * lax.broadcasted_iota(jnp.int32, shape, 0) + first
    own = level == lax.broadcasted_iota(jnp.int32, shape, 1)
    return jnp.sum(jnp.where(own, row, 0.0), axis=1, keepdims=True)


def joined(ref, rows=slice(None)):
    return jnp.concatenate([ref[0, rows, :], ref[1, rows, :]], axis=1)


def keep(ref, rows, value):
    ref[0, rows, :] = value[:, :128]
    ref[1, rows, :] = value[:, 128:]


def even_odd(ref, levels):
    return [joined(ref, pl.ds(first, levels // 2, stride=2)) for first in (0, 1)]


def without_odd(diagonals, couplings, rights):
    (diagonal, odd_diagonal), (coupling, odd_coupling) = diagonals, couplings
    right, odd_right = rights
    inverse = 1.0 / odd_diagonal
    below, above = coupling * inverse, odd_coupling * inverse
    shifted = lambda a: jnp.concatenate([jnp.zeros_like(a[:1]), a[:-1]], axis=0)
    left = (
        diagonal - coupling * below - shifted(odd_coupling * above),
        -below * odd_coupling,
        right - below * odd_right - shifted(above * odd_right),
    )
    return left, (inverse * odd_right, below, above)


def put_back(even, rest, ref):
    own, below, above = rest
    next_even = jnp.concatenate([even[1:], jnp.zeros_like(even[:1])], axis=0)
    count = even.shape[0]
    keep(ref, pl.ds(0, count, stride=2), even)
    keep(ref, pl.ds(1, count, stride=2), own - below * even - above * next_even)


def reduced(diagonal, coupling, right):
    levels = right.shape[0]
    stride = 1
    while stride < levels:
        shared = levels - stride
        reciprocal = 1.0 / diagonal
        near = coupling[:shared]
        from_above = near * reciprocal[stride:]
        from_below = near * reciprocal[:shared]
        gap = jnp.zeros((stride, right.shape[1]), jnp.float32)
        low = lambda a: jnp.concatenate([a, gap], axis=0)
        high = lambda a: jnp.concatenate([gap, a], axis=0)
        right = right - low(from_above * right[stride:]) - high(from_below * right[:shared])
        diagonal = diagonal - low(near * from_above) - high(near * from_below)
        if shared > stride:
            coupling = low(-from_above * coupling[stride:])
        stride *= 2
    return right / diagonal


def solve_kernel(lines, basis, level_steps, shift, result, tiled, solved, *half):
    tiled[...] = lines[:, 0, :]
    thickness, spacing = level_rows(level_steps)
    level = lax.broadcasted_iota(jnp.int32, (1, LEVELS), 1)
    inv_space = 1.0 / spacing
    middle = inv_space + lanes_down(inv_space)
    between = jnp.where(level < LEVELS - 1, -inv_space, 0.0)
    thick = [column_of(thickness, first) for first in (0, 1)]
    diagonals = [column_of(middle, first) + thick[first] * shift[...] for first in (0, 1)]
    couplings = [column_of(between, first) for first in (0, 1)]
    values = lessened(tiled[...], SECOND)
    keep(solved, slice(None), product(values, basis[...], ((0,), (0,))))
    rights = [-t * part for t, part in zip(thick, even_odd(solved, LEVELS))]
    left, rest = without_odd(diagonals, couplings, rights)
    for ref, value in zip(half, left):
        keep(ref, slice(None), value)
    left, rest_of_half = without_odd(*[even_odd(ref, LEVELS // 2) for ref in half])
    put_back(reduced(*left), rest_of_half, half[0])
    put_back(joined(half[0]), rest, solved)
    keep(solved, slice(LEVELS, WIDE), jnp.zeros((WIDE - LEVELS, LINE), jnp.float32))
    back = product(basis[...], joined(solved), ((1,), (1,)))
    result[:, 0, :128] = back[:, :128]
    result[:, 0, 128:] = back[:, 128:] + repacked(back, FIRST)


def backward_kernel(lines, basis, message, tiled):
    tiled[...] = lines[:, 0, :]
    back = product(basis[...], tiled[...])
    message[:, :128] = back[:, :128]
    message[:, 128:] = back[:, 128:] + repacked(back, SECOND)


def correct_kernel(message, inner, fluid, *rest):
    edges, halos, level_steps = rest[:4], rest[4:8], rest[8]
    updated, pressure, fields, cells, sems = rest[9:]
    fields[...] = inner[...]
    add_outer_faces(FIELDS, fields, edges, halos, fluid)
    copies = loaded([(fields.at[3:5], updated.at[3:5])], sems.at[pl.ds(2 * TILE // PART, 1)])
    inv_space = 1.0 / level_rows(level_steps)[1]
    lines = message[...].reshape(LINE, WIDE)
    north = unpacked(lines, FIRST, "high")[:, :LEVELS]
    east = unpacked(lines, SECOND, "low")[:, :LEVELS]
    for x in range(TILE):
        p = message[:, x, :LEVELS]
        p_east = message[:, x + 1, :LEVELS] if x < TILE - 1 else east
        p_north = jnp.concatenate([p[1:], north[x : x + 1]], axis=0)
        p_upper = jnp.concatenate([p[:, 1:], jnp.zeros_like(p[:, :1])], axis=1)
        open_cell = fluid[x]
        fields[0, x] = open_cell * (fields[0, x] - (p_east - p))
        fields[1, x] = open_cell * (fields[1, x] - (p_north - p))
        fields[2, x] = open_cell * (fields[2, x] - (p_upper - p) * inv_space)
        cells[x] = p
        part = parts_of(x)
        if part is not None:
            pairs = [(fields.at[0:3, part], updated.at[0:3, part]), (cells.at[part], pressure.at[part])]
            copies += loaded(pairs, sems.at[pl.ds(x // PART * 2, 2)])
    for copy in copies:
        copy.wait()


def shaped(*shape):
    return jax.ShapeDtypeStruct(shape, jnp.float32)


def call(kernel, out_shape, *operands, flops=0, **options):
    here = pl.BlockSpec(memory_space=pltpu.VMEM)
    options.setdefault("in_specs", [here] * len(operands))
    options.setdefault("out_specs", jax.tree.map(lambda _: here, out_shape))
    count = sum(int(np.prod(a.shape)) for a in operands) * 4
    return pl.pallas_call(
        kernel,
        out_shape=out_shape,
        name=kernel.__name__,
        compiler_params=pltpu.CompilerParams(vmem_limit_bytes=12 * 1024 * 1024),
        cost_estimate=pl.CostEstimate(flops=flops, bytes_accessed=count, transcendentals=0),
        **options,
    )(*operands)


def swapped(block, axis, outer):
    count = lax.axis_size(axis)
    partner = [((i + outer) ^ 1) - outer for i in range(count)]
    return lax.ppermute(block, axis, [(i, p % count) for i, p in enumerate(partner)])


def eigenvalues(frequency):
    return 2.0 - 2.0 * jnp.cos((2.0 * jnp.pi / LINE) * frequency.astype(jnp.float32))


def per_device(state, memory, level_steps, building_height):
    plane = shaped(5, TILE, LEVELS)
    edges = call(edges_kernel, [plane] * 4, state)
    own_x = lax.axis_index("py") * lax.axis_size("px") + lax.axis_index("px")
    shift = eigenvalues(jnp.arange(LINE, dtype=jnp.int32)) + eigenvalues(own_x)
    halos = [
        swapped(edges[i], axis, outer)
        for i, (axis, outer) in enumerate([("px", 1), ("px", 0), ("py", 1), ("py", 0)])
    ]

    steps = level_steps.reshape(1, LEVELS)
    basis = jnp.asarray(BASIS)
    hbm = pl.BlockSpec(memory_space=pltpu.HBM)
    scratch = lambda *shape: pltpu.VMEM(shape, jnp.float32)
    sems = pltpu.SemaphoreType.DMA

    inner, fluid, message, shift = call(
        interior_kernel,
        [
            shaped(FIELDS, TILE, TILE, LEVELS),
            shaped(TILE, TILE, LEVELS),
            shaped(TILE, TILE, WIDE),
            shaped(1, LINE),
        ],
        state, memory, steps, building_height, shift.reshape(1, LINE),
        flops=10**7,
    )
    message = call(
        momentum_kernel,
        shaped(TILE, TILE, WIDE),
        inner, fluid, message, *edges, *halos, steps,
        flops=10**7,
    )
    lines = lax.all_to_all(message, "px", split_axis=0, concat_axis=0, tiled=True)
    spectrum = call(
        forward_kernel, shaped(LINE, 1, WIDE), lines.reshape(LINE, WIDE), basis
    )
    lines = lax.all_to_all(spectrum, ("py", "px"), split_axis=0, concat_axis=0, tiled=True)
    solved = call(
        solve_kernel, shaped(LINE, 1, WIDE), lines, basis, steps, shift,
        scratch_shapes=[scratch(LINE, WIDE), scratch(2, WIDE, 128)]
        + [scratch(2, LEVELS // 2, 128)] * 3,
    )
    lines = lax.all_to_all(solved, ("py", "px"), split_axis=0, concat_axis=0, tiled=True)
    message = call(
        backward_kernel, shaped(LINE, WIDE), lines, basis, scratch_shapes=[scratch(LINE, WIDE)]
    )
    message = lax.all_to_all(
        message.reshape(TILE, TILE, WIDE), "px", split_axis=0, concat_axis=0, tiled=True
    )
    return call(
        correct_kernel,
        [shaped(5, TILE, TILE, LEVELS), shaped(TILE, TILE, LEVELS)],
        message, inner, fluid, *edges, *halos, steps,
        out_specs=[hbm] * 2,
        scratch_shapes=[
            scratch(FIELDS, TILE, TILE, LEVELS),
            scratch(TILE, TILE, LEVELS),
            sems((2 * TILE // PART + 1,)),
        ],
    )


def solution(mesh):
    return jax.shard_map(
        per_device,
        mesh=mesh,
        in_specs=(P(None, "px", "py", None), P(None, "px", "py", None), P(), P("px", "py")),
        out_specs=(P(None, "px", "py", None), P("px", "py", None)),
        check_vma=False,
    )
```
